32 devices in a mesh: groups: 2 (over x), rows: 16 (over z, y, core).
Axes of the slice: x: 2, y: 2, z: 4, core: 2. Of those that a mesh axis runs over, the one named last changes fastest.
Arguments:
- dictionary: bfloat16 [8192, 32768], P('rows'), may hold values from -0.0625 to 0.0625
- patches: bfloat16 [8192, 2048], P('rows', 'groups'), parts along dimension 1, may hold values from -6 to 6
- initial_codes: bfloat16 [32, 16, 4096], P(('groups', 'rows')), parts along dimension 0, may hold values from -3 to 3
- support: int32 [32, 16], P('groups'), parts along dimension 0, may hold values from 0 to 511, as said below
- counts: int32 [32], P('groups'), parts along dimension 0, may hold values from 4 to 16, as said below
- group_order: int32 [32], P('groups'), parts along dimension 0, may hold values from 0 to 15, each once
- penalty: float32 [32, 64], P('groups'), parts along dimension 0, may hold values from 0.05 to 0.5
Outputs:
- codes: float32 [32, 16, 4096], P(('groups', 'rows')), parts along dimension 0
The draws below stay inside these ranges and needn't reach their ends.
There are 2 independent parts, one for each index of `groups`. The reference program is written for one: setup_inputs(seed, part) draws one part's arguments, and reference() takes and returns one part's arrays. A program takes and returns all parts, laid end to end along the dimension named above; an argument that names none is the same for every part. Nothing has to cross between parts.
Inputs may be any that keep to these rules, and one draw needn't show every extreme that they name: `support`: in each group's list the first counts entries are distinct block ids; entries at positions counts and beyond are padding and are ignored. The counts of one part sum to exactly 160.
All inputs are finite; a program needn't handle non-finite values.
Results may differ from the reference program's by a relative error of at most 0.0055.
Values may be sent and summed in bfloat16 or wider, within the bound.
No kernel may reach another device: no remote copies, remote signals or barrier semaphores. Data moves between devices by JAX's collectives and lax.ppermute only.
A program may use at most 192 MiB of HBM per device.

```python
import math
import jax
import jax.numpy as jnp
from jax import lax

PIX = 8192
NB = 512
BLOCK = 64
SLOTS = 16
PATCHES = 64
ITERS = 3
GROUPS = 16
ATOMS = 32768
BATCH = 1024
TILE = 4096


def draw_support(key, part):
    keys = jax.random.split(jax.random.fold_in(key, 11), GROUPS)
    lists = jax.vmap(lambda single: jax.random.permutation(single, NB)[:SLOTS])(keys)
    return lists.astype(jnp.int32)


def draw_counts(key, part):
    half_key, pick_key, order_key = jax.random.split(jax.random.fold_in(key, 23), 3)
    halves = GROUPS // 2
    first_half = jax.random.randint(half_key, (halves,), 4, 17)
    chosen = jax.random.randint(pick_key, (), 0, halves)
    first_half = jnp.where(jnp.arange(halves) == chosen, 16, first_half)
    joined = jnp.concatenate([first_half, 20 - first_half])
    shuffle = jax.random.permutation(order_key, GROUPS)
    return joined[shuffle].astype(jnp.int32)


def block_scale(own_key, dims, cuts, smallest, top_value):
    factor_of = 1.0
    for dim, blocks in cuts:
        steps = jax.random.uniform(jax.random.fold_in(jax.random.fold_in(own_key, 6), dim), (blocks,), jnp.float32, smallest / len(cuts), top_value / len(cuts))
        factor_of = factor_of * jnp.repeat(jnp.exp(steps), dims[dim] // blocks).reshape((-1,) + (1,) * (len(dims) - 1 - dim))
    return factor_of


def centred(stream_key, extent, deviation, most, shards=(), kind=jnp.bfloat16):
    factor_of = block_scale(stream_key, extent, shards, -0.22, 0.18) if shards else 1.0
    result = jax.random.normal(stream_key, extent, jnp.float32) * deviation * factor_of
    return jnp.minimum(jnp.maximum(result, -most), most).astype(kind)


def setup_inputs(seed: int = 0, part: int = 0) -> dict:
    seeds = jax.random.split(jax.random.key(seed), 8)
    part_keys = jax.random.split(jax.random.fold_in(seeds[7], part), 8)
    return {
        "dictionary": centred(seeds[0], (PIX, ATOMS), PIX ** -0.5, 0.0625, ((0, 16),)),
        "patches": centred(part_keys[1], (PIX, BATCH), 1.0, 6.0, ((0, 16),)),
        "initial_codes": centred(part_keys[2], (GROUPS, SLOTS, TILE), 0.5, 3.0, ((0, 16),)),
        "support": draw_support(jax.random.fold_in(jax.random.fold_in(seeds[7], part), 71), part),
        "counts": draw_counts(jax.random.fold_in(jax.random.fold_in(seeds[7], part), 71), part),
        "group_order": jax.random.permutation(part_keys[5], GROUPS).astype(jnp.int32),
        "penalty": jnp.clip(jnp.exp(jax.random.uniform(part_keys[6], (GROUPS, PATCHES), jnp.float32, math.log(0.05), math.log(0.5))), 0.05, 0.5),
    }


def momentum_list():
    values = []
    tvalue = 1.0
    for turn in range(ITERS):
        tnext = (1.0 + (1.0 + 4.0 * tvalue * tvalue) ** 0.5) / 2.0
        values.append((tvalue - 1.0) / tnext)
        tvalue = tnext
    return values


def reference(dictionary, patches, initial_codes, support, counts, group_order, penalty):
    blocks_all = dictionary.reshape(PIX, NB, BLOCK)
    momenta = momentum_list()

    def one_group(position):
        group = group_order[position]
        block_ids = support[group]
        dict_blocks = jnp.take(blocks_all, block_ids, axis=1).astype(jnp.float32)
        target = lax.dynamic_slice_in_dim(patches, (group * PATCHES).astype(jnp.int32), PATCHES, 1).astype(jnp.float32)
        live_mask = (jnp.arange(SLOTS) < counts[group]).astype(jnp.float32)[:, None, None]
        thresh = (0.5 * penalty[group])[None, :, None]
        previous = initial_codes[position].reshape(SLOTS, PATCHES, BLOCK).astype(jnp.float32) * live_mask
        point = previous
        for weight in momenta:
            rounded = lax.optimization_barrier(point.astype(jnp.bfloat16)).astype(jnp.float32)
            residual = jnp.einsum("psa,sna->pn", dict_blocks, rounded, precision=lax.Precision.HIGHEST) - target
            residual = lax.optimization_barrier(residual.astype(jnp.bfloat16)).astype(jnp.float32)
            gradient = jnp.einsum("pn,psa->sna", residual, dict_blocks, precision=lax.Precision.HIGHEST)
            stepped = point - 0.5 * gradient
            current = (stepped - jnp.clip(stepped, -thresh, thresh)) * live_mask
            point = current + weight * (current - previous)
            previous = current
        return previous.reshape(SLOTS, PATCHES * BLOCK)

    return lax.map(one_group, jnp.arange(GROUPS, dtype=jnp.int32))
```

```python
import functools

import jax
import jax.numpy as jnp
from jax import lax
from jax.experimental import pallas as pl
from jax.experimental.pallas import tpu as pltpu
from jax.sharding import PartitionSpec as P

BLOCK = 64
SLOTS = 16
PATCHES = 64
ITERS = 3
MEAN_LIVE = 10
LANES = 2 * BLOCK
SLOT_PAIRS = SLOTS // 2
VMEM_LIMIT = 56 * 1024 * 1024


def momentum_list():
    values = []
    tvalue = 1.0
    for turn in range(ITERS):
        tnext = (1.0 + (1.0 + 4.0 * tvalue * tvalue) ** 0.5) / 2.0
        values.append((tvalue - 1.0) / tnext)
        tvalue = tnext
    return values


def swap_halves(value):
    return jnp.concatenate([value[:, BLOCK:], value[:, :BLOCK]], axis=1)


def upper_half(shape):
    return lax.broadcasted_iota(jnp.int32, shape, 1) >= BLOCK


def support_kernel(order, support, counts, dictionary, out, held, sems):
    step = pl.program_id(0)

    def each_copy(index, act):
        group = order[index]
        half = index % 2
        for slot in range(SLOTS):

            @pl.when(slot < counts[group])
            def _():
                start = pl.multiple_of((support[group, slot] // 2) * LANES, LANES)
                act(pltpu.make_async_copy(dictionary.at[:, pl.ds(start, LANES)], held.at[half, slot], sems.at[half, slot]))

    @pl.when(step == 0)
    def _():
        each_copy(step, lambda copy: copy.start())

    @pl.when(step + 1 < pl.num_programs(0))
    def _():
        each_copy(step + 1, lambda copy: copy.start())

    each_copy(step, lambda copy: copy.wait())
    group = order[step]
    live = counts[group]
    half = step % 2
    upper = upper_half(held.shape[2:])
    for pair in range(SLOT_PAIRS):
        parts = []
        for side in range(2):
            slot = 2 * pair + side
            block = held[half, slot]
            swap = (support[group, slot] % 2) != side
            block = jnp.where(swap, swap_halves(block), block)
            parts.append(jnp.where(slot < live, block, jnp.zeros_like(block)))
        out[0, :, pair * LANES : (pair + 1) * LANES] = jnp.where(upper, parts[1], parts[0])


def collect_support(order, support, counts, dictionary):
    groups = order.shape[0]
    rows = dictionary.shape[0]
    return pl.pallas_call(
        support_kernel,
        grid_spec=pltpu.PrefetchScalarGridSpec(
            num_scalar_prefetch=3,
            grid=(groups,),
            in_specs=[pl.BlockSpec(memory_space=pl.ANY)],
            out_specs=pl.BlockSpec((1, rows, SLOTS * BLOCK), lambda j, *_: (j, 0, 0)),
            scratch_shapes=[
                pltpu.VMEM((2, SLOTS, rows, LANES), dictionary.dtype),
                pltpu.SemaphoreType.DMA((2, SLOTS)),
            ],
        ),
        out_shape=jax.ShapeDtypeStruct((groups, rows, SLOTS * BLOCK), dictionary.dtype),
        compiler_params=pltpu.CompilerParams(vmem_limit_bytes=VMEM_LIMIT),
        cost_estimate=pl.CostEstimate(
            flops=0, transcendentals=0, bytes_accessed=3 * groups * rows * SLOTS * BLOCK * 2
        ),
        name="collect_support",
    )(order, support, counts, dictionary)


def gradient_kernel(packed_in, packed_out, order, counts, own, blocks, codes, targets, *rest):
    if packed_out:
        (out, lhs, offset_ref) = rest
    else:
        (out, own_codes, lhs, offset_ref) = rest
    step = pl.program_id(0)
    live = counts[order[step]]

    @pl.when(step == 0)
    def _():
        offset_ref[0] = 0

    offset = offset_ref[0]
    first = offset // 2
    odd = (offset % 2) == 1
    shape = (PATCHES, LANES)
    upper = upper_half(shape)
    side = upper.astype(jnp.int32)
    if packed_in:
        last = codes.shape[0] - 1
        loads = [codes[jnp.minimum(first + pair, last)] for pair in range(SLOT_PAIRS + 1)]
        swapped = [swap_halves(value) for value in loads]
    for pair in range(SLOT_PAIRS):
        if packed_in:
            value = jnp.where(odd, jnp.where(upper, swapped[pair + 1], swapped[pair]), loads[pair])
        else:
            value = codes[0, pair]
        value = jnp.where(2 * pair + side < live, value, jnp.zeros_like(value))
        lhs[:, pair * LANES : (pair + 1) * LANES] = value
        if not packed_out:

            @pl.when(step == own[0])
            def _(pair=pair, value=value):
                own_codes[pair] = value

    matrix = blocks[0]
    residual = lax.dot_general(lhs[...], matrix, (((1,), (1,)), ((), ())), preferred_element_type=jnp.float32)
    residual = (residual - targets[...].astype(jnp.float32)).astype(jnp.bfloat16)
    gradient = jnp.dot(residual, matrix, preferred_element_type=jnp.float32)
    parts = [gradient[:, pair * LANES : (pair + 1) * LANES] for pair in range(SLOT_PAIRS)]
    if packed_out:
        turned = [swap_halves(part) for part in parts]
        final = out.shape[0] - 1
        for pair in range(SLOT_PAIRS + 1):
            straight = parts[min(pair, SLOT_PAIRS - 1)]
            before = turned[max(pair - 1, 0)]
            after = turned[min(pair, SLOT_PAIRS - 1)]
            value = jnp.where(odd, jnp.where(upper, after, before), straight)
            entry = 2 * (first + pair) + side
            mine = (entry >= offset) & (entry < offset + live)
            place = jnp.minimum(first + pair, final)
            out[place] = jnp.where(mine, value.astype(out.dtype), out[place])
    else:
        for pair in range(SLOT_PAIRS):
            out[0, pair] = parts[pair].astype(out.dtype)
    offset_ref[0] = offset + live


def gradient_call(order, counts, own, blocks, codes, targets, packed_in, packed_out, pairs):
    groups, rows, width = blocks.shape
    if packed_in:
        code_spec = pl.BlockSpec((pairs, PATCHES, LANES), lambda j, *_: (0, 0, 0))
    else:
        code_spec = pl.BlockSpec((1, SLOT_PAIRS, PATCHES, LANES), lambda j, *_: (j, 0, 0, 0))
    if packed_out:
        out_shape = [jax.ShapeDtypeStruct((pairs, PATCHES, LANES), jnp.float32)]
        out_specs = [pl.BlockSpec((pairs, PATCHES, LANES), lambda j, *_: (0, 0, 0))]
    else:
        out_shape = [
            jax.ShapeDtypeStruct((groups, SLOT_PAIRS, PATCHES, LANES), jnp.float32),
            jax.ShapeDtypeStruct((SLOT_PAIRS, PATCHES, LANES), jnp.bfloat16),
        ]
        out_specs = [
            pl.BlockSpec((1, SLOT_PAIRS, PATCHES, LANES), lambda j, *_: (j, 0, 0, 0)),
            pl.BlockSpec((SLOT_PAIRS, PATCHES, LANES), lambda j, *_: (0, 0, 0)),
        ]
    return pl.pallas_call(
        functools.partial(gradient_kernel, packed_in, packed_out),
        grid_spec=pltpu.PrefetchScalarGridSpec(
            num_scalar_prefetch=3,
            grid=(groups,),
            in_specs=[
                pl.BlockSpec((1, rows, width), lambda j, *_: (j, 0, 0)),
                code_spec,
                pl.BlockSpec((PATCHES, rows), lambda j, order, *_: (order[j], 0)),
            ],
            out_specs=out_specs,
            scratch_shapes=[pltpu.VMEM((PATCHES, width), jnp.bfloat16), pltpu.SMEM((1,), jnp.int32)],
        ),
        out_shape=out_shape,
        compiler_params=pltpu.CompilerParams(vmem_limit_bytes=VMEM_LIMIT),
        cost_estimate=pl.CostEstimate(
            flops=4 * groups * rows * width * PATCHES, transcendentals=0, bytes_accessed=groups * rows * width * 2
        ),
        name="gradient",
    )(order, counts, own, blocks, codes, targets)


def shrink(value, thresh):
    return value - jnp.clip(value, -thresh, thresh)


def local(dictionary, patches, initial_codes, support, counts, group_order, penalty):
    groups = group_order.shape[0]
    position = lax.axis_index("rows")
    devices = lax.axis_size("rows")
    momenta = momentum_list()
    owned_entries = MEAN_LIVE * groups // devices
    owned_pairs = owned_entries // 2
    pairs = owned_pairs * devices

    laid = initial_codes.reshape(SLOT_PAIRS, 2, PATCHES, BLOCK).transpose(0, 2, 1, 3)
    laid = laid.reshape(1, SLOT_PAIRS, PATCHES, LANES)
    start = lax.all_gather(laid, "rows", axis=0, tiled=True)

    own = position.astype(jnp.int32).reshape(1)
    blocks = collect_support(group_order, support, counts, dictionary)
    targets = patches.T

    half_penalty = 0.5 * penalty
    ends = jnp.cumsum(jnp.take(counts, group_order))
    entry = position * owned_entries + jnp.arange(owned_entries)
    holder = jnp.sum((entry[:, None] >= ends[None, :]).astype(jnp.int32), axis=1)
    thresh = jnp.take(half_penalty, jnp.take(group_order, holder), axis=0)
    thresh = jnp.repeat(thresh.reshape(owned_pairs, 2, PATCHES).transpose(0, 2, 1), BLOCK, axis=2)
    own_thresh = lax.dynamic_index_in_dim(half_penalty, group_order[position], 0, False)[None, :, None]

    def masked_start():
        begins = ends - jnp.take(counts, group_order)
        slot = entry - jnp.take(begins, holder)
        flat = start.reshape(groups * SLOT_PAIRS, PATCHES, 2, BLOCK)
        picked = [
            lax.dynamic_slice(
                flat,
                (holder[i] * SLOT_PAIRS + slot[i] // 2, 0, slot[i] % 2, 0),
                (1, PATCHES, 1, BLOCK),
            ).reshape(PATCHES, BLOCK)
            for i in range(owned_entries)
        ]
        return jnp.stack(
            [jnp.concatenate([picked[2 * i], picked[2 * i + 1]], axis=1) for i in range(owned_pairs)]
        )

    def run(codes, packed_in, packed_out):
        return gradient_call(group_order, counts, own, blocks, codes, targets, packed_in, packed_out, pairs)

    def scatter(value):
        return lax.psum_scatter(value, "rows", scatter_dimension=0, tiled=True)

    point = masked_start().astype(jnp.float32)
    previous = point
    codes = start
    for turn in range(ITERS - 1):
        (partial,) = run(codes, turn > 0, True)
        current = shrink(point - 0.5 * scatter(partial), thresh)
        point = current + momenta[turn] * (current - previous)
        previous = current
        codes = lax.all_gather(point.astype(jnp.bfloat16), "rows", axis=0, tiled=True)
    partial, sent = run(codes, True, False)
    gradient = scatter(partial)[0]
    result = shrink(sent.astype(jnp.float32) - 0.5 * gradient, own_thresh)
    result = result.reshape(SLOT_PAIRS, PATCHES, 2, BLOCK).transpose(0, 2, 1, 3)
    return result.reshape(1, SLOTS, PATCHES * BLOCK)


def solution(mesh):
    in_specs = (
        P("rows", None),
        P("rows", "groups"),
        P(("groups", "rows"), None, None),
        P("groups", None),
        P("groups"),
        P("groups"),
        P("groups", None),
    )
    out_specs = P(("groups", "rows"), None, None)
    return jax.shard_map(local, mesh=mesh, in_specs=in_specs, out_specs=out_specs, check_vma=False)
```

```python
import functools

import jax
import jax.numpy as jnp
from jax import lax
from jax.experimental import pallas as pl
from jax.experimental.pallas import tpu as pltpu
from jax.sharding import PartitionSpec as P

BLOCK = 64
SLOTS = 16
PATCHES = 64
ITERS = 3
MEAN_LIVE = 10
LANES = 2 * BLOCK
SLOT_PAIRS = SLOTS // 2
VMEM_LIMIT = 56 * 1024 * 1024


def momentum_list():
    values = []
    tvalue = 1.0
    for turn in range(ITERS):
        tnext = (1.0 + (1.0 + 4.0 * tvalue * tvalue) ** 0.5) / 2.0
        values.append((tvalue - 1.0) / tnext)
        tvalue = tnext
    return values


def swap_halves(value):
    return jnp.concatenate([value[:, BLOCK:], value[:, :BLOCK]], axis=1)


def upper_half(shape):
    return lax.broadcasted_iota(jnp.int32, shape, 1) >= BLOCK


def support_kernel(order, support, counts, dictionary, out, held, sems):
    step = pl.program_id(0)

    def each_copy(index, act):
        group = order[index]
        half = index % 2
        for slot in range(SLOTS):

            @pl.when(slot < counts[group])
            def _():
                start = pl.multiple_of((support[group, slot] // 2) * LANES, LANES)
                act(pltpu.make_async_copy(dictionary.at[:, pl.ds(start, LANES)], held.at[half, slot], sems.at[half, slot]))

    @pl.when(step == 0)
    def _():
        each_copy(step, lambda copy: copy.start())

    @pl.when(step + 1 < pl.num_programs(0))
    def _():
        each_copy(step + 1, lambda copy: copy.start())

    each_copy(step, lambda copy: copy.wait())
    group = order[step]
    live = counts[group]
    half = step % 2
    upper = upper_half(held.shape[2:])
    for pair in range(SLOT_PAIRS):
        parts = []
        for side in range(2):
            slot = 2 * pair + side
            block = held[half, slot]
            swap = (support[group, slot] % 2) != side
            block = jnp.where(swap, swap_halves(block), block)
            parts.append(jnp.where(slot < live, block, jnp.zeros_like(block)))
        out[0, :, pair * LANES : (pair + 1) * LANES] = jnp.where(upper, parts[1], parts[0])


def collect_support(order, support, counts, dictionary):
    groups = order.shape[0]
    rows = dictionary.shape[0]
    return pl.pallas_call(
        support_kernel,
        grid_spec=pltpu.PrefetchScalarGridSpec(
            num_scalar_prefetch=3,
            grid=(groups,),
            in_specs=[pl.BlockSpec(memory_space=pl.ANY)],
            out_specs=pl.BlockSpec((1, rows, SLOTS * BLOCK), lambda j, *_: (j, 0, 0)),
            scratch_shapes=[
                pltpu.VMEM((2, SLOTS, rows, LANES), dictionary.dtype),
                pltpu.SemaphoreType.DMA((2, SLOTS)),
            ],
        ),
        out_shape=jax.ShapeDtypeStruct((groups, rows, SLOTS * BLOCK), dictionary.dtype),
        compiler_params=pltpu.CompilerParams(vmem_limit_bytes=VMEM_LIMIT),
        cost_estimate=pl.CostEstimate(
            flops=0, transcendentals=0, bytes_accessed=3 * groups * rows * SLOTS * BLOCK * 2
        ),
        name="collect_support",
    )(order, support, counts, dictionary)


def relative_slot(index, me, devices):
    apart = index ^ me
    return (apart % 2) * (devices // 2) + ((apart // 2) % 2) * (devices // 4) + apart // 4


def gradient_kernel(
    packed_in, packed_out, shards, order, counts, own, blocks, near, far, targets, keep, send, extra, codes, lhs, offset_ref
):
    step = pl.program_id(0)
    me = own[0]
    live = counts[order[step]]
    half_in = near.shape[0]
    shard_in = 2 * half_in // shards
    half_out = keep.shape[0]
    shard_out = 2 * half_out // shards

    @pl.when(step == 0)
    def _():
        offset_ref[0] = 0
        codes[:half_in] = near[...]
        codes[half_in:] = far[...]

    offset = offset_ref[0]
    first = offset // 2
    odd = (offset % 2) == 1
    upper = upper_half((PATCHES, LANES))
    side = upper.astype(jnp.int32)

    def place(pair, shard):
        holder = pair // shard
        return relative_slot(holder, me, shards) * shard + (pair - holder * shard)

    def packed(parts):
        turned = [swap_halves(part) for part in parts]
        for pair in range(SLOT_PAIRS + 1):
            straight = parts[min(pair, SLOT_PAIRS - 1)]
            before = turned[max(pair - 1, 0)]
            after = turned[min(pair, SLOT_PAIRS - 1)]
            value = jnp.where(odd, jnp.where(upper, after, before), straight)
            entry = 2 * (first + pair) + side
            yield first + pair, value, (entry >= offset) & (entry < offset + live)

    if packed_in:
        last = 2 * half_in - 1
        loads = [codes[place(jnp.minimum(first + pair, last), shard_in)] for pair in range(SLOT_PAIRS + 1)]
        swapped = [swap_halves(value) for value in loads]
    values = []
    for pair in range(SLOT_PAIRS):
        if packed_in:
            value = jnp.where(odd, jnp.where(upper, swapped[pair + 1], swapped[pair]), loads[pair])
        else:
            value = codes[place(step * SLOT_PAIRS + pair, shard_in)]
        value = jnp.where(2 * pair + side < live, value, jnp.zeros_like(value))
        lhs[:, pair * LANES : (pair + 1) * LANES] = value
        values.append(value)
    if packed_out and not packed_in:
        for pair, value, mine in packed(values):
            nearby = pair - me * shard_out

            @pl.when((nearby >= 0) & (nearby < shard_out))
            def _(value=value, mine=mine, nearby=nearby):
                extra[nearby] = jnp.where(mine, value, extra[nearby])

    if not packed_out:

        @pl.when(step == me)
        def _():
            for pair in range(SLOT_PAIRS):
                extra[pair] = values[pair]

    matrix = blocks[0]
    residual = lax.dot_general(lhs[...], matrix, (((1,), (1,)), ((), ())), preferred_element_type=jnp.float32)
    residual = (residual - targets[...].astype(jnp.float32)).astype(jnp.bfloat16)
    gradient = jnp.dot(residual, matrix, preferred_element_type=jnp.float32)
    parts = [gradient[:, pair * LANES : (pair + 1) * LANES] for pair in range(SLOT_PAIRS)]
    if packed_out:
        final = 2 * half_out - 1
        for pair, value, mine in packed(parts):
            spot = place(jnp.minimum(pair, final), shard_out)

            @pl.when(spot < half_out)
            def _(value=value, mine=mine, spot=spot):
                keep[spot] = jnp.where(mine, value, keep[spot])

            @pl.when(spot >= half_out)
            def _(value=value, mine=mine, spot=spot):
                send[spot - half_out] = jnp.where(mine, value.astype(send.dtype), send[spot - half_out])

    else:
        spot = place(step * SLOT_PAIRS, shard_out)

        @pl.when(spot < half_out)
        def _():
            for pair in range(SLOT_PAIRS):
                keep[spot + pair] = parts[pair]

        @pl.when(spot >= half_out)
        def _():
            for pair in range(SLOT_PAIRS):
                send[spot - half_out + pair] = parts[pair].astype(send.dtype)

    offset_ref[0] = offset + live


def gradient_call(order, counts, own, blocks, near, far, targets, packed_in, packed_out, shards, packed_pairs):
    groups, rows, width = blocks.shape
    half_in = near.shape[0]
    pairs = packed_pairs if packed_out else groups * SLOT_PAIRS
    half_out = pairs // 2
    extra = packed_pairs // shards if packed_out else SLOT_PAIRS
    whole = lambda j, *_: (0, 0, 0)
    shapes = [
        jax.ShapeDtypeStruct((half_out, PATCHES, LANES), jnp.float32),
        jax.ShapeDtypeStruct((half_out, PATCHES, LANES), jnp.bfloat16),
        jax.ShapeDtypeStruct((extra, PATCHES, LANES), jnp.bfloat16),
    ]
    return pl.pallas_call(
        functools.partial(gradient_kernel, packed_in, packed_out, shards),
        grid_spec=pltpu.PrefetchScalarGridSpec(
            num_scalar_prefetch=3,
            grid=(groups,),
            in_specs=[
                pl.BlockSpec((1, rows, width), lambda j, *_: (j, 0, 0)),
                pl.BlockSpec((half_in, PATCHES, LANES), whole),
                pl.BlockSpec((half_in, PATCHES, LANES), whole),
                pl.BlockSpec((PATCHES, rows), lambda j, order, *_: (order[j], 0)),
            ],
            out_specs=[pl.BlockSpec(shape.shape, whole) for shape in shapes],
            scratch_shapes=[
                pltpu.VMEM((2 * half_in, PATCHES, LANES), jnp.bfloat16),
                pltpu.VMEM((PATCHES, width), jnp.bfloat16),
                pltpu.SMEM((1,), jnp.int32),
            ],
        ),
        out_shape=shapes,
        compiler_params=pltpu.CompilerParams(vmem_limit_bytes=VMEM_LIMIT),
        cost_estimate=pl.CostEstimate(
            flops=4 * groups * rows * width * PATCHES, transcendentals=0, bytes_accessed=groups * rows * width * 2
        ),
        name="gradient",
    )(order, counts, own, blocks, near, far, targets)


def exchange(value, distance):
    devices = lax.axis_size("rows")
    return lax.ppermute(value, "rows", [(i, i ^ distance) for i in range(devices)])


def gather_shards(own):
    devices = lax.axis_size("rows")
    parts = [own] + [exchange(own, 4 * k) for k in range(1, devices // 4)]
    quarter = jnp.concatenate(parts, axis=0)
    near = jnp.concatenate([quarter, exchange(quarter, 2)], axis=0)
    return near, exchange(near, 1)


def reduce_shards(keep, send):
    devices = lax.axis_size("rows")
    half = keep + exchange(send, 1).astype(jnp.float32)
    middle = half.shape[0] // 2
    quarter = half[:middle] + exchange(half[middle:].astype(jnp.bfloat16), 2).astype(jnp.float32)
    size = quarter.shape[0] // (devices // 4)
    sent = quarter.astype(jnp.bfloat16)
    total = quarter[:size]
    for k in range(1, devices // 4):
        total = total + exchange(sent[k * size : (k + 1) * size], 4 * k).astype(jnp.float32)
    return total


def shrink(value, thresh):
    return value - jnp.clip(value, -thresh, thresh)


def local(dictionary, patches, initial_codes, support, counts, group_order, penalty):
    groups = group_order.shape[0]
    position = lax.axis_index("rows")
    devices = lax.axis_size("rows")
    momenta = momentum_list()
    owned_entries = MEAN_LIVE * groups // devices
    owned_pairs = owned_entries // 2
    pairs = owned_pairs * devices

    laid = initial_codes.reshape(SLOT_PAIRS, 2, PATCHES, BLOCK).transpose(0, 2, 1, 3)
    near, far = gather_shards(laid.reshape(SLOT_PAIRS, PATCHES, LANES))

    own = position.astype(jnp.int32).reshape(1)
    blocks = collect_support(group_order, support, counts, dictionary)
    targets = patches.T

    half_penalty = 0.5 * penalty
    ends = jnp.cumsum(jnp.take(counts, group_order))
    entry = position * owned_entries + jnp.arange(owned_entries)
    holder = jnp.sum((entry[:, None] >= ends[None, :]).astype(jnp.int32), axis=1)
    thresh = jnp.take(half_penalty, jnp.take(group_order, holder), axis=0)
    thresh = jnp.repeat(thresh.reshape(owned_pairs, 2, PATCHES).transpose(0, 2, 1), BLOCK, axis=2)
    own_thresh = lax.dynamic_index_in_dim(half_penalty, group_order[position], 0, False)[None, :, None]

    def run(near, far, packed_in, packed_out):
        return gradient_call(
            group_order, counts, own, blocks, near, far, targets, packed_in, packed_out, devices, pairs
        )

    point = previous = None
    for turn in range(ITERS - 1):
        keep, send, extra = run(near, far, turn > 0, True)
        if turn == 0:
            point = previous = extra.astype(jnp.float32)
        current = shrink(point - 0.5 * reduce_shards(keep, send), thresh)
        point = current + momenta[turn] * (current - previous)
        previous = current
        near, far = gather_shards(point.astype(jnp.bfloat16))
    keep, send, sent = run(near, far, True, False)
    result = shrink(sent.astype(jnp.float32) - 0.5 * reduce_shards(keep, send), own_thresh)
    result = result.reshape(SLOT_PAIRS, PATCHES, 2, BLOCK).transpose(0, 2, 1, 3)
    return result.reshape(1, SLOTS, PATCHES * BLOCK)


def solution(mesh):
    in_specs = (
        P("rows", None),
        P("rows", "groups"),
        P(("groups", "rows"), None, None),
        P("groups", None),
        P("groups"),
        P("groups"),
        P("groups", None),
    )
    out_specs = P(("groups", "rows"), None, None)
    return jax.shard_map(local, mesh=mesh, in_specs=in_specs, out_specs=out_specs, check_vma=False)
```

```python
import functools

import jax
import jax.numpy as jnp
from jax import lax
from jax.experimental import pallas as pl
from jax.experimental.pallas import tpu as pltpu
from jax.sharding import PartitionSpec as P

BLOCK = 64
SLOTS = 16
PATCHES = 64
ITERS = 3
MEAN_LIVE = 10
LANES = 2 * BLOCK
SLOT_PAIRS = SLOTS // 2
VMEM_LIMIT = 40 * 1024 * 1024


def momentum_list():
    values = []
    tvalue = 1.0
    for turn in range(ITERS):
        tnext = (1.0 + (1.0 + 4.0 * tvalue * tvalue) ** 0.5) / 2.0
        values.append((tvalue - 1.0) / tnext)
        tvalue = tnext
    return values


def swap_halves(value):
    return jnp.concatenate([value[:, BLOCK:], value[:, :BLOCK]], axis=1)


def upper_half(shape):
    return lax.broadcasted_iota(jnp.int32, shape, 1) >= BLOCK


def support_kernel(order, support, counts, dictionary, out, held, ids, sems, out_sems):
    rows = held.shape[1]

    def fetch(entry, block):
        start = pl.multiple_of((block // 2) * LANES, LANES)
        return pltpu.make_async_copy(dictionary.at[:, pl.ds(start, LANES)], held.at[entry], sems.at[entry])

    def start_group(index, offset):
        group = order[index]
        live = counts[group]

        def start_slot(slot, carry):
            block = support[group, slot]
            ids[offset + slot] = block
            fetch(offset + slot, block).start()
            return carry

        lax.fori_loop(0, live, start_slot, 0)
        return offset + live

    lax.fori_loop(0, order.shape[0], start_group, 0)
    upper = upper_half((rows, LANES))

    def store(pair):
        return pltpu.make_async_copy(held.at[2 * pair], out.at[pair], out_sems.at[pair])

    def pack(pair, carry):
        parts = []
        for side in range(2):
            entry = 2 * pair + side
            block = ids[entry]
            fetch(entry, block).wait()
            value = held[entry]
            parts.append(jnp.where((block % 2) != side, swap_halves(value), value))
        held[2 * pair] = jnp.where(upper, parts[1], parts[0])
        store(pair).start()
        return carry

    pairs = out.shape[0]
    lax.fori_loop(0, pairs, pack, 0)

    def drain(pair, carry):
        store(pair).wait()
        return carry

    lax.fori_loop(0, pairs, drain, 0)


def collect_support(order, support, counts, dictionary, pairs):
    rows = dictionary.shape[0]
    return pl.pallas_call(
        support_kernel,
        grid_spec=pltpu.PrefetchScalarGridSpec(
            num_scalar_prefetch=3,
            grid=(),
            in_specs=[pl.BlockSpec(memory_space=pl.ANY)],
            out_specs=pl.BlockSpec(memory_space=pl.ANY),
            scratch_shapes=[
                pltpu.VMEM((2 * pairs, rows, LANES), dictionary.dtype),
                pltpu.SMEM((2 * pairs,), jnp.int32),
                pltpu.SemaphoreType.DMA((2 * pairs,)),
                pltpu.SemaphoreType.DMA((pairs,)),
            ],
        ),
        out_shape=jax.ShapeDtypeStruct((pairs, rows, LANES), dictionary.dtype),
        compiler_params=pltpu.CompilerParams(vmem_limit_bytes=VMEM_LIMIT),
        cost_estimate=pl.CostEstimate(
            flops=0, transcendentals=0, bytes_accessed=3 * pairs * rows * LANES * 2
        ),
        name="collect_support",
    )(order, support, counts, dictionary)


def relative_slot(index, me, devices):
    apart = index ^ me
    return (apart % 2) * (devices // 2) + ((apart // 2) % 2) * (devices // 4) + apart // 4


def gradient_kernel(
    packed_in, packed_out, shards, order, counts, own, blocks, near, far, targets, keep, send, extra,
    held, codes, total, start_codes, offsets, sems, code_sems,
):
    groups = order.shape[0]
    me = own[0]
    pairs = blocks.shape[0]
    piece = pairs // shards
    half_in = near.shape[0]
    shard_in = 2 * half_in // shards
    half_out = keep.shape[0]
    shard_out = 2 * half_out // shards

    def load(index):
        span = pl.ds(index * piece, piece)
        return pltpu.make_async_copy(blocks.at[span], held.at[span], sems.at[index])

    code_loads = [
        pltpu.make_async_copy(near, codes.at[pl.ds(0, half_in)], code_sems.at[0]),
        pltpu.make_async_copy(far, codes.at[pl.ds(half_in, half_in)], code_sems.at[1]),
    ]
    for copy in code_loads:
        copy.start()
    for index in range(shards):
        load(index).start()
    held[pairs:] = jnp.zeros((held.shape[0] - pairs,) + held.shape[1:], held.dtype)
    for copy in code_loads:
        copy.wait()

    upper = upper_half((PATCHES, LANES))
    side = upper.astype(jnp.int32)

    def place(pair, shard):
        holder = pair // shard
        return relative_slot(holder, me, shards) * shard + (pair - holder * shard)

    def spot_of(pair, shard):
        return jnp.where(pair < pairs, place(jnp.minimum(pair, pairs - 1), shard), pair)

    def shifted(parts, count, odd, ahead):
        turned = [swap_halves(part) for part in parts]
        last = len(parts) - 1
        moved = []
        for pair in range(count):
            low, high = (pair, pair + 1) if ahead else (pair - 1, pair)
            low, high = min(max(low, 0), last), min(max(high, 0), last)
            value = jnp.where(upper, turned[high], turned[low])
            moved.append(jnp.where(odd, value, parts[min(pair, last)]))
        return moved

    def read_codes(index, offset, live, count):
        first = offset // 2
        if packed_in:
            parts = [codes[place(jnp.minimum(first + pair, pairs - 1), shard_in)] for pair in range(count)]
        else:
            base = place(index * SLOT_PAIRS, shard_in)
            slots = min(count, SLOT_PAIRS)
            parts = shifted([codes[base + pair] for pair in range(slots)], count, offset % 2 == 1, False)
        masked = []
        for pair, part in enumerate(parts):
            entry = 2 * (first + pair) + side
            mine = (entry >= offset) & (entry < offset + live)
            masked.append(jnp.where(mine, part, jnp.zeros_like(part)))
        return masked

    def write_packed(ref, parts, offset, shard):
        first = offset // 2
        for pair, part in enumerate(parts):
            spot = spot_of(first + pair, shard)
            if pair == 0:
                part = jnp.where(upper | (offset % 2 == 0), part, ref[spot])
            ref[spot] = part

    def one_group(index, offset, live, count):
        first = offset // 2
        parts = read_codes(index, offset, live, count)
        if packed_out and not packed_in:
            first_pair = offset // 2
            for pair, part in enumerate(parts):
                if pair == 0:
                    part = jnp.where(upper | (offset % 2 == 0), part, start_codes[first_pair])
                start_codes[first_pair + pair] = part
        matrix = jnp.concatenate([held[first + pair] for pair in range(count)], axis=1)
        point = jnp.concatenate(parts, axis=1)
        residual = lax.dot_general(point, matrix, (((1,), (1,)), ((), ())), preferred_element_type=jnp.float32)
        column = pl.multiple_of(order[index] * PATCHES, PATCHES)
        target = targets[pl.ds(column, PATCHES), :].astype(jnp.float32)
        residual = (residual - target).astype(jnp.bfloat16)
        gradient = jnp.dot(residual, matrix, preferred_element_type=jnp.float32)
        grads = [gradient[:, pair * LANES : (pair + 1) * LANES] for pair in range(count)]
        if packed_out:
            write_packed(total, grads, offset, shard_out)
        else:
            base = place(index * SLOT_PAIRS, shard_out)
            moved = shifted(grads, min(count, SLOT_PAIRS), offset % 2 == 1, True)
            for pair in range(SLOT_PAIRS):
                if pair < len(moved):
                    value = jnp.where(2 * pair + side < live, moved[pair], 0.0)
                else:
                    value = jnp.zeros((PATCHES, LANES), jnp.float32)
                total[base + pair] = value

    def two_groups(step, carry):
        offset, waited = carry
        picks = []
        chunks = 1
        for index in (2 * step, 2 * step + 1):
            live = counts[order[index]]
            offsets[index] = offset
            picks.append((index, offset, live))
            chunks = jnp.maximum(chunks, (live + offset % 2 + 3) // 4)
            offset = offset + live
        reach = jnp.minimum(picks[1][1] // 2 + 2 * chunks - 1, pairs - 1)
        needed = reach // piece + 1

        def wait_piece(index, inner):
            load(index).wait()
            return inner

        lax.fori_loop(waited, needed, wait_piece, 0)
        for count in range(1, SLOTS // 4 + 2):

            @pl.when(chunks == count)
            def _(count=count):
                for pick in picks:
                    one_group(*pick, 2 * count)

        return offset, jnp.maximum(waited, needed)

    _, waited = lax.fori_loop(0, groups // 2, two_groups, (jnp.int32(0), jnp.int32(0)))

    def wait_rest(index, inner):
        load(index).wait()
        return inner

    lax.fori_loop(waited, shards, wait_rest, 0)
    keep[...] = total[:half_out]
    send[...] = total[half_out : 2 * half_out].astype(send.dtype)
    if packed_out and not packed_in:
        extra[...] = start_codes[pl.ds(me * shard_out, shard_out)]
    elif not packed_out:
        mine = offsets[me]
        parts = read_codes(me, mine, counts[order[me]], SLOT_PAIRS + 1)
        for pair, part in enumerate(shifted(parts, SLOT_PAIRS, mine % 2 == 1, True)):
            extra[pair] = part
    else:
        extra[...] = jnp.zeros(extra.shape, extra.dtype)


def gradient_call(order, counts, own, blocks, near, far, targets, packed_in, packed_out, shards):
    pairs, rows, _ = blocks.shape
    groups = order.shape[0]
    half_in = near.shape[0]
    half_out = (pairs if packed_out else groups * SLOT_PAIRS) // 2
    extra = pairs // shards if packed_out else SLOT_PAIRS
    spare = SLOT_PAIRS + 2
    tile = (PATCHES, LANES)
    return pl.pallas_call(
        functools.partial(gradient_kernel, packed_in, packed_out, shards),
        grid_spec=pltpu.PrefetchScalarGridSpec(
            num_scalar_prefetch=3,
            grid=(),
            in_specs=[
                pl.BlockSpec(memory_space=pl.ANY),
                pl.BlockSpec(memory_space=pl.ANY),
                pl.BlockSpec(memory_space=pl.ANY),
                pl.BlockSpec(memory_space=pltpu.VMEM),
            ],
            out_specs=[pl.BlockSpec(memory_space=pltpu.VMEM)] * 3,
            scratch_shapes=[
                pltpu.VMEM((pairs + spare, rows, LANES), jnp.bfloat16),
                pltpu.VMEM((2 * half_in,) + tile, jnp.bfloat16),
                pltpu.VMEM((2 * half_out + spare,) + tile, jnp.float32),
                pltpu.VMEM((pairs + spare,) + tile, jnp.bfloat16),
                pltpu.SMEM((groups,), jnp.int32),
                pltpu.SemaphoreType.DMA((shards,)),
                pltpu.SemaphoreType.DMA((2,)),
            ],
        ),
        out_shape=[
            jax.ShapeDtypeStruct((half_out,) + tile, jnp.float32),
            jax.ShapeDtypeStruct((half_out,) + tile, jnp.bfloat16),
            jax.ShapeDtypeStruct((extra,) + tile, jnp.bfloat16),
        ],
        compiler_params=pltpu.CompilerParams(vmem_limit_bytes=VMEM_LIMIT),
        cost_estimate=pl.CostEstimate(
            flops=4 * pairs * rows * LANES * PATCHES, transcendentals=0, bytes_accessed=pairs * rows * LANES * 2
        ),
        name="gradient",
    )(order, counts, own, blocks, near, far, targets)


def exchange(value, distance):
    devices = lax.axis_size("rows")
    return lax.ppermute(value, "rows", [(i, i ^ distance) for i in range(devices)])


def gather_shards(own, beside=None):
    devices = lax.axis_size("rows")
    parts = [own] + [exchange(own, 4 * k) for k in range(1, devices // 4)]
    quarter = jnp.concatenate(parts, axis=0)
    near = jnp.concatenate([quarter, exchange(quarter, 2)], axis=0)
    if beside is not None:
        near, beside = lax.optimization_barrier((near, beside))
        return near, exchange(near, 1), beside
    return near, exchange(near, 1)


def reduce_shards(keep, send):
    devices = lax.axis_size("rows")
    half = keep + exchange(send, 1).astype(jnp.float32)
    middle = half.shape[0] // 2
    quarter = half[:middle] + exchange(half[middle:].astype(jnp.bfloat16), 2).astype(jnp.float32)
    size = quarter.shape[0] // (devices // 4)
    sent = quarter.astype(jnp.bfloat16)
    total = quarter[:size]
    for k in range(1, devices // 4):
        total = total + exchange(sent[k * size : (k + 1) * size], 4 * k).astype(jnp.float32)
    return total


def shrink(value, thresh):
    return value - jnp.clip(value, -thresh, thresh)


def local(dictionary, patches, initial_codes, support, counts, group_order, penalty):
    groups = group_order.shape[0]
    position = lax.axis_index("rows")
    devices = lax.axis_size("rows")
    momenta = momentum_list()
    owned_entries = MEAN_LIVE * groups // devices
    owned_pairs = owned_entries // 2
    pairs = owned_pairs * devices

    laid = initial_codes.reshape(SLOT_PAIRS, 2, PATCHES, BLOCK).transpose(0, 2, 1, 3)
    blocks = collect_support(group_order, support, counts, dictionary, pairs)
    near, far, blocks = gather_shards(laid.reshape(SLOT_PAIRS, PATCHES, LANES), blocks)

    own = position.astype(jnp.int32).reshape(1)
    targets = patches.T

    half_penalty = 0.5 * penalty
    ends = jnp.cumsum(jnp.take(counts, group_order))
    entry = position * owned_entries + jnp.arange(owned_entries)
    holder = jnp.sum((entry[:, None] >= ends[None, :]).astype(jnp.int32), axis=1)
    thresh = jnp.take(half_penalty, jnp.take(group_order, holder), axis=0)
    thresh = jnp.repeat(thresh.reshape(owned_pairs, 2, PATCHES).transpose(0, 2, 1), BLOCK, axis=2)
    own_thresh = lax.dynamic_index_in_dim(half_penalty, group_order[position], 0, False)[None, :, None]

    def run(near, far, packed_in, packed_out):
        return gradient_call(
            group_order, counts, own, blocks, near, far, targets, packed_in, packed_out, devices
        )

    point = previous = None
    for turn in range(ITERS - 1):
        keep, send, extra = run(near, far, turn > 0, True)
        if turn == 0:
            point = previous = extra.astype(jnp.float32)
        current = shrink(point - 0.5 * reduce_shards(keep, send), thresh)
        point = current + momenta[turn] * (current - previous)
        previous = current
        near, far = gather_shards(point.astype(jnp.bfloat16))
    keep, send, sent = run(near, far, True, False)
    result = shrink(sent.astype(jnp.float32) - 0.5 * reduce_shards(keep, send), own_thresh)
    result = result.reshape(SLOT_PAIRS, PATCHES, 2, BLOCK).transpose(0, 2, 1, 3)
    return result.reshape(1, SLOTS, PATCHES * BLOCK)


def solution(mesh):
    in_specs = (
        P("rows", None),
        P("rows", "groups"),
        P(("groups", "rows"), None, None),
        P("groups", None),
        P("groups"),
        P("groups"),
        P("groups", None),
    )
    out_specs = P(("groups", "rows"), None, None)
    return jax.shard_map(local, mesh=mesh, in_specs=in_specs, out_specs=out_specs, check_vma=False)
```

```python
import functools

import jax
import jax.numpy as jnp
from jax import lax
from jax.experimental import pallas as pl
from jax.experimental.pallas import tpu as pltpu
from jax.sharding import PartitionSpec as P

BLOCK = 64
SLOTS = 16
PATCHES = 64
ITERS = 3
MEAN_LIVE = 10
LANES = 2 * BLOCK
SLOT_PAIRS = SLOTS // 2
VMEM_LIMIT = 32 * 1024 * 1024
SUPPORT_VMEM = 58 * 1024 * 1024


def momentum_list():
    values = []
    tvalue = 1.0
    for turn in range(ITERS):
        tnext = (1.0 + (1.0 + 4.0 * tvalue * tvalue) ** 0.5) / 2.0
        values.append((tvalue - 1.0) / tnext)
        tvalue = tnext
    return values


def swap_halves(value):
    return jnp.concatenate([value[:, BLOCK:], value[:, :BLOCK]], axis=1)


def upper_half(shape):
    return lax.broadcasted_iota(jnp.int32, shape, 1) >= BLOCK


def support_kernel(begin, order, support, counts, dictionary, out, held, picks, ids, sems, out_sems):
    entries, rows, _ = held.shape
    pairs = entries // 2

    def fetch(entry, block):
        start = pl.multiple_of((block // 2) * LANES, LANES)
        return pltpu.make_async_copy(dictionary.at[:, pl.ds(start, LANES)], held.at[entry], sems.at[entry])

    def start_group(index, offset):
        group = order[index]
        live = counts[group]

        def start_slot(slot, carry):
            block = support[group, slot]
            ids[offset + slot] = block
            fetch(offset + slot, block).start()
            return carry

        lax.fori_loop(jnp.clip(-offset, 0, live), jnp.clip(entries - offset, 0, live), start_slot, 0)
        return offset + live

    lax.fori_loop(0, order.shape[0], start_group, jnp.int32(-begin))
    shape = (2 * LANES, LANES)
    source = lax.broadcasted_iota(jnp.int32, shape, 0)
    target = lax.broadcasted_iota(jnp.int32, shape, 1)
    for choice in range(4):
        wanted = jnp.where(target < BLOCK, (choice % 2) * BLOCK + target, LANES + (choice // 2) * BLOCK + target - BLOCK)
        picks[choice] = (source == wanted).astype(jnp.float32).astype(jnp.bfloat16)

    def store(pair):
        return pltpu.make_async_copy(held.at[2 * pair], out.at[pair], out_sems.at[pair])

    def pack(step, carry):
        for pair in (2 * step, 2 * step + 1):
            fetch(2 * pair, ids[2 * pair]).wait()
            fetch(2 * pair + 1, ids[2 * pair + 1]).wait()
        packed = []
        for pair in (2 * step, 2 * step + 1):
            choice = ids[2 * pair] % 2 + 2 * (ids[2 * pair + 1] % 2)
            both = jnp.concatenate([held[2 * pair], held[2 * pair + 1]], axis=1)
            packed.append(jnp.dot(both, picks[choice], preferred_element_type=jnp.float32).astype(jnp.bfloat16))
        for pair, value in zip((2 * step, 2 * step + 1), packed):
            held[2 * pair] = value
            store(pair).start()
        return carry

    lax.fori_loop(0, pairs // 2, pack, 0)

    def drain(pair, carry):
        store(pair).wait()
        return carry

    lax.fori_loop(0, pairs, drain, 0)


def collect_support(order, support, counts, dictionary, begin, entries):
    rows = dictionary.shape[0]
    pairs = entries // 2
    return pl.pallas_call(
        functools.partial(support_kernel, begin),
        grid_spec=pltpu.PrefetchScalarGridSpec(
            num_scalar_prefetch=3,
            grid=(),
            in_specs=[pl.BlockSpec(memory_space=pl.ANY)],
            out_specs=pl.BlockSpec(memory_space=pl.ANY),
            scratch_shapes=[
                pltpu.VMEM((entries, rows, LANES), dictionary.dtype),
                pltpu.VMEM((4, 2 * LANES, LANES), jnp.bfloat16),
                pltpu.SMEM((entries,), jnp.int32),
                pltpu.SemaphoreType.DMA((entries,)),
                pltpu.SemaphoreType.DMA((pairs,)),
            ],
        ),
        out_shape=jax.ShapeDtypeStruct((pairs, rows, LANES), dictionary.dtype),
        compiler_params=pltpu.CompilerParams(vmem_limit_bytes=SUPPORT_VMEM),
        cost_estimate=pl.CostEstimate(
            flops=0, transcendentals=0, bytes_accessed=3 * pairs * rows * LANES * 2
        ),
        name="collect_support",
    )(order, support, counts, dictionary)


def relative_slot(index, me, devices):
    apart = index ^ me
    return (apart % 2) * (devices // 2) + ((apart // 2) % 2) * (devices // 4) + apart // 4


def gradient_kernel(
    packed_in, packed_out, shards, order, counts, own, blocks, blocks_b, near, far, targets, keep, send, extra,
    held, codes, total, start_codes, offsets, sems, code_sems,
):
    groups = order.shape[0]
    me = own[0]
    pairs = 2 * blocks.shape[0]
    piece = pairs // shards
    half_in = near.shape[0]
    shard_in = 2 * half_in // shards
    half_out = keep.shape[0]
    shard_out = 2 * half_out // shards

    def load(index, source=blocks, begin=0):
        span = pl.ds(index * piece, piece)
        return pltpu.make_async_copy(source.at[pl.ds(begin, piece)], held.at[span], sems.at[index])

    code_loads = [
        pltpu.make_async_copy(near, codes.at[pl.ds(0, half_in)], code_sems.at[0]),
        pltpu.make_async_copy(far, codes.at[pl.ds(half_in, half_in)], code_sems.at[1]),
    ]
    for copy in code_loads:
        copy.start()
    for index in range(shards):
        source = (blocks, blocks_b)[2 * index // shards]
        load(index, source, (index % (shards // 2)) * piece).start()
    held[pairs:] = jnp.zeros((held.shape[0] - pairs,) + held.shape[1:], held.dtype)
    for copy in code_loads:
        copy.wait()

    upper = upper_half((PATCHES, LANES))
    side = upper.astype(jnp.int32)

    def place(pair, shard):
        holder = pair // shard
        return relative_slot(holder, me, shards) * shard + (pair - holder * shard)

    def spot_of(pair, shard):
        return jnp.where(pair < pairs, place(jnp.minimum(pair, pairs - 1), shard), pair)

    def shifted(parts, count, odd, ahead):
        turned = [swap_halves(part) for part in parts]
        last = len(parts) - 1
        moved = []
        for pair in range(count):
            low, high = (pair, pair + 1) if ahead else (pair - 1, pair)
            low, high = min(max(low, 0), last), min(max(high, 0), last)
            value = jnp.where(upper, turned[high], turned[low])
            moved.append(jnp.where(odd, value, parts[min(pair, last)]))
        return moved

    def read_codes(index, offset, live, count):
        first = offset // 2
        if packed_in:
            parts = [codes[place(jnp.minimum(first + pair, pairs - 1), shard_in)] for pair in range(count)]
        else:
            base = place(index * SLOT_PAIRS, shard_in)
            slots = min(count, SLOT_PAIRS)
            parts = shifted([codes[base + pair] for pair in range(slots)], count, offset % 2 == 1, False)
        masked = []
        for pair, part in enumerate(parts):
            entry = 2 * (first + pair) + side
            mine = (entry >= offset) & (entry < offset + live)
            masked.append(jnp.where(mine, part, jnp.zeros_like(part)))
        return masked

    def write_packed(ref, parts, offset, shard):
        first = offset // 2
        for pair, part in enumerate(parts):
            spot = spot_of(first + pair, shard)
            if pair == 0:
                part = jnp.where(upper | (offset % 2 == 0), part, ref[spot])
            ref[spot] = part

    def one_group(index, offset, live, count):
        first = offset // 2
        parts = read_codes(index, offset, live, count)
        if packed_out and not packed_in:
            first_pair = offset // 2
            for pair, part in enumerate(parts):
                if pair == 0:
                    part = jnp.where(upper | (offset % 2 == 0), part, start_codes[first_pair])
                start_codes[first_pair + pair] = part
        matrix = jnp.concatenate([held[first + pair] for pair in range(count)], axis=1)
        point = jnp.concatenate(parts, axis=1)
        residual = lax.dot_general(point, matrix, (((1,), (1,)), ((), ())), preferred_element_type=jnp.float32)
        column = pl.multiple_of(order[index] * PATCHES, PATCHES)
        target = targets[pl.ds(column, PATCHES), :].astype(jnp.float32)
        residual = (residual - target).astype(jnp.bfloat16)
        gradient = jnp.dot(residual, matrix, preferred_element_type=jnp.float32)
        grads = [gradient[:, pair * LANES : (pair + 1) * LANES] for pair in range(count)]
        if packed_out:
            write_packed(total, grads, offset, shard_out)
        else:
            base = place(index * SLOT_PAIRS, shard_out)
            moved = shifted(grads, min(count, SLOT_PAIRS), offset % 2 == 1, True)
            for pair in range(SLOT_PAIRS):
                if pair < len(moved):
                    value = jnp.where(2 * pair + side < live, moved[pair], 0.0)
                else:
                    value = jnp.zeros((PATCHES, LANES), jnp.float32)
                total[base + pair] = value

    def two_groups(step, carry):
        offset, waited = carry
        picks = []
        chunks = 1
        for index in (2 * step, 2 * step + 1):
            live = counts[order[index]]
            offsets[index] = offset
            picks.append((index, offset, live))
            chunks = jnp.maximum(chunks, (live + offset % 2 + 3) // 4)
            offset = offset + live
        reach = jnp.minimum(picks[1][1] // 2 + 2 * chunks - 1, pairs - 1)
        needed = reach // piece + 1

        def wait_piece(index, inner):
            load(index).wait()
            return inner

        lax.fori_loop(waited, needed, wait_piece, 0)
        for count in range(1, SLOTS // 4 + 2):

            @pl.when(chunks == count)
            def _(count=count):
                for pick in picks:
                    one_group(*pick, 2 * count)

        return offset, jnp.maximum(waited, needed)

    _, waited = lax.fori_loop(0, groups // 2, two_groups, (jnp.int32(0), jnp.int32(0)))

    def wait_rest(index, inner):
        load(index).wait()
        return inner

    lax.fori_loop(waited, shards, wait_rest, 0)
    keep[...] = total[:half_out]
    send[...] = total[half_out : 2 * half_out].astype(send.dtype)
    if packed_out and not packed_in:
        extra[...] = start_codes[pl.ds(me * shard_out, shard_out)]
    elif not packed_out:
        mine = offsets[me]
        parts = read_codes(me, mine, counts[order[me]], SLOT_PAIRS + 1)
        for pair, part in enumerate(shifted(parts, SLOT_PAIRS, mine % 2 == 1, True)):
            extra[pair] = part
    else:
        extra[...] = jnp.zeros(extra.shape, extra.dtype)


def gradient_call(order, counts, own, blocks, near, far, targets, packed_in, packed_out, shards):
    pairs, rows, _ = blocks[0].shape
    pairs = 2 * pairs
    groups = order.shape[0]
    half_in = near.shape[0]
    half_out = (pairs if packed_out else groups * SLOT_PAIRS) // 2
    extra = pairs // shards if packed_out else SLOT_PAIRS
    spare = SLOT_PAIRS + 2
    tile = (PATCHES, LANES)
    return pl.pallas_call(
        functools.partial(gradient_kernel, packed_in, packed_out, shards),
        grid_spec=pltpu.PrefetchScalarGridSpec(
            num_scalar_prefetch=3,
            grid=(),
            in_specs=[pl.BlockSpec(memory_space=pl.ANY)] * 4 + [pl.BlockSpec(memory_space=pltpu.VMEM)],
            out_specs=[pl.BlockSpec(memory_space=pltpu.VMEM)] * 3,
            scratch_shapes=[
                pltpu.VMEM((pairs + spare, rows, LANES), jnp.bfloat16),
                pltpu.VMEM((2 * half_in,) + tile, jnp.bfloat16),
                pltpu.VMEM((2 * half_out + spare,) + tile, jnp.float32),
                pltpu.VMEM((pairs + spare,) + tile, jnp.bfloat16),
                pltpu.SMEM((groups,), jnp.int32),
                pltpu.SemaphoreType.DMA((shards,)),
                pltpu.SemaphoreType.DMA((2,)),
            ],
        ),
        out_shape=[
            jax.ShapeDtypeStruct((half_out,) + tile, jnp.float32),
            jax.ShapeDtypeStruct((half_out,) + tile, jnp.bfloat16),
            jax.ShapeDtypeStruct((extra,) + tile, jnp.bfloat16),
        ],
        compiler_params=pltpu.CompilerParams(vmem_limit_bytes=VMEM_LIMIT),
        cost_estimate=pl.CostEstimate(
            flops=4 * pairs * rows * LANES * PATCHES, transcendentals=0, bytes_accessed=pairs * rows * LANES * 2
        ),
        name="gradient",
    )(order, counts, own, *blocks, near, far, targets)


def exchange(value, distance):
    devices = lax.axis_size("rows")
    return lax.ppermute(value, "rows", [(i, i ^ distance) for i in range(devices)])


def gather_shards(own, beside=()):
    devices = lax.axis_size("rows")
    parts = [own] + [exchange(own, 4 * k) for k in range(1, devices // 4)]
    quarter = jnp.concatenate(parts, axis=0)
    if beside:
        quarter, first = lax.optimization_barrier((quarter, beside[0]))
    near = jnp.concatenate([quarter, exchange(quarter, 2)], axis=0)
    if beside:
        near, second = lax.optimization_barrier((near, beside[1]))
        return near, exchange(near, 1), (first, second)
    return near, exchange(near, 1)


def reduce_shards(keep, send):
    devices = lax.axis_size("rows")
    half = keep + exchange(send, 1).astype(jnp.float32)
    middle = half.shape[0] // 2
    quarter = half[:middle] + exchange(half[middle:].astype(jnp.bfloat16), 2).astype(jnp.float32)
    size = quarter.shape[0] // (devices // 4)
    sent = quarter.astype(jnp.bfloat16)
    total = quarter[:size]
    for k in range(1, devices // 4):
        total = total + exchange(sent[k * size : (k + 1) * size], 4 * k).astype(jnp.float32)
    return total


def shrink(value, thresh):
    return value - jnp.clip(value, -thresh, thresh)


def local(dictionary, patches, initial_codes, support, counts, group_order, penalty):
    groups = group_order.shape[0]
    position = lax.axis_index("rows")
    devices = lax.axis_size("rows")
    momenta = momentum_list()
    owned_entries = MEAN_LIVE * groups // devices
    owned_pairs = owned_entries // 2
    pairs = owned_pairs * devices

    laid = initial_codes.reshape(SLOT_PAIRS, 2, PATCHES, BLOCK).transpose(0, 2, 1, 3)
    blocks = [collect_support(group_order, support, counts, dictionary, begin, pairs) for begin in (0, pairs)]
    near, far, blocks = gather_shards(laid.reshape(SLOT_PAIRS, PATCHES, LANES), blocks)

    own = position.astype(jnp.int32).reshape(1)
    targets = patches.T

    half_penalty = 0.5 * penalty
    ends = jnp.cumsum(jnp.take(counts, group_order))
    entry = position * owned_entries + jnp.arange(owned_entries)
    holder = jnp.sum((entry[:, None] >= ends[None, :]).astype(jnp.int32), axis=1)
    thresh = jnp.take(half_penalty, jnp.take(group_order, holder), axis=0)
    thresh = jnp.repeat(thresh.reshape(owned_pairs, 2, PATCHES).transpose(0, 2, 1), BLOCK, axis=2)
    own_thresh = lax.dynamic_index_in_dim(half_penalty, group_order[position], 0, False)[None, :, None]

    def run(near, far, packed_in, packed_out):
        return gradient_call(
            group_order, counts, own, blocks, near, far, targets, packed_in, packed_out, devices
        )

    point = previous = None
    for turn in range(ITERS - 1):
        keep, send, extra = run(near, far, turn > 0, True)
        if turn == 0:
            point = previous = extra.astype(jnp.float32)
        current = shrink(point - 0.5 * reduce_shards(keep, send), thresh)
        point = current + momenta[turn] * (current - previous)
        previous = current
        near, far = gather_shards(point.astype(jnp.bfloat16))
    keep, send, sent = run(near, far, True, False)
    result = shrink(sent.astype(jnp.float32) - 0.5 * reduce_shards(keep, send), own_thresh)
    result = result.reshape(SLOT_PAIRS, PATCHES, 2, BLOCK).transpose(0, 2, 1, 3)
    return result.reshape(1, SLOTS, PATCHES * BLOCK)


def solution(mesh):
    in_specs = (
        P("rows", None),
        P("rows", "groups"),
        P(("groups", "rows"), None, None),
        P("groups", None),
        P("groups"),
        P("groups"),
        P("groups", None),
    )
    out_specs = P(("groups", "rows"), None, None)
    return jax.shard_map(local, mesh=mesh, in_specs=in_specs, out_specs=out_specs, check_vma=False)
```

```python
import functools

import jax
import jax.numpy as jnp
from jax import lax
from jax.experimental import pallas as pl
from jax.experimental.pallas import tpu as pltpu
from jax.sharding import PartitionSpec as P

BLOCK = 64
SLOTS = 16
PATCHES = 64
ITERS = 3
MEAN_LIVE = 10
LANES = 2 * BLOCK
SLOT_PAIRS = SLOTS // 2
VMEM_LIMIT = 60 * 1024 * 1024


def momentum_list():
    values = []
    tvalue = 1.0
    for turn in range(ITERS):
        tnext = (1.0 + (1.0 + 4.0 * tvalue * tvalue) ** 0.5) / 2.0
        values.append((tvalue - 1.0) / tnext)
        tvalue = tnext
    return values


def swap_halves(value):
    return jnp.concatenate([value[:, BLOCK:], value[:, :BLOCK]], axis=1)


def upper_half(shape):
    return lax.broadcasted_iota(jnp.int32, shape, 1) >= BLOCK


def support_kernel(begin, order, support, counts, dictionary, out, held, picks, ids, sems, out_sems):
    entries, rows, _ = held.shape
    pairs = entries // 2

    def fetch(entry, block):
        start = pl.multiple_of((block // 2) * LANES, LANES)
        return pltpu.make_async_copy(dictionary.at[:, pl.ds(start, LANES)], held.at[entry], sems.at[entry])

    def start_group(index, offset):
        group = order[index]
        live = counts[group]

        def start_slot(slot, carry):
            block = support[group, slot]
            ids[offset + slot] = block
            fetch(offset + slot, block).start()
            return carry

        lax.fori_loop(jnp.clip(-offset, 0, live), jnp.clip(entries - offset, 0, live), start_slot, 0)
        return offset + live

    lax.fori_loop(0, order.shape[0], start_group, jnp.int32(-begin))
    shape = (2 * LANES, LANES)
    source = lax.broadcasted_iota(jnp.int32, shape, 0)
    target = lax.broadcasted_iota(jnp.int32, shape, 1)
    for choice in range(4):
        wanted = jnp.where(target < BLOCK, (choice % 2) * BLOCK + target, LANES + (choice // 2) * BLOCK + target - BLOCK)
        picks[choice] = (source == wanted).astype(jnp.float32).astype(jnp.bfloat16)

    def store(pair):
        return pltpu.make_async_copy(held.at[2 * pair], out.at[pair], out_sems.at[pair])

    def pack(step, carry):
        for pair in (2 * step, 2 * step + 1):
            fetch(2 * pair, ids[2 * pair]).wait()
            fetch(2 * pair + 1, ids[2 * pair + 1]).wait()
        packed = []
        for pair in (2 * step, 2 * step + 1):
            choice = ids[2 * pair] % 2 + 2 * (ids[2 * pair + 1] % 2)
            both = jnp.concatenate([held[2 * pair], held[2 * pair + 1]], axis=1)
            packed.append(jnp.dot(both, picks[choice], preferred_element_type=jnp.float32).astype(jnp.bfloat16))
        for pair, value in zip((2 * step, 2 * step + 1), packed):
            held[2 * pair] = value
            store(pair).start()
        return carry

    lax.fori_loop(0, pairs // 2, pack, 0)

    def drain(pair, carry):
        store(pair).wait()
        return carry

    lax.fori_loop(0, pairs, drain, 0)


def collect_support(order, support, counts, dictionary, begin, entries):
    rows = dictionary.shape[0]
    pairs = entries // 2
    return pl.pallas_call(
        functools.partial(support_kernel, begin),
        grid_spec=pltpu.PrefetchScalarGridSpec(
            num_scalar_prefetch=3,
            grid=(),
            in_specs=[pl.BlockSpec(memory_space=pl.ANY)],
            out_specs=pl.BlockSpec(memory_space=pl.ANY),
            scratch_shapes=[
                pltpu.VMEM((entries, rows, LANES), dictionary.dtype),
                pltpu.VMEM((4, 2 * LANES, LANES), jnp.bfloat16),
                pltpu.SMEM((entries,), jnp.int32),
                pltpu.SemaphoreType.DMA((entries,)),
                pltpu.SemaphoreType.DMA((pairs,)),
            ],
        ),
        out_shape=jax.ShapeDtypeStruct((pairs, rows, LANES), dictionary.dtype),
        compiler_params=pltpu.CompilerParams(vmem_limit_bytes=VMEM_LIMIT),
        cost_estimate=pl.CostEstimate(
            flops=0, transcendentals=0, bytes_accessed=3 * pairs * rows * LANES * 2
        ),
        name="collect_support",
    )(order, support, counts, dictionary)


def relative_slot(index, me, devices):
    apart = index ^ me
    return (apart % 2) * (devices // 2) + ((apart // 2) % 2) * (devices // 4) + index // 4


def gradient_kernel(
    packed_in, packed_out, shards, order, counts, own, blocks, blocks_b, near, far, targets, keep, send, extra,
    held, codes, total, start_codes, offsets, sems, code_sems,
):
    groups = order.shape[0]
    me = own[0]
    pairs = 2 * blocks.shape[0]
    piece = pairs // shards
    half_in = near.shape[0]
    shard_in = 2 * half_in // shards
    half_out = keep.shape[0]
    shard_out = 2 * half_out // shards

    def load(index, source=blocks, begin=0):
        span = pl.ds(index * piece, piece)
        return pltpu.make_async_copy(source.at[pl.ds(begin, piece)], held.at[span], sems.at[index])

    code_loads = [
        pltpu.make_async_copy(near, codes.at[pl.ds(0, half_in)], code_sems.at[0]),
        pltpu.make_async_copy(far, codes.at[pl.ds(half_in, half_in)], code_sems.at[1]),
    ]
    for copy in code_loads:
        copy.start()
    for index in range(shards):
        source = (blocks, blocks_b)[2 * index // shards]
        load(index, source, (index % (shards // 2)) * piece).start()
    held[pairs:] = jnp.zeros((held.shape[0] - pairs,) + held.shape[1:], held.dtype)
    for copy in code_loads:
        copy.wait()

    upper = upper_half((PATCHES, LANES))
    side = upper.astype(jnp.int32)

    def place(pair, shard):
        holder = pair // shard
        return relative_slot(holder, me, shards) * shard + (pair - holder * shard)

    def spot_of(pair, shard):
        return jnp.where(pair < pairs, place(jnp.minimum(pair, pairs - 1), shard), pair)

    def shifted(parts, count, odd, ahead):
        turned = [swap_halves(part) for part in parts]
        last = len(parts) - 1
        moved = []
        for pair in range(count):
            low, high = (pair, pair + 1) if ahead else (pair - 1, pair)
            low, high = min(max(low, 0), last), min(max(high, 0), last)
            value = jnp.where(upper, turned[high], turned[low])
            moved.append(jnp.where(odd, value, parts[min(pair, last)]))
        return moved

    def read_codes(index, offset, live, count):
        first = offset // 2
        if packed_in:
            parts = [codes[place(jnp.minimum(first + pair, pairs - 1), shard_in)] for pair in range(count)]
        else:
            base = place(index * SLOT_PAIRS, shard_in)
            slots = min(count, SLOT_PAIRS)
            parts = shifted([codes[base + pair] for pair in range(slots)], count, offset % 2 == 1, False)
        masked = []
        for pair, part in enumerate(parts):
            entry = 2 * (first + pair) + side
            mine = (entry >= offset) & (entry < offset + live)
            masked.append(jnp.where(mine, part, jnp.zeros_like(part)))
        return masked

    def write_packed(ref, parts, offset, shard):
        first = offset // 2
        for pair, part in enumerate(parts):
            spot = spot_of(first + pair, shard)
            if pair == 0:
                part = jnp.where(upper | (offset % 2 == 0), part, ref[spot])
            ref[spot] = part

    def one_group(index, offset, live, count):
        first = offset // 2
        parts = read_codes(index, offset, live, count)
        if packed_out and not packed_in:
            first_pair = offset // 2
            for pair, part in enumerate(parts):
                if pair == 0:
                    part = jnp.where(upper | (offset % 2 == 0), part, start_codes[first_pair])
                start_codes[first_pair + pair] = part
        matrix = jnp.concatenate([held[first + pair] for pair in range(count)], axis=1)
        point = jnp.concatenate(parts, axis=1)
        residual = lax.dot_general(point, matrix, (((1,), (1,)), ((), ())), preferred_element_type=jnp.float32)
        column = pl.multiple_of(order[index] * PATCHES, PATCHES)
        target = targets[pl.ds(column, PATCHES), :].astype(jnp.float32)
        residual = (residual - target).astype(jnp.bfloat16)
        gradient = jnp.dot(residual, matrix, preferred_element_type=jnp.float32)
        grads = [gradient[:, pair * LANES : (pair + 1) * LANES] for pair in range(count)]
        if packed_out:
            write_packed(total, grads, offset, shard_out)
        else:
            base = place(index * SLOT_PAIRS, shard_out)
            moved = shifted(grads, min(count, SLOT_PAIRS), offset % 2 == 1, True)
            for pair in range(SLOT_PAIRS):
                if pair < len(moved):
                    value = jnp.where(2 * pair + side < live, moved[pair], 0.0)
                else:
                    value = jnp.zeros((PATCHES, LANES), jnp.float32)
                total[base + pair] = value

    def two_groups(step, carry):
        offset, waited = carry
        picks = []
        chunks = 1
        for index in (2 * step, 2 * step + 1):
            live = counts[order[index]]
            offsets[index] = offset
            picks.append((index, offset, live))
            chunks = jnp.maximum(chunks, (live + offset % 2 + 3) // 4)
            offset = offset + live
        reach = jnp.minimum(picks[1][1] // 2 + 2 * chunks - 1, pairs - 1)
        needed = reach // piece + 1

        def wait_piece(index, inner):
            load(index).wait()
            return inner

        lax.fori_loop(waited, needed, wait_piece, 0)
        for count in range(1, SLOTS // 4 + 2):

            @pl.when(chunks == count)
            def _(count=count):
                for pick in picks:
                    one_group(*pick, 2 * count)

        return offset, jnp.maximum(waited, needed)

    _, waited = lax.fori_loop(0, groups // 2, two_groups, (jnp.int32(0), jnp.int32(0)))

    def wait_rest(index, inner):
        load(index).wait()
        return inner

    lax.fori_loop(waited, shards, wait_rest, 0)
    keep[...] = total[:half_out]
    send[...] = total[half_out : 2 * half_out].astype(send.dtype)
    if packed_out and not packed_in:
        extra[...] = start_codes[pl.ds(me * shard_out, shard_out)]
    elif not packed_out:
        mine = offsets[me]
        parts = read_codes(me, mine, counts[order[me]], SLOT_PAIRS + 1)
        for pair, part in enumerate(shifted(parts, SLOT_PAIRS, mine % 2 == 1, True)):
            extra[pair] = part
    else:
        extra[...] = jnp.zeros(extra.shape, extra.dtype)


def gradient_call(order, counts, own, blocks, near, far, targets, packed_in, packed_out, shards):
    pairs, rows, _ = blocks[0].shape
    pairs = 2 * pairs
    groups = order.shape[0]
    half_in = near.shape[0]
    half_out = (pairs if packed_out else groups * SLOT_PAIRS) // 2
    extra = pairs // shards if packed_out else SLOT_PAIRS
    spare = SLOT_PAIRS + 2
    tile = (PATCHES, LANES)
    return pl.pallas_call(
        functools.partial(gradient_kernel, packed_in, packed_out, shards),
        grid_spec=pltpu.PrefetchScalarGridSpec(
            num_scalar_prefetch=3,
            grid=(),
            in_specs=[pl.BlockSpec(memory_space=pl.ANY)] * 4 + [pl.BlockSpec(memory_space=pltpu.VMEM)],
            out_specs=[pl.BlockSpec(memory_space=pltpu.VMEM)] * 3,
            scratch_shapes=[
                pltpu.VMEM((pairs + spare, rows, LANES), jnp.bfloat16),
                pltpu.VMEM((2 * half_in,) + tile, jnp.bfloat16),
                pltpu.VMEM((2 * half_out + spare,) + tile, jnp.float32),
                pltpu.VMEM((pairs + spare,) + tile, jnp.bfloat16),
                pltpu.SMEM((groups,), jnp.int32),
                pltpu.SemaphoreType.DMA((shards,)),
                pltpu.SemaphoreType.DMA((2,)),
            ],
        ),
        out_shape=[
            jax.ShapeDtypeStruct((half_out,) + tile, jnp.float32),
            jax.ShapeDtypeStruct((half_out,) + tile, jnp.bfloat16),
            jax.ShapeDtypeStruct((extra,) + tile, jnp.bfloat16),
        ],
        compiler_params=pltpu.CompilerParams(vmem_limit_bytes=VMEM_LIMIT),
        cost_estimate=pl.CostEstimate(
            flops=4 * pairs * rows * LANES * PATCHES, transcendentals=0, bytes_accessed=pairs * rows * LANES * 2
        ),
        name="gradient",
    )(order, counts, own, *blocks, near, far, targets)


def exchange(value, distance):
    devices = lax.axis_size("rows")
    return lax.ppermute(value, "rows", [(i, i ^ distance) for i in range(devices)])


def trade(value):
    columns = lax.axis_size("rows") // 4
    groups = [[4 * i + rest for i in range(columns)] for rest in range(4)]
    return lax.all_to_all(value, "rows", 0, 0, axis_index_groups=groups, tiled=True)


def gather_shards(own, beside=()):
    devices = lax.axis_size("rows")
    quarter = trade(jnp.concatenate([own] * (devices // 4), axis=0))
    if beside:
        quarter, first = lax.optimization_barrier((quarter, beside[0]))
    near = jnp.concatenate([quarter, exchange(quarter, 2)], axis=0)
    if beside:
        near, second = lax.optimization_barrier((near, beside[1]))
        return near, exchange(near, 1), (first, second)
    return near, exchange(near, 1)


def reduce_shards(keep, send):
    devices = lax.axis_size("rows")
    half = keep + exchange(send, 1).astype(jnp.float32)
    middle = half.shape[0] // 2
    quarter = half[:middle] + exchange(half[middle:].astype(jnp.bfloat16), 2).astype(jnp.float32)
    shares = trade(quarter.astype(jnp.bfloat16)).astype(jnp.float32)
    return jnp.sum(shares.reshape((devices // 4, -1) + shares.shape[1:]), axis=0)


def shrink(value, thresh):
    return value - jnp.clip(value, -thresh, thresh)


def local(dictionary, patches, initial_codes, support, counts, group_order, penalty):
    groups = group_order.shape[0]
    position = lax.axis_index("rows")
    devices = lax.axis_size("rows")
    momenta = momentum_list()
    owned_entries = MEAN_LIVE * groups // devices
    owned_pairs = owned_entries // 2
    pairs = owned_pairs * devices

    laid = initial_codes.reshape(SLOT_PAIRS, 2, PATCHES, BLOCK).transpose(0, 2, 1, 3)
    blocks = [collect_support(group_order, support, counts, dictionary, begin, pairs) for begin in (0, pairs)]
    near, far, blocks = gather_shards(laid.reshape(SLOT_PAIRS, PATCHES, LANES), blocks)

    own = position.astype(jnp.int32).reshape(1)
    targets = patches.T

    half_penalty = 0.5 * penalty
    ends = jnp.cumsum(jnp.take(counts, group_order))
    entry = position * owned_entries + jnp.arange(owned_entries)
    holder = jnp.sum((entry[:, None] >= ends[None, :]).astype(jnp.int32), axis=1)
    thresh = jnp.take(half_penalty, jnp.take(group_order, holder), axis=0)
    thresh = jnp.repeat(thresh.reshape(owned_pairs, 2, PATCHES).transpose(0, 2, 1), BLOCK, axis=2)
    own_thresh = lax.dynamic_index_in_dim(half_penalty, group_order[position], 0, False)[None, :, None]

    def run(near, far, packed_in, packed_out):
        return gradient_call(
            group_order, counts, own, blocks, near, far, targets, packed_in, packed_out, devices
        )

    point = previous = None
    for turn in range(ITERS - 1):
        keep, send, extra = run(near, far, turn > 0, True)
        if turn == 0:
            point = previous = extra.astype(jnp.float32)
        current = shrink(point - 0.5 * reduce_shards(keep, send), thresh)
        point = current + momenta[turn] * (current - previous)
        previous = current
        near, far = gather_shards(point.astype(jnp.bfloat16))
    keep, send, sent = run(near, far, True, False)
    result = shrink(sent.astype(jnp.float32) - 0.5 * reduce_shards(keep, send), own_thresh)
    result = result.reshape(SLOT_PAIRS, PATCHES, 2, BLOCK).transpose(0, 2, 1, 3)
    return result.reshape(1, SLOTS, PATCHES * BLOCK)


def solution(mesh):
    in_specs = (
        P("rows", None),
        P("rows", "groups"),
        P(("groups", "rows"), None, None),
        P("groups", None),
        P("groups"),
        P("groups"),
        P("groups", None),
    )
    out_specs = P(("groups", "rows"), None, None)
    return jax.shard_map(local, mesh=mesh, in_specs=in_specs, out_specs=out_specs, check_vma=False)
```

```python
import functools

import jax
import jax.numpy as jnp
from jax import lax
from jax.experimental import pallas as pl
from jax.experimental.pallas import tpu as pltpu
from jax.sharding import PartitionSpec as P

BLOCK = 64
SLOTS = 16
PATCHES = 64
ITERS = 3
MEAN_LIVE = 10
LANES = 2 * BLOCK
SLOT_PAIRS = SLOTS // 2
VMEM_LIMIT = 28 * 1024 * 1024
SUPPORT_VMEM = 34 * 1024 * 1024
SPARE = SLOT_PAIRS + 2


def momentum_list():
    values = []
    tvalue = 1.0
    for turn in range(ITERS):
        tnext = (1.0 + (1.0 + 4.0 * tvalue * tvalue) ** 0.5) / 2.0
        values.append((tvalue - 1.0) / tnext)
        tvalue = tnext
    return values


def swap_halves(value):
    return jnp.concatenate([value[:, BLOCK:], value[:, :BLOCK]], axis=1)


def upper_half(shape):
    return lax.broadcasted_iota(jnp.int32, shape, 1) >= BLOCK


def support_kernel(begin, order, support, counts, dictionary, *rest):
    *before, out, held, picks, ids, sems, early_sem = rest
    entries, rows, _ = held.shape
    pairs = entries // 2
    begin_pair = begin // 2

    def fetch(entry, block):
        start = pl.multiple_of((block // 2) * LANES, LANES)
        return pltpu.make_async_copy(dictionary.at[:, pl.ds(start, LANES)], held.at[entry], sems.at[entry])

    def start_group(index, offset):
        group = order[index]
        live = counts[group]

        def start_slot(slot, carry):
            block = support[group, slot]
            ids[offset + slot] = block
            fetch(offset + slot, block).start()
            return carry

        lax.fori_loop(jnp.clip(-offset, 0, live), jnp.clip(entries - offset, 0, live), start_slot, 0)
        return offset + live

    lax.fori_loop(0, order.shape[0], start_group, jnp.int32(-begin))
    early = [pltpu.make_async_copy(ref, out.at[pl.ds(0, begin_pair)], early_sem) for ref in before]
    for copy in early:
        copy.start()
    shape = (2 * LANES, LANES)
    source = lax.broadcasted_iota(jnp.int32, shape, 0)
    target = lax.broadcasted_iota(jnp.int32, shape, 1)
    for choice in range(4):
        wanted = jnp.where(target < BLOCK, (choice % 2) * BLOCK + target, LANES + (choice // 2) * BLOCK + target - BLOCK)
        picks[choice] = (source == wanted).astype(jnp.float32).astype(jnp.bfloat16)

    def pack(step, carry):
        for pair in (2 * step, 2 * step + 1):
            fetch(2 * pair, ids[2 * pair]).wait()
            fetch(2 * pair + 1, ids[2 * pair + 1]).wait()
        for pair in (2 * step, 2 * step + 1):
            choice = ids[2 * pair] % 2 + 2 * (ids[2 * pair + 1] % 2)
            both = jnp.concatenate([held[2 * pair], held[2 * pair + 1]], axis=1)
            value = jnp.dot(both, picks[choice], preferred_element_type=jnp.float32)
            out[begin_pair + pair] = value.astype(out.dtype)
        return carry

    lax.fori_loop(0, pairs // 2, pack, 0)
    rest_pairs = out.shape[0] - begin_pair - pairs
    if rest_pairs:
        out[begin_pair + pairs :] = jnp.zeros((rest_pairs,) + out.shape[1:], out.dtype)
    for copy in early:
        copy.wait()


def collect_support(order, support, counts, dictionary, begin, entries, before=()):
    rows = dictionary.shape[0]
    pairs = entries // 2
    places = begin // 2 + pairs + SPARE if before else pairs
    return pl.pallas_call(
        functools.partial(support_kernel, begin),
        grid_spec=pltpu.PrefetchScalarGridSpec(
            num_scalar_prefetch=3,
            grid=(),
            in_specs=[pl.BlockSpec(memory_space=pl.ANY)] + [pl.BlockSpec(memory_space=pltpu.VMEM)] * len(before),
            out_specs=pl.BlockSpec(memory_space=pltpu.VMEM),
            scratch_shapes=[
                pltpu.VMEM((entries, rows, LANES), dictionary.dtype),
                pltpu.VMEM((4, 2 * LANES, LANES), jnp.bfloat16),
                pltpu.SMEM((entries,), jnp.int32),
                pltpu.SemaphoreType.DMA((entries,)),
                pltpu.SemaphoreType.DMA,
            ],
        ),
        out_shape=jax.ShapeDtypeStruct((places, rows, LANES), dictionary.dtype),
        compiler_params=pltpu.CompilerParams(vmem_limit_bytes=SUPPORT_VMEM),
        cost_estimate=pl.CostEstimate(
            flops=0, transcendentals=0, bytes_accessed=3 * pairs * rows * LANES * 2
        ),
        name="collect_support",
    )(order, support, counts, dictionary, *before)


def relative_slot(index, me, devices):
    apart = index ^ me
    return (apart % 2) * (devices // 2) + ((apart // 2) % 2) * (devices // 4) + apart // 4


def gradient_kernel(
    packed_in, packed_out, shards, order, counts, own, held, near, far, targets, keep, send, extra,
    codes, total, start_codes, offsets,
):
    groups = order.shape[0]
    me = own[0]
    pairs = held.shape[0] - SPARE
    half_in = near.shape[0]
    shard_in = 2 * half_in // shards
    half_out = keep.shape[0]
    shard_out = 2 * half_out // shards
    codes[:half_in] = near[...]
    codes[half_in:] = far[...]

    upper = upper_half((PATCHES, LANES))
    side = upper.astype(jnp.int32)

    def place(pair, shard):
        holder = pair // shard
        return relative_slot(holder, me, shards) * shard + (pair - holder * shard)

    def spot_of(pair, shard):
        return jnp.where(pair < pairs, place(jnp.minimum(pair, pairs - 1), shard), pair)

    def shifted(parts, count, odd, ahead):
        turned = [swap_halves(part) for part in parts]
        last = len(parts) - 1
        moved = []
        for pair in range(count):
            low, high = (pair, pair + 1) if ahead else (pair - 1, pair)
            low, high = min(max(low, 0), last), min(max(high, 0), last)
            value = jnp.where(upper, turned[high], turned[low])
            moved.append(jnp.where(odd, value, parts[min(pair, last)]))
        return moved

    def read_codes(index, offset, live, count):
        first = offset // 2
        if packed_in:
            parts = [codes[place(jnp.minimum(first + pair, pairs - 1), shard_in)] for pair in range(count)]
        else:
            base = place(index * SLOT_PAIRS, shard_in)
            slots = min(count, SLOT_PAIRS)
            parts = shifted([codes[base + pair] for pair in range(slots)], count, offset % 2 == 1, False)
        masked = []
        for pair, part in enumerate(parts):
            entry = 2 * (first + pair) + side
            mine = (entry >= offset) & (entry < offset + live)
            masked.append(jnp.where(mine, part, jnp.zeros_like(part)))
        return masked

    def write_packed(ref, parts, offset, shard):
        first = offset // 2
        for pair, part in enumerate(parts):
            spot = spot_of(first + pair, shard)
            if pair == 0:
                part = jnp.where(upper | (offset % 2 == 0), part, ref[spot])
            ref[spot] = part

    def one_group(index, offset, live, count):
        first = offset // 2
        parts = read_codes(index, offset, live, count)
        if packed_out and not packed_in:
            first_pair = offset // 2
            for pair, part in enumerate(parts):
                if pair == 0:
                    part = jnp.where(upper | (offset % 2 == 0), part, start_codes[first_pair])
                start_codes[first_pair + pair] = part
        matrix = jnp.concatenate([held[first + pair] for pair in range(count)], axis=1)
        point = jnp.concatenate(parts, axis=1)
        residual = lax.dot_general(point, matrix, (((1,), (1,)), ((), ())), preferred_element_type=jnp.float32)
        column = pl.multiple_of(order[index] * PATCHES, PATCHES)
        target = targets[pl.ds(column, PATCHES), :].astype(jnp.float32)
        residual = (residual - target).astype(jnp.bfloat16)
        gradient = jnp.dot(residual, matrix, preferred_element_type=jnp.float32)
        grads = [gradient[:, pair * LANES : (pair + 1) * LANES] for pair in range(count)]
        if packed_out:
            write_packed(total, grads, offset, shard_out)
        else:
            base = place(index * SLOT_PAIRS, shard_out)
            moved = shifted(grads, min(count, SLOT_PAIRS), offset % 2 == 1, True)
            for pair in range(SLOT_PAIRS):
                if pair < len(moved):
                    value = jnp.where(2 * pair + side < live, moved[pair], 0.0)
                else:
                    value = jnp.zeros((PATCHES, LANES), jnp.float32)
                total[base + pair] = value

    def two_groups(step, offset):
        picks = []
        chunks = 1
        for index in (2 * step, 2 * step + 1):
            live = counts[order[index]]
            offsets[index] = offset
            picks.append((index, offset, live))
            chunks = jnp.maximum(chunks, (live + offset % 2 + 3) // 4)
            offset = offset + live
        for count in range(1, SLOTS // 4 + 2):

            @pl.when(chunks == count)
            def _(count=count):
                for pick in picks:
                    one_group(*pick, 2 * count)

        return offset

    lax.fori_loop(0, groups // 2, two_groups, jnp.int32(0))
    keep[...] = total[:half_out]
    send[...] = total[half_out : 2 * half_out].astype(send.dtype)
    if packed_out and not packed_in:
        extra[...] = start_codes[pl.ds(me * shard_out, shard_out)]
    elif not packed_out:
        mine = offsets[me]
        parts = read_codes(me, mine, counts[order[me]], SLOT_PAIRS + 1)
        for pair, part in enumerate(shifted(parts, SLOT_PAIRS, mine % 2 == 1, True)):
            extra[pair] = part
    else:
        extra[...] = jnp.zeros(extra.shape, extra.dtype)


def gradient_call(order, counts, own, blocks, near, far, targets, packed_in, packed_out, shards):
    places, rows, _ = blocks.shape
    pairs = places - SPARE
    groups = order.shape[0]
    half_in = near.shape[0]
    half_out = (pairs if packed_out else groups * SLOT_PAIRS) // 2
    extra = pairs // shards if packed_out else SLOT_PAIRS
    tile = (PATCHES, LANES)
    return pl.pallas_call(
        functools.partial(gradient_kernel, packed_in, packed_out, shards),
        grid_spec=pltpu.PrefetchScalarGridSpec(
            num_scalar_prefetch=3,
            grid=(),
            in_specs=[pl.BlockSpec(memory_space=pltpu.VMEM)] * 4,
            out_specs=[pl.BlockSpec(memory_space=pltpu.VMEM)] * 3,
            scratch_shapes=[
                pltpu.VMEM((2 * half_in,) + tile, jnp.bfloat16),
                pltpu.VMEM((2 * half_out + SPARE,) + tile, jnp.float32),
                pltpu.VMEM((pairs + SPARE,) + tile, jnp.bfloat16),
                pltpu.SMEM((groups,), jnp.int32),
            ],
        ),
        out_shape=[
            jax.ShapeDtypeStruct((half_out,) + tile, jnp.float32),
            jax.ShapeDtypeStruct((half_out,) + tile, jnp.bfloat16),
            jax.ShapeDtypeStruct((extra,) + tile, jnp.bfloat16),
        ],
        compiler_params=pltpu.CompilerParams(vmem_limit_bytes=VMEM_LIMIT),
        cost_estimate=pl.CostEstimate(
            flops=4 * pairs * rows * LANES * PATCHES, transcendentals=0, bytes_accessed=pairs * rows * LANES * 2
        ),
        name="gradient",
    )(order, counts, own, blocks, near, far, targets)


def exchange(value, distance):
    devices = lax.axis_size("rows")
    return lax.ppermute(value, "rows", [(i, i ^ distance) for i in range(devices)])


def gather_shards(own, beside=None, finish=None):
    devices = lax.axis_size("rows")
    parts = [own] + [exchange(own, 4 * k) for k in range(1, devices // 4)]
    quarter = jnp.concatenate(parts, axis=0)
    if finish is not None:
        quarter, beside = lax.optimization_barrier((quarter, beside))
    near = jnp.concatenate([quarter, exchange(quarter, 2)], axis=0)
    if finish is not None:
        near, beside = lax.optimization_barrier((near, finish(beside)))
        return near, exchange(near, 1), beside
    return near, exchange(near, 1)


def reduce_shards(keep, send):
    devices = lax.axis_size("rows")
    half = keep + exchange(send, 1).astype(jnp.float32)
    middle = half.shape[0] // 2
    quarter = half[:middle] + exchange(half[middle:].astype(jnp.bfloat16), 2).astype(jnp.float32)
    size = quarter.shape[0] // (devices // 4)
    sent = quarter.astype(jnp.bfloat16)
    total = quarter[:size]
    for k in range(1, devices // 4):
        total = total + exchange(sent[k * size : (k + 1) * size], 4 * k).astype(jnp.float32)
    return total


def shrink(value, thresh):
    return value - jnp.clip(value, -thresh, thresh)


def local(dictionary, patches, initial_codes, support, counts, group_order, penalty):
    groups = group_order.shape[0]
    position = lax.axis_index("rows")
    devices = lax.axis_size("rows")
    momenta = momentum_list()
    owned_entries = MEAN_LIVE * groups // devices
    owned_pairs = owned_entries // 2
    pairs = owned_pairs * devices

    laid = initial_codes.reshape(SLOT_PAIRS, 2, PATCHES, BLOCK).transpose(0, 2, 1, 3)
    collect = functools.partial(collect_support, group_order, support, counts, dictionary)
    near, far, blocks = gather_shards(
        laid.reshape(SLOT_PAIRS, PATCHES, LANES), collect(0, pairs), lambda first: collect(pairs, pairs, (first,))
    )

    own = position.astype(jnp.int32).reshape(1)
    targets = patches.T

    half_penalty = 0.5 * penalty
    ends = jnp.cumsum(jnp.take(counts, group_order))
    entry = position * owned_entries + jnp.arange(owned_entries)
    holder = jnp.sum((entry[:, None] >= ends[None, :]).astype(jnp.int32), axis=1)
    thresh = jnp.take(half_penalty, jnp.take(group_order, holder), axis=0)
    thresh = jnp.repeat(thresh.reshape(owned_pairs, 2, PATCHES).transpose(0, 2, 1), BLOCK, axis=2)
    own_thresh = lax.dynamic_index_in_dim(half_penalty, group_order[position], 0, False)[None, :, None]

    def run(near, far, packed_in, packed_out):
        return gradient_call(
            group_order, counts, own, blocks, near, far, targets, packed_in, packed_out, devices
        )

    point = previous = None
    for turn in range(ITERS - 1):
        keep, send, extra = run(near, far, turn > 0, True)
        if turn == 0:
            point = previous = extra.astype(jnp.float32)
        current = shrink(point - 0.5 * reduce_shards(keep, send), thresh)
        point = current + momenta[turn] * (current - previous)
        previous = current
        near, far = gather_shards(point.astype(jnp.bfloat16))
    keep, send, sent = run(near, far, True, False)
    result = shrink(sent.astype(jnp.float32) - 0.5 * reduce_shards(keep, send), own_thresh)
    result = result.reshape(SLOT_PAIRS, PATCHES, 2, BLOCK).transpose(0, 2, 1, 3)
    return result.reshape(1, SLOTS, PATCHES * BLOCK)


def solution(mesh):
    in_specs = (
        P("rows", None),
        P("rows", "groups"),
        P(("groups", "rows"), None, None),
        P("groups", None),
        P("groups"),
        P("groups"),
        P("groups", None),
    )
    out_specs = P(("groups", "rows"), None, None)
    return jax.shard_map(local, mesh=mesh, in_specs=in_specs, out_specs=out_specs, check_vma=False)
```

```python
import functools

import jax
import jax.numpy as jnp
from jax import lax
from jax.experimental import pallas as pl
from jax.experimental.pallas import tpu as pltpu
from jax.sharding import PartitionSpec as P

BLOCK = 64
SLOTS = 16
PATCHES = 64
ITERS = 3
MEAN_LIVE = 10
LANES = 2 * BLOCK
SLOT_PAIRS = SLOTS // 2
VMEM_MARGIN = 3 * 1024 * 1024
SPARE = SLOT_PAIRS + 2


def momentum_list():
    values = []
    tvalue = 1.0
    for turn in range(ITERS):
        tnext = (1.0 + (1.0 + 4.0 * tvalue * tvalue) ** 0.5) / 2.0
        values.append((tvalue - 1.0) / tnext)
        tvalue = tnext
    return values


def swap_halves(value):
    return jnp.concatenate([value[:, BLOCK:], value[:, :BLOCK]], axis=1)


def upper_half(shape):
    return lax.broadcasted_iota(jnp.int32, shape, 1) >= BLOCK


def support_kernel(begin, order, support, counts, dictionary, *rest):
    *before, out, held, picks, ids, sems, early_sem = rest
    entries, rows, _ = held.shape
    pairs = entries // 2
    begin_pair = begin // 2

    def fetch(entry, block):
        start = pl.multiple_of((block // 2) * LANES, LANES)
        return pltpu.make_async_copy(dictionary.at[:, pl.ds(start, LANES)], held.at[entry], sems.at[entry])

    def start_group(index, offset):
        group = order[index]
        live = counts[group]

        def start_slot(slot, carry):
            block = support[group, slot]
            ids[offset + slot] = block
            fetch(offset + slot, block).start()
            return carry

        lax.fori_loop(jnp.clip(-offset, 0, live), jnp.clip(entries - offset, 0, live), start_slot, 0)
        return offset + live

    lax.fori_loop(0, order.shape[0], start_group, jnp.int32(-begin))
    early = [pltpu.make_async_copy(ref, out.at[pl.ds(0, begin_pair)], early_sem) for ref in before]
    for copy in early:
        copy.start()
    shape = (2 * LANES, LANES)
    source = lax.broadcasted_iota(jnp.int32, shape, 0)
    target = lax.broadcasted_iota(jnp.int32, shape, 1)
    for choice in range(4):
        wanted = jnp.where(target < BLOCK, (choice % 2) * BLOCK + target, LANES + (choice // 2) * BLOCK + target - BLOCK)
        picks[choice] = (source == wanted).astype(jnp.float32).astype(jnp.bfloat16)

    def pack(step, carry):
        for pair in (2 * step, 2 * step + 1):
            fetch(2 * pair, ids[2 * pair]).wait()
            fetch(2 * pair + 1, ids[2 * pair + 1]).wait()
        for pair in (2 * step, 2 * step + 1):
            choice = ids[2 * pair] % 2 + 2 * (ids[2 * pair + 1] % 2)
            both = jnp.concatenate([held[2 * pair], held[2 * pair + 1]], axis=1)
            value = jnp.dot(both, picks[choice], preferred_element_type=jnp.float32)
            out[begin_pair + pair] = value.astype(out.dtype)
        return carry

    lax.fori_loop(0, pairs // 2, pack, 0)
    rest_pairs = out.shape[0] - begin_pair - pairs
    if rest_pairs:
        out[begin_pair + pairs :] = jnp.zeros((rest_pairs,) + out.shape[1:], out.dtype)
    for copy in early:
        copy.wait()


def collect_support(order, support, counts, dictionary, begin, entries, before=()):
    rows = dictionary.shape[0]
    pairs = entries // 2
    places = begin // 2 + pairs + SPARE if before else pairs
    return pl.pallas_call(
        functools.partial(support_kernel, begin),
        grid_spec=pltpu.PrefetchScalarGridSpec(
            num_scalar_prefetch=3,
            grid=(),
            in_specs=[pl.BlockSpec(memory_space=pl.ANY)] + [pl.BlockSpec(memory_space=pltpu.VMEM)] * len(before),
            out_specs=pl.BlockSpec(memory_space=pltpu.VMEM),
            scratch_shapes=[
                pltpu.VMEM((entries, rows, LANES), dictionary.dtype),
                pltpu.VMEM((4, 2 * LANES, LANES), jnp.bfloat16),
                pltpu.SMEM((entries,), jnp.int32),
                pltpu.SemaphoreType.DMA((entries,)),
                pltpu.SemaphoreType.DMA,
            ],
        ),
        out_shape=jax.ShapeDtypeStruct((places, rows, LANES), dictionary.dtype),
        compiler_params=pltpu.CompilerParams(vmem_limit_bytes=entries * rows * LANES * 2 + VMEM_MARGIN),
        cost_estimate=pl.CostEstimate(
            flops=0, transcendentals=0, bytes_accessed=3 * pairs * rows * LANES * 2
        ),
        name="collect_support",
    )(order, support, counts, dictionary, *before)


def relative_slot(index, me, devices):
    apart = index ^ me
    return (apart % 2) * (devices // 2) + ((apart // 2) % 2) * (devices // 4) + apart // 4


def gradient_kernel(
    packed_in, packed_out, shards, order, counts, own, held, near, far, targets, keep, send, extra,
    codes, total, start_codes, offsets,
):
    groups = order.shape[0]
    me = own[0]
    pairs = held.shape[0] - SPARE
    half_in = near.shape[0]
    shard_in = 2 * half_in // shards
    half_out = keep.shape[0]
    shard_out = 2 * half_out // shards
    codes[:half_in] = near[...]
    codes[half_in:] = far[...]

    upper = upper_half((PATCHES, LANES))
    side = upper.astype(jnp.int32)

    def place(pair, shard):
        holder = pair // shard
        return relative_slot(holder, me, shards) * shard + (pair - holder * shard)

    def spot_of(pair, shard):
        return jnp.where(pair < pairs, place(jnp.minimum(pair, pairs - 1), shard), pair)

    def shifted(parts, count, odd, ahead):
        turned = [swap_halves(part) for part in parts]
        last = len(parts) - 1
        moved = []
        for pair in range(count):
            low, high = (pair, pair + 1) if ahead else (pair - 1, pair)
            low, high = min(max(low, 0), last), min(max(high, 0), last)
            value = jnp.where(upper, turned[high], turned[low])
            moved.append(jnp.where(odd, value, parts[min(pair, last)]))
        return moved

    def read_codes(index, offset, live, count):
        first = offset // 2
        if packed_in:
            parts = [codes[place(jnp.minimum(first + pair, pairs - 1), shard_in)] for pair in range(count)]
        else:
            base = place(index * SLOT_PAIRS, shard_in)
            slots = min(count, SLOT_PAIRS)
            parts = shifted([codes[base + pair] for pair in range(slots)], count, offset % 2 == 1, False)
        masked = []
        for pair, part in enumerate(parts):
            entry = 2 * (first + pair) + side
            mine = (entry >= offset) & (entry < offset + live)
            masked.append(jnp.where(mine, part, jnp.zeros_like(part)))
        return masked

    def write_packed(ref, parts, offset, shard):
        first = offset // 2
        for pair, part in enumerate(parts):
            spot = spot_of(first + pair, shard)
            if pair == 0:
                part = jnp.where(upper | (offset % 2 == 0), part, ref[spot])
            ref[spot] = part

    def one_group(index, offset, live, count):
        first = offset // 2
        parts = read_codes(index, offset, live, count)
        if packed_out and not packed_in:
            first_pair = offset // 2
            for pair, part in enumerate(parts):
                if pair == 0:
                    part = jnp.where(upper | (offset % 2 == 0), part, start_codes[first_pair])
                start_codes[first_pair + pair] = part
        matrix = jnp.concatenate([held[first + pair] for pair in range(count)], axis=1)
        point = jnp.concatenate(parts, axis=1)
        residual = lax.dot_general(point, matrix, (((1,), (1,)), ((), ())), preferred_element_type=jnp.float32)
        column = pl.multiple_of(order[index] * PATCHES, PATCHES)
        target = targets[pl.ds(column, PATCHES), :].astype(jnp.float32)
        residual = (residual - target).astype(jnp.bfloat16)
        gradient = jnp.dot(residual, matrix, preferred_element_type=jnp.float32)
        grads = [gradient[:, pair * LANES : (pair + 1) * LANES] for pair in range(count)]
        if packed_out:
            write_packed(total, grads, offset, shard_out)
        else:
            base = place(index * SLOT_PAIRS, shard_out)
            moved = shifted(grads, min(count, SLOT_PAIRS), offset % 2 == 1, True)
            for pair in range(SLOT_PAIRS):
                if pair < len(moved):
                    value = jnp.where(2 * pair + side < live, moved[pair], 0.0)
                else:
                    value = jnp.zeros((PATCHES, LANES), jnp.float32)
                total[base + pair] = value

    def two_groups(step, offset):
        picks = []
        chunks = 1
        for index in (2 * step, 2 * step + 1):
            live = counts[order[index]]
            offsets[index] = offset
            picks.append((index, offset, live))
            chunks = jnp.maximum(chunks, (live + offset % 2 + 3) // 4)
            offset = offset + live
        for count in range(1, SLOTS // 4 + 2):

            @pl.when(chunks == count)
            def _(count=count):
                for pick in picks:
                    one_group(*pick, 2 * count)

        return offset

    lax.fori_loop(0, groups // 2, two_groups, jnp.int32(0))
    keep[...] = total[:half_out]
    send[...] = total[half_out : 2 * half_out].astype(send.dtype)
    if packed_out and not packed_in:
        extra[...] = start_codes[pl.ds(me * shard_out, shard_out)]
    elif not packed_out:
        mine = offsets[me]
        parts = read_codes(me, mine, counts[order[me]], SLOT_PAIRS + 1)
        for pair, part in enumerate(shifted(parts, SLOT_PAIRS, mine % 2 == 1, True)):
            extra[pair] = part
    else:
        extra[...] = jnp.zeros(extra.shape, extra.dtype)


def gradient_call(order, counts, own, blocks, near, far, targets, packed_in, packed_out, shards):
    places, rows, _ = blocks.shape
    pairs = places - SPARE
    groups = order.shape[0]
    half_in = near.shape[0]
    half_out = (pairs if packed_out else groups * SLOT_PAIRS) // 2
    extra = pairs // shards if packed_out else SLOT_PAIRS
    tile = (PATCHES, LANES)
    scratch = (2 * half_in * 2 + (2 * half_out + SPARE) * 4 + places * 2) * PATCHES * LANES
    return pl.pallas_call(
        functools.partial(gradient_kernel, packed_in, packed_out, shards),
        grid_spec=pltpu.PrefetchScalarGridSpec(
            num_scalar_prefetch=3,
            grid=(),
            in_specs=[pl.BlockSpec(memory_space=pltpu.VMEM)] * 4,
            out_specs=[pl.BlockSpec(memory_space=pltpu.VMEM)] * 3,
            scratch_shapes=[
                pltpu.VMEM((2 * half_in,) + tile, jnp.bfloat16),
                pltpu.VMEM((2 * half_out + SPARE,) + tile, jnp.float32),
                pltpu.VMEM((places,) + tile, jnp.bfloat16),
                pltpu.SMEM((groups,), jnp.int32),
            ],
        ),
        out_shape=[
            jax.ShapeDtypeStruct((half_out,) + tile, jnp.float32),
            jax.ShapeDtypeStruct((half_out,) + tile, jnp.bfloat16),
            jax.ShapeDtypeStruct((extra,) + tile, jnp.bfloat16),
        ],
        compiler_params=pltpu.CompilerParams(vmem_limit_bytes=scratch + VMEM_MARGIN),
        cost_estimate=pl.CostEstimate(
            flops=4 * pairs * rows * LANES * PATCHES, transcendentals=0, bytes_accessed=pairs * rows * LANES * 2
        ),
        name="gradient",
    )(order, counts, own, blocks, near, far, targets)


def exchange(value, distance):
    devices = lax.axis_size("rows")
    return lax.ppermute(value, "rows", [(i, i ^ distance) for i in range(devices)])


def distances():
    columns = lax.axis_size("rows") // 4
    return [4 * column + 2 * row for row in range(2) for column in range(columns)]


def gather_staged(own, beside, finish):
    columns = lax.axis_size("rows") // 4
    quarter = jnp.concatenate([own] + [exchange(own, 4 * k) for k in range(1, columns)], axis=0)
    quarter, beside = lax.optimization_barrier((quarter, beside))
    near = jnp.concatenate([quarter, exchange(quarter, 2)], axis=0)
    near, beside = lax.optimization_barrier((near, finish(beside)))
    return near, exchange(near, 1), beside


def gather_shards(own):
    near = jnp.concatenate([own] + [exchange(own, distance) for distance in distances()[1:]], axis=0)
    return near, exchange(near, 1)


def reduce_shards(keep, send):
    half = keep + exchange(send, 1).astype(jnp.float32)
    apart = distances()
    size = half.shape[0] // len(apart)
    sent = half.astype(jnp.bfloat16)
    total = half[:size]
    for place in range(1, len(apart)):
        share = exchange(sent[place * size : (place + 1) * size], apart[place])
        total = total + share.astype(jnp.float32)
    return total


def shrink(value, thresh):
    return value - jnp.clip(value, -thresh, thresh)


def local(dictionary, patches, initial_codes, support, counts, group_order, penalty):
    groups = group_order.shape[0]
    position = lax.axis_index("rows")
    devices = lax.axis_size("rows")
    momenta = momentum_list()
    owned_entries = MEAN_LIVE * groups // devices
    owned_pairs = owned_entries // 2
    pairs = owned_pairs * devices

    laid = initial_codes.reshape(SLOT_PAIRS, 2, PATCHES, BLOCK).transpose(0, 2, 1, 3)
    collect = functools.partial(collect_support, group_order, support, counts, dictionary)
    near, far, blocks = gather_staged(
        laid.reshape(SLOT_PAIRS, PATCHES, LANES), collect(0, pairs), lambda first: collect(pairs, pairs, (first,))
    )

    own = position.astype(jnp.int32).reshape(1)
    targets = patches.T

    half_penalty = 0.5 * penalty
    ends = jnp.cumsum(jnp.take(counts, group_order))
    entry = position * owned_entries + jnp.arange(owned_entries)
    holder = jnp.sum((entry[:, None] >= ends[None, :]).astype(jnp.int32), axis=1)
    thresh = jnp.take(half_penalty, jnp.take(group_order, holder), axis=0)
    thresh = jnp.repeat(thresh.reshape(owned_pairs, 2, PATCHES).transpose(0, 2, 1), BLOCK, axis=2)
    own_thresh = lax.dynamic_index_in_dim(half_penalty, group_order[position], 0, False)[None, :, None]

    def run(near, far, packed_in, packed_out):
        return gradient_call(
            group_order, counts, own, blocks, near, far, targets, packed_in, packed_out, devices
        )

    point = previous = None
    for turn in range(ITERS - 1):
        keep, send, extra = run(near, far, turn > 0, True)
        if turn == 0:
            point = previous = extra.astype(jnp.float32)
        current = shrink(point - 0.5 * reduce_shards(keep, send), thresh)
        point = current + momenta[turn] * (current - previous)
        previous = current
        near, far = gather_shards(point.astype(jnp.bfloat16))
    keep, send, sent = run(near, far, True, False)
    result = shrink(sent.astype(jnp.float32) - 0.5 * reduce_shards(keep, send), own_thresh)
    result = result.reshape(SLOT_PAIRS, PATCHES, 2, BLOCK).transpose(0, 2, 1, 3)
    return result.reshape(1, SLOTS, PATCHES * BLOCK)


def solution(mesh):
    in_specs = (
        P("rows", None),
        P("rows", "groups"),
        P(("groups", "rows"), None, None),
        P("groups", None),
        P("groups"),
        P("groups"),
        P("groups", None),
    )
    out_specs = P(("groups", "rows"), None, None)
    return jax.shard_map(local, mesh=mesh, in_specs=in_specs, out_specs=out_specs, check_vma=False)
```

```python
import functools
import math

import jax
import jax.numpy as jnp
from jax import lax
from jax.experimental import pallas as pl
from jax.experimental.pallas import tpu as pltpu
from jax.sharding import PartitionSpec as P

BLOCK = 64
SLOTS = 16
PATCHES = 64
ITERS = 3
MEAN_LIVE = 10
LEAST_LIVE = 4
LANES = 2 * BLOCK
SLOT_PAIRS = SLOTS // 2
SPARE = SLOT_PAIRS + 2
ROW_TILE = 16
PIECE = 4
MATRIX_UNIT = 256
VMEM_MARGIN = 3 * 1024 * 1024


def momentum_list():
    values = []
    tvalue = 1.0
    for turn in range(ITERS):
        tnext = (1.0 + (1.0 + 4.0 * tvalue * tvalue) ** 0.5) / 2.0
        values.append((tvalue - 1.0) / tnext)
        tvalue = tnext
    return values


def swap_halves(value):
    return jnp.concatenate([value[:, BLOCK:], value[:, :BLOCK]], axis=1)


def upper_half(shape):
    return lax.broadcasted_iota(jnp.int32, shape, 1) >= BLOCK


def group_at(index, seq, order, counts):
    position = seq[index]
    group = order[position]
    return position, group, counts[group]


def support_kernel(chain, seq, order, support, counts, dictionary, out, held, picks, ids, sems, out_sems):
    entries, rows, _ = held.shape
    pairs = entries // 2
    seats = order.shape[0] // 2

    def fetch(entry, block):
        start = pl.multiple_of((block // 2) * LANES, LANES)
        return pltpu.make_async_copy(dictionary.at[:, pl.ds(start, LANES)], held.at[entry], sems.at[entry])

    def start_group(index, offset):
        _, group, live = group_at(index, seq, order, counts)

        def start_slot(slot, carry):
            block = support[group, slot]
            ids[offset + slot] = block
            fetch(offset + slot, block).start()
            return carry

        lax.fori_loop(0, live, start_slot, 0)
        return offset + live

    used = lax.fori_loop(chain * seats, (chain + 1) * seats, start_group, jnp.int32(0))

    def clear(entry, carry):
        ids[entry] = 0
        held[entry] = jnp.zeros((rows, LANES), held.dtype)
        return carry

    lax.fori_loop(used, entries, clear, 0)
    shape = (2 * LANES, LANES)
    source = lax.broadcasted_iota(jnp.int32, shape, 0)
    target = lax.broadcasted_iota(jnp.int32, shape, 1)
    for choice in range(4):
        wanted = jnp.where(target < BLOCK, (choice % 2) * BLOCK + target, LANES + (choice // 2) * BLOCK + target - BLOCK)
        picks[choice] = (source == wanted).astype(jnp.float32).astype(jnp.bfloat16)

    def store(pair):
        return pltpu.make_async_copy(held.at[2 * pair], out.at[pair], out_sems.at[pair])

    def pack(step, carry):
        for entry in range(4):
            index = 4 * step + entry

            @pl.when(index < used)
            def _(index=index):
                fetch(index, ids[index]).wait()

        packed = []
        for pair in (2 * step, 2 * step + 1):
            choice = ids[2 * pair] % 2 + 2 * (ids[2 * pair + 1] % 2)
            both = jnp.concatenate([held[2 * pair], held[2 * pair + 1]], axis=1)
            packed.append(jnp.dot(both, picks[choice], preferred_element_type=jnp.float32).astype(jnp.bfloat16))
        for pair, value in zip((2 * step, 2 * step + 1), packed):
            held[2 * pair] = value
            store(pair).start()
        return carry

    lax.fori_loop(0, pairs // 2, pack, 0)

    def drain(pair, carry):
        store(pair).wait()
        return carry

    lax.fori_loop(0, pairs, drain, 0)


def collect_support(chain, seq, order, support, counts, dictionary, pairs):
    rows = dictionary.shape[0]
    entries = 2 * pairs
    return pl.pallas_call(
        functools.partial(support_kernel, chain),
        grid_spec=pltpu.PrefetchScalarGridSpec(
            num_scalar_prefetch=4,
            grid=(),
            in_specs=[pl.BlockSpec(memory_space=pltpu.HBM)],
            out_specs=pl.BlockSpec(memory_space=pltpu.HBM),
            scratch_shapes=[
                pltpu.VMEM((entries, rows, LANES), dictionary.dtype),
                pltpu.VMEM((4, 2 * LANES, LANES), jnp.bfloat16),
                pltpu.SMEM((entries,), jnp.int32),
                pltpu.SemaphoreType.DMA((entries,)),
                pltpu.SemaphoreType.DMA((pairs,)),
            ],
        ),
        out_shape=jax.ShapeDtypeStruct((pairs, rows, LANES), dictionary.dtype),
        compiler_params=pltpu.CompilerParams(vmem_limit_bytes=entries * rows * LANES * 2 + VMEM_MARGIN),
        cost_estimate=pl.CostEstimate(flops=0, transcendentals=0, bytes_accessed=6 * pairs * rows * LANES * 2),
        name="collect_support",
    )(seq, order, support, counts, dictionary)


def reversed_bits(index, size):
    result = 0
    while size > 1:
        result = 2 * result + index % 2
        index //= 2
        size //= 2
    return result


def gradient_kernel(chain, mode, shards, seq, order, counts, own, blocks, near, far, targets, *refs):
    refs = list(refs)
    take = lambda: refs.pop(0)
    if mode == "first":
        thresh = take()
    if mode == "final":
        other = take()
    if mode == "raw":
        total, sent = take(), take()
    else:
        keep, send = take(), take()
        if mode == "first":
            start_out, thresh_out = take(), take()
        if mode == "final":
            sent = take()
    held, codes = take(), take()
    if mode != "raw":
        total = take()
    if mode == "first":
        starts, limits = take(), take()
    offsets, sems = refs

    seats = order.shape[0] // 2
    pairs = blocks.shape[0]
    places = pairs + SPARE
    pieces = pairs // PIECE
    base = places if mode == "final" else 0
    me = own[0]

    def load(index):
        span = pl.ds(index * PIECE, PIECE)
        return pltpu.make_async_copy(blocks.at[span], held.at[span], sems.at[index])

    for index in range(pieces):
        load(index).start()
    held[pairs:] = jnp.zeros((SPARE,) + held.shape[1:], held.dtype)

    def shard_span(slot, size):
        return pl.ds(pl.multiple_of((reversed_bits(slot, shards) ^ me) * size, ROW_TILE), size)

    size_in = 2 * near.shape[0] // shards
    for slot in range(shards):
        source = near if slot < shards // 2 else far
        begin = slot % (shards // 2) * size_in
        codes[shard_span(slot, size_in), :] = source[begin : begin + size_in, :]

    for which in range(2):

        def seat(index, offset):
            position, _, live = group_at(index, seq, order, counts)
            offsets[position] = offset
            return offset + live

        lax.fori_loop(which * seats, (which + 1) * seats, seat, jnp.int32(which * 2 * places))

    upper = upper_half((PATCHES, LANES))
    side = upper.astype(jnp.int32)

    def tile(pair):
        return pl.ds(pl.multiple_of(pair * PATCHES, PATCHES), PATCHES)

    def shifted(parts, count, odd, ahead):
        turned = [swap_halves(part) for part in parts]
        last = len(parts) - 1
        moved = []
        for pair in range(count):
            low, high = (pair, pair + 1) if ahead else (pair - 1, pair)
            low, high = min(max(low, 0), last), min(max(high, 0), last)
            value = jnp.where(upper, turned[high], turned[low])
            moved.append(jnp.where(odd, value, parts[min(pair, last)]))
        return moved

    def read_codes(position, offset, live, count):
        first = offset // 2
        if mode == "first":
            parts = [codes[tile(position * SLOT_PAIRS + pair), :] for pair in range(min(count, SLOT_PAIRS))]
            parts = shifted(parts, count, offset % 2 == 1, False)
        else:
            parts = [codes[tile(first + pair), :] for pair in range(count)]
        masked = []
        for pair, part in enumerate(parts):
            entry = 2 * (first + pair) + side
            mine = (entry >= offset) & (entry < offset + live)
            masked.append(jnp.where(mine, part, jnp.zeros_like(part)))
        return masked

    def write_packed(ref, parts, offset, begin=0):
        first = offset // 2
        for pair, part in enumerate(parts):
            if pair == 0:
                part = jnp.where(upper | (offset % 2 == 0), part, ref[tile(begin + first), :])
            ref[tile(begin + first + pair), :] = part

    def one_group(position, group, offset, live, count):
        first = offset // 2
        parts = read_codes(position, offset, live, count)
        if mode == "first":
            write_packed(starts, parts, offset)
            write_packed(limits, [thresh[group]] * count, offset)
        matrix = jnp.concatenate([held[first + pair] for pair in range(count)], axis=1)
        point = jnp.concatenate(parts, axis=1)
        residual = lax.dot_general(point, matrix, (((1,), (1,)), ((), ())), preferred_element_type=jnp.float32)
        target = targets[tile(group), :].astype(jnp.float32)
        residual = (residual - target).astype(jnp.bfloat16)
        gradient = jnp.dot(residual, matrix, preferred_element_type=jnp.float32)
        write_packed(total, [gradient[:, pair * LANES : (pair + 1) * LANES] for pair in range(count)], offset, base)

    def wait_piece(index, carry):
        load(index).wait()
        return carry

    def two_groups(step, waited):
        picks = []
        chunks = 1
        for index in (2 * step, 2 * step + 1):
            position, group, live = group_at(chain * seats + index, seq, order, counts)
            offset = offsets[position] - chain * 2 * places
            picks.append((position, group, offset, live))
            chunks = jnp.maximum(chunks, (live + offset % 2 + 3) // 4)
        reach = jnp.minimum(picks[1][2] // 2 + 2 * chunks - 1, pairs - 1)
        needed = jnp.maximum(reach // PIECE + 1, waited)
        lax.fori_loop(waited, needed, wait_piece, 0)
        for count in range(1, SLOTS // 4 + 2):

            @pl.when(chunks == count)
            def _(count=count):
                for pick in picks:
                    one_group(*pick, 2 * count)

        return needed

    waited = lax.fori_loop(0, seats // 2, two_groups, jnp.int32(0))
    lax.fori_loop(waited, pieces, wait_piece, 0)

    if mode in ("first", "shards"):
        size = 2 * keep.shape[0] // shards
        for slot in range(shards):
            begin = slot % (shards // 2) * size
            value = total[shard_span(slot, size), :]
            if slot < shards // 2:
                keep[begin : begin + size, :] = value
            else:
                send[begin : begin + size, :] = value.astype(send.dtype)
    if mode == "first":
        size = start_out.shape[0]
        span = pl.ds(pl.multiple_of(me * size, ROW_TILE), size)
        start_out[...] = starts[span, :]
        thresh_out[...] = limits[span, :]
    if mode in ("raw", "final"):
        offset = offsets[me] - chain * 2 * places
        mine = (offset >= 0) & (offset < 2 * places)

        @pl.when(mine)
        def _():
            parts = read_codes(me, offset, counts[order[me]], SLOT_PAIRS + 1)
            for pair, part in enumerate(shifted(parts, SLOT_PAIRS, offset % 2 == 1, True)):
                sent[pair] = part

        @pl.when(jnp.logical_not(mine))
        def _():
            sent[...] = jnp.zeros(sent.shape, sent.dtype)

    if mode == "final":
        total[: places * PATCHES, :] = other[...]
        for slot in range(shards):
            position = reversed_bits(slot, shards) ^ me
            offset = offsets[position]
            live = counts[order[position]]
            parts = [total[tile(offset // 2 + pair), :] for pair in range(SLOT_PAIRS + 1)]
            begin = slot % (shards // 2) * SLOT_PAIRS * PATCHES
            for pair, part in enumerate(shifted(parts, SLOT_PAIRS, offset % 2 == 1, True)):
                value = jnp.where(2 * pair + side < live, part, 0.0)
                rows = slice(begin + pair * PATCHES, begin + (pair + 1) * PATCHES)
                if slot < shards // 2:
                    keep[rows, :] = value
                else:
                    send[rows, :] = value.astype(send.dtype)


def gradient_call(chain, mode, shards, scalars, blocks, near, far, targets, extra=()):
    pairs, rows, _ = blocks.shape
    places = pairs + SPARE
    groups = scalars[1].shape[0]
    half_in = near.shape[0]
    single, double = jnp.bfloat16, jnp.float32
    packed = (places * PATCHES, LANES)
    half_out = (groups * SLOT_PAIRS if mode == "final" else pairs) * PATCHES // 2
    shard = (2 * half_out // shards, LANES)
    slots = (SLOT_PAIRS, PATCHES, LANES)
    if mode == "raw":
        outs = [(packed, double), (slots, single)]
    else:
        outs = [((half_out, LANES), double), ((half_out, LANES), single)]
        if mode == "first":
            outs += [(shard, single), (shard, double)]
        if mode == "final":
            outs += [(slots, single)]
    codes = groups * SLOT_PAIRS * PATCHES if mode == "first" else packed[0]
    scratch = [((places, rows, LANES), single), ((codes, LANES), single)]
    if mode == "final":
        scratch += [((2 * packed[0], LANES), double)]
    elif mode != "raw":
        scratch += [(packed, double)]
    if mode == "first":
        scratch += [(packed, single), (packed, double)]
    room = sum(math.prod(shape) * jnp.dtype(kind).itemsize for shape, kind in scratch)
    return pl.pallas_call(
        functools.partial(gradient_kernel, chain, mode, shards),
        grid_spec=pltpu.PrefetchScalarGridSpec(
            num_scalar_prefetch=4,
            grid=(),
            in_specs=[pl.BlockSpec(memory_space=pltpu.HBM)]
            + [pl.BlockSpec(memory_space=pltpu.VMEM)] * (3 + len(extra)),
            out_specs=[pl.BlockSpec(memory_space=pltpu.VMEM)] * len(outs),
            scratch_shapes=[pltpu.VMEM(shape, kind) for shape, kind in scratch]
            + [pltpu.SMEM((groups,), jnp.int32), pltpu.SemaphoreType.DMA((pairs // PIECE,))],
        ),
        out_shape=[jax.ShapeDtypeStruct(shape, kind) for shape, kind in outs],
        compiler_params=pltpu.CompilerParams(vmem_limit_bytes=room + VMEM_MARGIN),
        cost_estimate=pl.CostEstimate(
            flops=4 * pairs * rows * LANES * MATRIX_UNIT, transcendentals=0, bytes_accessed=pairs * rows * LANES * 2
        ),
        name="gradient",
    )(*scalars, blocks, near, far, targets, *extra)


def exchange(value, distance):
    devices = lax.axis_size("rows")
    return lax.ppermute(value, "rows", [(i, i ^ distance) for i in range(devices)])


def double_up(value, distance):
    return jnp.concatenate([value, exchange(value, distance)], axis=0)


def gather_shards(own, beside=()):
    made = []
    value = own
    distance = lax.axis_size("rows") // 2
    while distance > 1:
        if beside and distance == 2:
            value, array = lax.optimization_barrier((value, beside[0]))
            made.append(array)
        value = double_up(value, distance)
        distance //= 2
    if beside:
        value, array = lax.optimization_barrier((value, beside[1]))
        made.append(array)
    return value, exchange(value, 1), made


def reduce_shards(keep, send):
    devices = lax.axis_size("rows")
    total = keep + exchange(send, 1).astype(jnp.float32)
    distance = 2
    while distance < devices:
        middle = total.shape[0] // 2
        total = total[:middle] + exchange(total[middle:].astype(jnp.bfloat16), distance).astype(jnp.float32)
        distance *= 2
    return total


def chain_seats(live):
    groups = live.shape[0]
    index = jnp.arange(groups)
    ahead = (live[None, :] > live[:, None]) | ((live[None, :] == live[:, None]) & (index[None, :] < index[:, None]))
    rank = jnp.sum(ahead.astype(jnp.int32), axis=1)
    spot = ((rank + 1) // 2 % 2) * (groups // 2) + rank // 2
    return jnp.sum(jnp.where(spot[:, None] == index[None, :], index[:, None], 0), axis=0).astype(jnp.int32)


def shrink(value, thresh):
    return value - jnp.clip(value, -thresh, thresh)


def local(dictionary, patches, initial_codes, support, counts, group_order, penalty):
    groups = group_order.shape[0]
    position = lax.axis_index("rows")
    devices = lax.axis_size("rows")
    momenta = momentum_list()
    most_entries = MEAN_LIVE * groups // 2 + (SLOTS - LEAST_LIVE) // 2
    shard_rows = -(-most_entries * PATCHES // (2 * devices * ROW_TILE)) * ROW_TILE
    pairs = shard_rows * devices // PATCHES

    laid = initial_codes.reshape(SLOT_PAIRS, 2, PATCHES, BLOCK).transpose(0, 2, 1, 3)
    laid = laid.reshape(SLOT_PAIRS * PATCHES, LANES)
    seq = chain_seats(jnp.take(counts, group_order))
    blocks = [collect_support(chain, seq, group_order, support, counts, dictionary, pairs) for chain in range(2)]
    near, far, blocks = gather_shards(laid, blocks)

    scalars = (seq, group_order, counts, position.astype(jnp.int32).reshape(1))
    targets = patches.T
    half_penalty = 0.5 * penalty
    thresh_tiles = jnp.broadcast_to(half_penalty[:, :, None], (groups, PATCHES, LANES))
    own_thresh = lax.dynamic_index_in_dim(half_penalty, group_order[position], 0, False)[None, :, None]

    chains = [dict(near=near, far=far) for _ in range(2)]
    for turn in range(ITERS - 1):
        for chain, state in enumerate(chains):
            mode, extra = ("first", (thresh_tiles,)) if turn == 0 else ("shards", ())
            keep, send, *more = gradient_call(
                chain, mode, devices, scalars, blocks[chain], state["near"], state["far"], targets, extra
            )
            if turn == 0:
                state["point"] = state["previous"] = more[0].astype(jnp.float32)
                state["thresh"] = more[1]
            current = shrink(state["point"] - 0.5 * reduce_shards(keep, send), state["thresh"])
            state["point"] = current + momenta[turn] * (current - state["previous"])
            state["previous"] = current
            state["near"], state["far"], _ = gather_shards(state["point"].astype(jnp.bfloat16))
    raw, sent = gradient_call(
        0, "raw", devices, scalars, blocks[0], chains[0]["near"], chains[0]["far"], targets
    )
    keep, send, more = gradient_call(
        1, "final", devices, scalars, blocks[1], chains[1]["near"], chains[1]["far"], targets, (raw,)
    )
    gradient = reduce_shards(keep, send).reshape(SLOT_PAIRS, PATCHES, LANES)
    sent = sent.astype(jnp.float32) + more.astype(jnp.float32)
    result = shrink(sent - 0.5 * gradient, own_thresh)
    result = result.reshape(SLOT_PAIRS, PATCHES, 2, BLOCK).transpose(0, 2, 1, 3)
    return result.reshape(1, SLOTS, PATCHES * BLOCK)


def solution(mesh):
    in_specs = (
        P("rows", None),
        P("rows", "groups"),
        P(("groups", "rows"), None, None),
        P("groups", None),
        P("groups"),
        P("groups"),
        P("groups", None),
    )
    out_specs = P(("groups", "rows"), None, None)
    return jax.shard_map(local, mesh=mesh, in_specs=in_specs, out_specs=out_specs, check_vma=False)
```

```python
import functools
import math

import jax
import jax.numpy as jnp
from jax import lax
from jax.experimental import pallas as pl
from jax.experimental.pallas import tpu as pltpu
from jax.sharding import PartitionSpec as P

BLOCK = 64
SLOTS = 16
PATCHES = 64
ITERS = 3
MEAN_LIVE = 10
LEAST_LIVE = 4
LANES = 2 * BLOCK
SLOT_PAIRS = SLOTS // 2
SPARE = SLOT_PAIRS + 2
ROW_TILE = 16
PIECE = 4
MATRIX_UNIT = 256
VMEM_MARGIN = 3 * 1024 * 1024
SUPPORT_VMEM = 40 * 1024 * 1024
HELD_BYTES = 65 * 1024 * 1024


def momentum_list():
    values = []
    tvalue = 1.0
    for turn in range(ITERS):
        tnext = (1.0 + (1.0 + 4.0 * tvalue * tvalue) ** 0.5) / 2.0
        values.append((tvalue - 1.0) / tnext)
        tvalue = tnext
    return values


def swap_halves(value):
    return jnp.concatenate([value[:, BLOCK:], value[:, :BLOCK]], axis=1)


def upper_half(shape):
    return lax.broadcasted_iota(jnp.int32, shape, 1) >= BLOCK


def group_at(index, seq, order, counts):
    position = seq[index]
    group = order[position]
    return position, group, counts[group]


def support_kernel(chain, seq, order, support, counts, dictionary, out, held, picks, ids, sems, out_sems):
    entries, rows, _ = held.shape
    pairs = entries // 2
    seats = order.shape[0] // 2

    def fetch(entry, block):
        start = pl.multiple_of((block // 2) * LANES, LANES)
        return pltpu.make_async_copy(dictionary.at[:, pl.ds(start, LANES)], held.at[entry], sems.at[entry])

    def start_group(index, offset):
        _, group, live = group_at(index, seq, order, counts)

        def start_slot(slot, carry):
            block = support[group, slot]
            ids[offset + slot] = block
            fetch(offset + slot, block).start()
            return carry

        lax.fori_loop(0, live, start_slot, 0)
        return offset + live

    used = lax.fori_loop(chain * seats, (chain + 1) * seats, start_group, jnp.int32(0))

    def clear(entry, carry):
        ids[entry] = 0
        held[entry] = jnp.zeros((rows, LANES), held.dtype)
        return carry

    lax.fori_loop(used, entries, clear, 0)
    shape = (2 * LANES, LANES)
    source = lax.broadcasted_iota(jnp.int32, shape, 0)
    target = lax.broadcasted_iota(jnp.int32, shape, 1)
    for choice in range(4):
        wanted = jnp.where(target < BLOCK, (choice % 2) * BLOCK + target, LANES + (choice // 2) * BLOCK + target - BLOCK)
        picks[choice] = (source == wanted).astype(jnp.float32).astype(jnp.bfloat16)

    def store(pair):
        return pltpu.make_async_copy(held.at[2 * pair], out.at[pair], out_sems.at[pair])

    def pack(step, carry):
        for entry in range(4):
            index = 4 * step + entry

            @pl.when(index < used)
            def _(index=index):
                fetch(index, ids[index]).wait()

        packed = []
        for pair in (2 * step, 2 * step + 1):
            choice = ids[2 * pair] % 2 + 2 * (ids[2 * pair + 1] % 2)
            both = jnp.concatenate([held[2 * pair], held[2 * pair + 1]], axis=1)
            packed.append(jnp.dot(both, picks[choice], preferred_element_type=jnp.float32).astype(jnp.bfloat16))
        for pair, value in zip((2 * step, 2 * step + 1), packed):
            held[2 * pair] = value
            store(pair).start()
        return carry

    lax.fori_loop(0, pairs // 2, pack, 0)

    def drain(pair, carry):
        store(pair).wait()
        return carry

    lax.fori_loop(0, pairs, drain, 0)


def collect_support(chain, seq, order, support, counts, dictionary, pairs):
    rows = dictionary.shape[0]
    entries = 2 * pairs
    return pl.pallas_call(
        functools.partial(support_kernel, chain),
        grid_spec=pltpu.PrefetchScalarGridSpec(
            num_scalar_prefetch=4,
            grid=(),
            in_specs=[pl.BlockSpec(memory_space=pltpu.HBM)],
            out_specs=pl.BlockSpec(memory_space=pltpu.HBM),
            scratch_shapes=[
                pltpu.VMEM((entries, rows, LANES), dictionary.dtype),
                pltpu.VMEM((4, 2 * LANES, LANES), jnp.bfloat16),
                pltpu.SMEM((entries,), jnp.int32),
                pltpu.SemaphoreType.DMA((entries,)),
                pltpu.SemaphoreType.DMA((pairs,)),
            ],
        ),
        out_shape=jax.ShapeDtypeStruct((HELD_BYTES // (rows * LANES * 2), rows, LANES), dictionary.dtype),
        compiler_params=pltpu.CompilerParams(vmem_limit_bytes=SUPPORT_VMEM),
        cost_estimate=pl.CostEstimate(flops=0, transcendentals=0, bytes_accessed=6 * pairs * rows * LANES * 2),
        name="collect_support",
    )(seq, order, support, counts, dictionary)


def reversed_bits(index, size):
    result = 0
    while size > 1:
        result = 2 * result + index % 2
        index //= 2
        size //= 2
    return result


def gradient_kernel(chain, mode, shards, pairs, seq, order, counts, own, blocks, near, far, targets, *refs):
    refs = list(refs)
    take = lambda: refs.pop(0)
    take()
    if mode == "first":
        thresh = take()
    if mode == "final":
        other = take()
    if mode == "raw":
        total, sent = take(), take()
    else:
        keep, send = take(), take()
        if mode == "first":
            start_out, thresh_out = take(), take()
        if mode == "final":
            sent = take()
    held, codes = take(), take()
    if mode != "raw":
        total = take()
    if mode == "first":
        starts, limits = take(), take()
    offsets, sems = refs

    seats = order.shape[0] // 2
    places = pairs + SPARE
    pieces = pairs // PIECE
    base = places if mode == "final" else 0
    me = own[0]

    def load(index):
        span = pl.ds(index * PIECE, PIECE)
        return pltpu.make_async_copy(blocks.at[span], held.at[span], sems.at[index])

    for index in range(pieces):
        load(index).start()
    held[pairs:] = jnp.zeros((SPARE,) + held.shape[1:], held.dtype)

    def shard_span(slot, size):
        return pl.ds(pl.multiple_of((reversed_bits(slot, shards) ^ me) * size, ROW_TILE), size)

    size_in = 2 * near.shape[0] // shards
    for slot in range(shards):
        source = near if slot < shards // 2 else far
        begin = slot % (shards // 2) * size_in
        codes[shard_span(slot, size_in), :] = source[begin : begin + size_in, :]

    for which in range(2):

        def seat(index, offset):
            position, _, live = group_at(index, seq, order, counts)
            offsets[position] = offset
            return offset + live

        lax.fori_loop(which * seats, (which + 1) * seats, seat, jnp.int32(which * 2 * places))

    upper = upper_half((PATCHES, LANES))
    side = upper.astype(jnp.int32)

    def tile(pair):
        return pl.ds(pl.multiple_of(pair * PATCHES, PATCHES), PATCHES)

    def shifted(parts, count, odd, ahead):
        turned = [swap_halves(part) for part in parts]
        last = len(parts) - 1
        moved = []
        for pair in range(count):
            low, high = (pair, pair + 1) if ahead else (pair - 1, pair)
            low, high = min(max(low, 0), last), min(max(high, 0), last)
            value = jnp.where(upper, turned[high], turned[low])
            moved.append(jnp.where(odd, value, parts[min(pair, last)]))
        return moved

    def read_codes(position, offset, live, count):
        first = offset // 2
        if mode == "first":
            parts = [codes[tile(position * SLOT_PAIRS + pair), :] for pair in range(min(count, SLOT_PAIRS))]
            parts = shifted(parts, count, offset % 2 == 1, False)
        else:
            parts = [codes[tile(first + pair), :] for pair in range(count)]
        masked = []
        for pair, part in enumerate(parts):
            entry = 2 * (first + pair) + side
            mine = (entry >= offset) & (entry < offset + live)
            masked.append(jnp.where(mine, part, jnp.zeros_like(part)))
        return masked

    def write_packed(ref, parts, offset, begin=0):
        first = offset // 2
        for pair, part in enumerate(parts):
            if pair == 0:
                part = jnp.where(upper | (offset % 2 == 0), part, ref[tile(begin + first), :])
            ref[tile(begin + first + pair), :] = part

    def one_group(position, group, offset, live, count):
        first = offset // 2
        parts = read_codes(position, offset, live, count)
        if mode == "first":
            write_packed(starts, parts, offset)
            write_packed(limits, [thresh[group]] * count, offset)
        matrix = jnp.concatenate([held[first + pair] for pair in range(count)], axis=1)
        point = jnp.concatenate(parts, axis=1)
        residual = lax.dot_general(point, matrix, (((1,), (1,)), ((), ())), preferred_element_type=jnp.float32)
        target = targets[tile(group), :].astype(jnp.float32)
        residual = (residual - target).astype(jnp.bfloat16)
        gradient = jnp.dot(residual, matrix, preferred_element_type=jnp.float32)
        write_packed(total, [gradient[:, pair * LANES : (pair + 1) * LANES] for pair in range(count)], offset, base)

    def wait_piece(index, carry):
        load(index).wait()
        return carry

    def two_groups(step, waited):
        picks = []
        chunks = 1
        for index in (2 * step, 2 * step + 1):
            position, group, live = group_at(chain * seats + index, seq, order, counts)
            offset = offsets[position] - chain * 2 * places
            picks.append((position, group, offset, live))
            chunks = jnp.maximum(chunks, (live + offset % 2 + 3) // 4)
        reach = jnp.minimum(picks[1][2] // 2 + 2 * chunks - 1, pairs - 1)
        needed = jnp.maximum(reach // PIECE + 1, waited)
        lax.fori_loop(waited, needed, wait_piece, 0)
        for count in range(1, SLOTS // 4 + 2):

            @pl.when(chunks == count)
            def _(count=count):
                for pick in picks:
                    one_group(*pick, 2 * count)

        return needed

    waited = lax.fori_loop(0, seats // 2, two_groups, jnp.int32(0))
    lax.fori_loop(waited, pieces, wait_piece, 0)

    if mode in ("first", "shards"):
        size = 2 * keep.shape[0] // shards
        for slot in range(shards):
            begin = slot % (shards // 2) * size
            value = total[shard_span(slot, size), :]
            if slot < shards // 2:
                keep[begin : begin + size, :] = value
            else:
                send[begin : begin + size, :] = value.astype(send.dtype)
    if mode == "first":
        size = start_out.shape[0]
        span = pl.ds(pl.multiple_of(me * size, ROW_TILE), size)
        start_out[...] = starts[span, :]
        thresh_out[...] = limits[span, :]
    if mode in ("raw", "final"):
        offset = offsets[me] - chain * 2 * places
        mine = (offset >= 0) & (offset < 2 * places)

        @pl.when(mine)
        def _():
            parts = read_codes(me, offset, counts[order[me]], SLOT_PAIRS + 1)
            for pair, part in enumerate(shifted(parts, SLOT_PAIRS, offset % 2 == 1, True)):
                sent[pair] = part

        @pl.when(jnp.logical_not(mine))
        def _():
            sent[...] = jnp.zeros(sent.shape, sent.dtype)

    if mode == "final":
        total[: places * PATCHES, :] = other[...]
        for slot in range(shards):
            position = reversed_bits(slot, shards) ^ me
            offset = offsets[position]
            live = counts[order[position]]
            parts = [total[tile(offset // 2 + pair), :] for pair in range(SLOT_PAIRS + 1)]
            begin = slot % (shards // 2) * SLOT_PAIRS * PATCHES
            for pair, part in enumerate(shifted(parts, SLOT_PAIRS, offset % 2 == 1, True)):
                value = jnp.where(2 * pair + side < live, part, 0.0)
                rows = slice(begin + pair * PATCHES, begin + (pair + 1) * PATCHES)
                if slot < shards // 2:
                    keep[rows, :] = value
                else:
                    send[rows, :] = value.astype(send.dtype)


def gradient_call(chain, mode, shards, pairs, scalars, blocks, near, far, targets, after, extra=()):
    rows = blocks.shape[1]
    places = pairs + SPARE
    groups = scalars[1].shape[0]
    half_in = near.shape[0]
    single, double = jnp.bfloat16, jnp.float32
    packed = (places * PATCHES, LANES)
    half_out = (groups * SLOT_PAIRS if mode == "final" else pairs) * PATCHES // 2
    shard = (2 * half_out // shards, LANES)
    slots = (SLOT_PAIRS, PATCHES, LANES)
    if mode == "raw":
        outs = [(packed, double), (slots, single)]
    else:
        outs = [((half_out, LANES), double), ((half_out, LANES), single)]
        if mode == "first":
            outs += [(shard, single), (shard, double)]
        if mode == "final":
            outs += [(slots, single)]
    codes = groups * SLOT_PAIRS * PATCHES if mode == "first" else packed[0]
    scratch = [((places, rows, LANES), single), ((codes, LANES), single)]
    if mode == "final":
        scratch += [((2 * packed[0], LANES), double)]
    elif mode != "raw":
        scratch += [(packed, double)]
    if mode == "first":
        scratch += [(packed, single), (packed, double)]
    room = sum(math.prod(shape) * jnp.dtype(kind).itemsize for shape, kind in scratch)
    return pl.pallas_call(
        functools.partial(gradient_kernel, chain, mode, shards, pairs),
        grid_spec=pltpu.PrefetchScalarGridSpec(
            num_scalar_prefetch=4,
            grid=(),
            in_specs=[pl.BlockSpec(memory_space=pltpu.HBM)]
            + [pl.BlockSpec(memory_space=pltpu.VMEM)] * 3
            + [pl.BlockSpec(memory_space=pl.ANY)]
            + [pl.BlockSpec(memory_space=pltpu.VMEM)] * len(extra),
            out_specs=[pl.BlockSpec(memory_space=pltpu.VMEM)] * len(outs),
            scratch_shapes=[pltpu.VMEM(shape, kind) for shape, kind in scratch]
            + [pltpu.SMEM((groups,), jnp.int32), pltpu.SemaphoreType.DMA((pairs // PIECE,))],
        ),
        out_shape=[jax.ShapeDtypeStruct(shape, kind) for shape, kind in outs],
        compiler_params=pltpu.CompilerParams(vmem_limit_bytes=room + VMEM_MARGIN),
        cost_estimate=pl.CostEstimate(
            flops=4 * pairs * rows * LANES * MATRIX_UNIT, transcendentals=0, bytes_accessed=pairs * rows * LANES * 2
        ),
        name="gradient",
    )(*scalars, blocks, near, far, targets, after, *extra)


def exchange(value, distance):
    devices = lax.axis_size("rows")
    return lax.ppermute(value, "rows", [(i, i ^ distance) for i in range(devices)])


def double_up(value, distance):
    return jnp.concatenate([value, exchange(value, distance)], axis=0)


def gather_shards(own, beside=()):
    made = []
    early = own
    value = own
    distance = lax.axis_size("rows") // 2
    while distance > 1:
        if beside and distance == 2:
            value, array = lax.optimization_barrier((value, beside[0]))
            made.append(array)
        early = value
        value = double_up(value, distance)
        distance //= 2
    if beside:
        value, array = lax.optimization_barrier((value, beside[1]))
        made.append(array)
    return value, exchange(value, 1), made or early[:ROW_TILE]


def reduce_shards(keep, send):
    devices = lax.axis_size("rows")
    total = keep + exchange(send, 1).astype(jnp.float32)
    early = total[:ROW_TILE]
    distance = 2
    while distance < devices:
        middle = total.shape[0] // 2
        total = total[:middle] + exchange(total[middle:].astype(jnp.bfloat16), distance).astype(jnp.float32)
        distance *= 2
    return total, early


def chain_seats(live):
    groups = live.shape[0]
    index = jnp.arange(groups)
    ahead = (live[None, :] > live[:, None]) | ((live[None, :] == live[:, None]) & (index[None, :] < index[:, None]))
    rank = jnp.sum(ahead.astype(jnp.int32), axis=1)
    spot = ((rank + 1) // 2 % 2) * (groups // 2) + rank // 2
    return jnp.sum(jnp.where(spot[:, None] == index[None, :], index[:, None], 0), axis=0).astype(jnp.int32)


def shrink(value, thresh):
    return value - jnp.clip(value, -thresh, thresh)


def local(dictionary, patches, initial_codes, support, counts, group_order, penalty):
    groups = group_order.shape[0]
    position = lax.axis_index("rows")
    devices = lax.axis_size("rows")
    momenta = momentum_list()
    most_entries = MEAN_LIVE * groups // 2 + (SLOTS - LEAST_LIVE) // 2
    shard_rows = -(-most_entries * PATCHES // (2 * devices * ROW_TILE)) * ROW_TILE
    pairs = shard_rows * devices // PATCHES

    laid = initial_codes.reshape(SLOT_PAIRS, 2, PATCHES, BLOCK).transpose(0, 2, 1, 3)
    laid = laid.reshape(SLOT_PAIRS * PATCHES, LANES)
    seq = chain_seats(jnp.take(counts, group_order))
    blocks = [collect_support(chain, seq, group_order, support, counts, dictionary, pairs) for chain in range(2)]
    near, far, blocks = gather_shards(laid, blocks)

    scalars = (seq, group_order, counts, position.astype(jnp.int32).reshape(1))
    targets = patches.T
    half_penalty = 0.5 * penalty
    thresh_tiles = jnp.broadcast_to(half_penalty[:, :, None], (groups, PATCHES, LANES))
    own_thresh = lax.dynamic_index_in_dim(half_penalty, group_order[position], 0, False)[None, :, None]

    chains = [dict(near=near, far=far) for _ in range(2)]
    after = targets[:ROW_TILE]
    run = functools.partial(gradient_call, shards=devices, pairs=pairs, scalars=scalars, targets=targets)
    for turn in range(ITERS - 1):
        for chain, state in enumerate(chains):
            mode, extra = ("first", (thresh_tiles,)) if turn == 0 else ("shards", ())
            keep, send, *more = run(
                chain, mode, blocks=blocks[chain], near=state["near"], far=state["far"], after=after, extra=extra
            )
            if turn == 0:
                state["point"] = state["previous"] = more[0].astype(jnp.float32)
                state["thresh"] = more[1]
            gradient, after = reduce_shards(keep, send)
            current = shrink(state["point"] - 0.5 * gradient, state["thresh"])
            state["point"] = current + momenta[turn] * (current - state["previous"])
            state["previous"] = current
            state["near"], state["far"], early = gather_shards(state["point"].astype(jnp.bfloat16))
        after = early
    raw, sent = run(0, "raw", blocks=blocks[0], near=chains[0]["near"], far=chains[0]["far"], after=after)
    keep, send, more = run(
        1, "final", blocks=blocks[1], near=chains[1]["near"], far=chains[1]["far"], after=after, extra=(raw,)
    )
    gradient = reduce_shards(keep, send)[0].reshape(SLOT_PAIRS, PATCHES, LANES)
    sent = sent.astype(jnp.float32) + more.astype(jnp.float32)
    result = shrink(sent - 0.5 * gradient, own_thresh)
    result = result.reshape(SLOT_PAIRS, PATCHES, 2, BLOCK).transpose(0, 2, 1, 3)
    return result.reshape(1, SLOTS, PATCHES * BLOCK)


def solution(mesh):
    in_specs = (
        P("rows", None),
        P("rows", "groups"),
        P(("groups", "rows"), None, None),
        P("groups", None),
        P("groups"),
        P("groups"),
        P("groups", None),
    )
    out_specs = P(("groups", "rows"), None, None)
    return jax.shard_map(local, mesh=mesh, in_specs=in_specs, out_specs=out_specs, check_vma=False)
```

```python
import functools
import math

import jax
import jax.numpy as jnp
from jax import lax
from jax.experimental import pallas as pl
from jax.experimental.pallas import tpu as pltpu
from jax.sharding import PartitionSpec as P

BLOCK = 64
SLOTS = 16
PATCHES = 64
ITERS = 3
MEAN_LIVE = 10
LANES = 2 * BLOCK
SLOT_PAIRS = SLOTS // 2
SPARE = SLOT_PAIRS + 2
ROW_TILE = 16
SUPPORT_PARTS = 4
PIECE = 5
MATRIX_UNIT = 256
VMEM_MARGIN = 3 * 1024 * 1024
SUPPORT_VMEM = 40 * 1024 * 1024
HELD_BYTES = 65 * 1024 * 1024


def momentum_list():
    values = []
    tvalue = 1.0
    for turn in range(ITERS):
        tnext = (1.0 + (1.0 + 4.0 * tvalue * tvalue) ** 0.5) / 2.0
        values.append((tvalue - 1.0) / tnext)
        tvalue = tnext
    return values


def swap_halves(value):
    return jnp.concatenate([value[:, BLOCK:], value[:, :BLOCK]], axis=1)


def upper_half(shape):
    return lax.broadcasted_iota(jnp.int32, shape, 1) >= BLOCK


def group_at(index, seq, order, counts):
    position = seq[index]
    group = order[position]
    return position, group, counts[group]


def support_kernel(begin, seq, order, support, counts, dictionary, *refs):
    out, held, picks, ids, sems, out_sems = refs[-6:]
    entries, rows, _ = held.shape
    pairs = entries // 2

    def fetch(entry, block):
        start = pl.multiple_of((block // 2) * LANES, LANES)
        return pltpu.make_async_copy(dictionary.at[:, pl.ds(start, LANES)], held.at[entry], sems.at[entry])

    def start_group(index, offset):
        _, group, live = group_at(index, seq, order, counts)

        def start_slot(slot, carry):
            block = support[group, slot]
            ids[offset + slot] = block
            fetch(offset + slot, block).start()
            return carry

        lax.fori_loop(jnp.clip(-offset, 0, live), jnp.clip(entries - offset, 0, live), start_slot, 0)
        return offset + live

    lax.fori_loop(0, order.shape[0], start_group, jnp.int32(-begin))
    shape = (2 * LANES, LANES)
    source = lax.broadcasted_iota(jnp.int32, shape, 0)
    target = lax.broadcasted_iota(jnp.int32, shape, 1)
    for choice in range(4):
        wanted = jnp.where(target < BLOCK, (choice % 2) * BLOCK + target, LANES + (choice // 2) * BLOCK + target - BLOCK)
        picks[choice] = (source == wanted).astype(jnp.float32).astype(jnp.bfloat16)

    def store(pair):
        return pltpu.make_async_copy(held.at[2 * pair], out.at[begin // 2 + pair], out_sems.at[pair])

    def pack(step, carry):
        for entry in range(4):
            index = 4 * step + entry
            fetch(index, ids[index]).wait()
        packed = []
        for pair in (2 * step, 2 * step + 1):
            choice = ids[2 * pair] % 2 + 2 * (ids[2 * pair + 1] % 2)
            both = jnp.concatenate([held[2 * pair], held[2 * pair + 1]], axis=1)
            packed.append(jnp.dot(both, picks[choice], preferred_element_type=jnp.float32).astype(jnp.bfloat16))
        for pair, value in zip((2 * step, 2 * step + 1), packed):
            held[2 * pair] = value
            store(pair).start()
        return carry

    lax.fori_loop(0, pairs // 2, pack, 0)

    def drain(pair, carry):
        store(pair).wait()
        return carry

    lax.fori_loop(0, pairs, drain, 0)


def collect_support(seq, order, support, counts, dictionary, pairs, part, *before):
    rows = dictionary.shape[0]
    pairs = pairs // SUPPORT_PARTS
    entries = 2 * pairs
    return pl.pallas_call(
        functools.partial(support_kernel, part * entries),
        grid_spec=pltpu.PrefetchScalarGridSpec(
            num_scalar_prefetch=4,
            grid=(),
            in_specs=[pl.BlockSpec(memory_space=pltpu.HBM)] * (1 + len(before)),
            out_specs=pl.BlockSpec(memory_space=pltpu.HBM),
            scratch_shapes=[
                pltpu.VMEM((entries, rows, LANES), dictionary.dtype),
                pltpu.VMEM((4, 2 * LANES, LANES), jnp.bfloat16),
                pltpu.SMEM((entries,), jnp.int32),
                pltpu.SemaphoreType.DMA((entries,)),
                pltpu.SemaphoreType.DMA((pairs,)),
            ],
        ),
        out_shape=jax.ShapeDtypeStruct((HELD_BYTES // (rows * LANES * 2), rows, LANES), dictionary.dtype),
        compiler_params=pltpu.CompilerParams(vmem_limit_bytes=SUPPORT_VMEM),
        cost_estimate=pl.CostEstimate(flops=0, transcendentals=0, bytes_accessed=6 * pairs * rows * LANES * 2),
        input_output_aliases={5: 0} if before else {},
        name="collect_support",
    )(seq, order, support, counts, dictionary, *before)


def stage_orders(devices):
    distances = [2**bit for bit in range(devices.bit_length() - 1)]
    return distances, distances[:1] + distances[2:] + distances[1:2]


def slot_distance(slot, distances):
    bits = reversed(range(len(distances)))
    return sum(distance for bit, distance in zip(bits, distances) if slot >> bit & 1)


def gradient_kernel(mode, shards, pairs, seq, order, counts, own, blocks, near, far, targets, *refs):
    refs = list(refs)
    take = lambda: refs.pop(0)
    if mode == "first":
        thresh = take()
    keep, send = take(), take()
    if mode == "first":
        start_out, thresh_out = take(), take()
    if mode == "final":
        sent = take()
    held, codes, total = take(), take(), take()
    if mode == "first":
        starts, limits = take(), take()
    offsets, sems = refs

    groups = order.shape[0]
    pieces = pairs // PIECE
    me = own[0]

    def load(index):
        span = pl.ds(index * PIECE, PIECE)
        return pltpu.make_async_copy(blocks.at[span], held.at[span], sems.at[index])

    for index in range(pieces):
        load(index).start()
    held[pairs:] = jnp.zeros((SPARE,) + held.shape[1:], held.dtype)

    orders = stage_orders(shards)

    def holder(slot):
        far_half = slot >= shards // 2
        even = slot_distance(slot, orders[1 if far_half else 0])
        odd = slot_distance(slot, orders[0 if far_half else 1])
        return jnp.where(me % 2 == 0, even, odd) ^ me

    def shard_span(slot, size):
        return pl.ds(pl.multiple_of(holder(slot) * size, ROW_TILE), size)

    size_in = 2 * near.shape[0] // shards
    for slot in range(shards):
        source = near if slot < shards // 2 else far
        begin = slot % (shards // 2) * size_in
        codes[shard_span(slot, size_in), :] = source[begin : begin + size_in, :]

    def seat(index, offset):
        position, _, live = group_at(index, seq, order, counts)
        offsets[position] = offset
        return offset + live

    lax.fori_loop(0, groups, seat, jnp.int32(0))

    upper = upper_half((PATCHES, LANES))
    side = upper.astype(jnp.int32)

    def tile(pair):
        return pl.ds(pl.multiple_of(pair * PATCHES, PATCHES), PATCHES)

    def shifted(parts, count, odd, ahead):
        turned = [swap_halves(part) for part in parts]
        last = len(parts) - 1
        moved = []
        for pair in range(count):
            low, high = (pair, pair + 1) if ahead else (pair - 1, pair)
            low, high = min(max(low, 0), last), min(max(high, 0), last)
            value = jnp.where(upper[: turned[low].shape[0]], turned[high], turned[low])
            moved.append(jnp.where(odd, value, parts[min(pair, last)]))
        return moved

    def read_codes(position, offset, live, count):
        first = offset // 2
        if mode == "first":
            parts = [codes[tile(position * SLOT_PAIRS + pair), :] for pair in range(min(count, SLOT_PAIRS))]
            parts = shifted(parts, count, offset % 2 == 1, False)
        else:
            parts = [codes[tile(first + pair), :] for pair in range(count)]
        masked = []
        for pair, part in enumerate(parts):
            entry = 2 * (first + pair) + side
            mine = (entry >= offset) & (entry < offset + live)
            masked.append(jnp.where(mine, part, jnp.zeros_like(part)))
        return masked

    def write_packed(ref, parts, offset):
        first = offset // 2
        for pair, part in enumerate(parts):
            if pair == 0:
                part = jnp.where(upper | (offset % 2 == 0), part, ref[tile(first), :])
            ref[tile(first + pair), :] = part

    def one_group(position, group, offset, live, count):
        first = offset // 2
        parts = read_codes(position, offset, live, count)
        if mode == "first":
            write_packed(starts, parts, offset)
            write_packed(limits, [thresh[group]] * count, offset)
        matrix = jnp.concatenate([held[first + pair] for pair in range(count)], axis=1)
        point = jnp.concatenate(parts, axis=1)
        residual = lax.dot_general(point, matrix, (((1,), (1,)), ((), ())), preferred_element_type=jnp.float32)
        target = targets[tile(group), :].astype(jnp.float32)
        residual = (residual - target).astype(jnp.bfloat16)
        gradient = jnp.dot(residual, matrix, preferred_element_type=jnp.float32)
        write_packed(total, [gradient[:, pair * LANES : (pair + 1) * LANES] for pair in range(count)], offset)

    def wait_piece(index, carry):
        load(index).wait()
        return carry

    def two_groups(step, waited):
        picks = []
        chunks = 1
        for index in (2 * step, 2 * step + 1):
            position, group, live = group_at(index, seq, order, counts)
            offset = offsets[position]
            picks.append((position, group, offset, live))
            chunks = jnp.maximum(chunks, (live + offset % 2 + 3) // 4)
        reach = jnp.minimum(picks[1][2] // 2 + 2 * chunks - 1, pairs - 1)
        needed = jnp.maximum(reach // PIECE + 1, waited)
        lax.fori_loop(waited, needed, wait_piece, 0)
        for count in range(1, SLOTS // 4 + 2):

            @pl.when(chunks == count)
            def _(count=count):
                for pick in picks:
                    one_group(*pick, 2 * count)

        return needed

    waited = lax.fori_loop(0, groups // 2, two_groups, jnp.int32(0))
    lax.fori_loop(waited, pieces, wait_piece, 0)

    if mode != "final":
        size = 2 * keep.shape[0] // shards
        for slot in range(shards):
            begin = slot % (shards // 2) * size
            value = total[shard_span(slot, size), :]
            if slot < shards // 2:
                keep[begin : begin + size, :] = value
            else:
                send[begin : begin + size, :] = value.astype(send.dtype)
    if mode == "first":
        size = start_out.shape[0]
        span = pl.ds(pl.multiple_of(me * size, ROW_TILE), size)
        start_out[...] = starts[span, :]
        thresh_out[...] = limits[span, :]
    if mode == "final":
        offset = offsets[me]
        parts = read_codes(me, offset, counts[order[me]], SLOT_PAIRS + 1)
        for pair, part in enumerate(shifted(parts, SLOT_PAIRS, offset % 2 == 1, True)):
            sent[pair] = part
        for slot in range(shards):
            position = holder(slot)
            offset = offsets[position]
            live = counts[order[position]]
            parts = [total[tile(offset // 2 + pair), :] for pair in range(SLOT_PAIRS + 1)]
            begin = slot % (shards // 2) * SLOT_PAIRS * PATCHES
            for pair, part in enumerate(shifted(parts, SLOT_PAIRS, offset % 2 == 1, True)):
                value = jnp.where(2 * pair + side < live, part, 0.0)
                rows = slice(begin + pair * PATCHES, begin + (pair + 1) * PATCHES)
                if slot < shards // 2:
                    keep[rows, :] = value
                else:
                    send[rows, :] = value.astype(send.dtype)


def gradient_call(mode, shards, pairs, scalars, blocks, near, far, targets, extra=()):
    rows = blocks.shape[1]
    places = pairs + SPARE
    groups = scalars[1].shape[0]
    single, double = jnp.bfloat16, jnp.float32
    packed = (places * PATCHES, LANES)
    half_out = (groups * SLOT_PAIRS if mode == "final" else pairs) * PATCHES // 2
    shard = (2 * half_out // shards, LANES)
    outs = [((half_out, LANES), double), ((half_out, LANES), single)]
    if mode == "first":
        outs += [(shard, single), (shard, double)]
    if mode == "final":
        outs += [((SLOT_PAIRS, PATCHES, LANES), single)]
    codes = groups * SLOT_PAIRS * PATCHES if mode == "first" else packed[0]
    scratch = [((places, rows, LANES), single), ((codes, LANES), single), (packed, double)]
    if mode == "first":
        scratch += [(packed, single), (packed, double)]
    room = sum(math.prod(shape) * jnp.dtype(kind).itemsize for shape, kind in scratch)
    return pl.pallas_call(
        functools.partial(gradient_kernel, mode, shards, pairs),
        grid_spec=pltpu.PrefetchScalarGridSpec(
            num_scalar_prefetch=4,
            grid=(),
            in_specs=[pl.BlockSpec(memory_space=pltpu.HBM)]
            + [pl.BlockSpec(memory_space=pltpu.VMEM)] * (3 + len(extra)),
            out_specs=[pl.BlockSpec(memory_space=pltpu.VMEM)] * len(outs),
            scratch_shapes=[pltpu.VMEM(shape, kind) for shape, kind in scratch]
            + [pltpu.SMEM((groups,), jnp.int32), pltpu.SemaphoreType.DMA((pairs // PIECE,))],
        ),
        out_shape=[jax.ShapeDtypeStruct(shape, kind) for shape, kind in outs],
        compiler_params=pltpu.CompilerParams(vmem_limit_bytes=room + VMEM_MARGIN),
        cost_estimate=pl.CostEstimate(
            flops=4 * pairs * rows * LANES * MATRIX_UNIT, transcendentals=0, bytes_accessed=pairs * rows * LANES * 2
        ),
        name="gradient",
    )(*scalars, blocks, near, far, targets, *extra)


def exchange(value, stage):
    devices = lax.axis_size("rows")
    orders = stage_orders(devices)
    return lax.ppermute(value, "rows", [(i, i ^ orders[i % 2][stage]) for i in range(devices)])


def gather_shards(own, beside=()):
    value, made = own, ()
    stages = len(stage_orders(lax.axis_size("rows"))[0])
    steps = list(beside)
    for stage in reversed(range(1, stages)):
        value = jnp.concatenate([value, exchange(value, stage)], axis=0)
        if steps:
            value, *made = lax.optimization_barrier((value, steps.pop(0)(*made)))
    for step in steps:
        value, *made = lax.optimization_barrier((value, step(*made)))
    return value, exchange(value, 0), made


def reduce_shards(keep, send):
    total = keep + exchange(send, 0).astype(jnp.float32)
    for stage in range(1, len(stage_orders(lax.axis_size("rows"))[0])):
        middle = total.shape[0] // 2
        total = total[:middle] + exchange(total[middle:].astype(jnp.bfloat16), stage).astype(jnp.float32)
    return total


def packed_order(live):
    index = jnp.arange(live.shape[0])
    ahead = (live[None, :] > live[:, None]) | ((live[None, :] == live[:, None]) & (index[None, :] < index[:, None]))
    rank = jnp.sum(ahead.astype(jnp.int32), axis=1)
    return jnp.sum(jnp.where(rank[:, None] == index[None, :], index[:, None], 0), axis=0).astype(jnp.int32)


def shrink(value, thresh):
    return value - jnp.clip(value, -thresh, thresh)


def local(dictionary, patches, initial_codes, support, counts, group_order, penalty):
    groups = group_order.shape[0]
    position = lax.axis_index("rows")
    devices = lax.axis_size("rows")
    momenta = momentum_list()
    pairs = MEAN_LIVE * groups // 2

    laid = initial_codes.reshape(SLOT_PAIRS, 2, PATCHES, BLOCK).transpose(0, 2, 1, 3)
    laid = laid.reshape(SLOT_PAIRS * PATCHES, LANES)
    seq = packed_order(jnp.take(counts, group_order))
    collect = functools.partial(collect_support, seq, group_order, support, counts, dictionary, pairs)
    near, far, (blocks,) = gather_shards(laid, [functools.partial(collect, part) for part in range(SUPPORT_PARTS)])

    scalars = (seq, group_order, counts, position.astype(jnp.int32).reshape(1))
    targets = patches.T
    half_penalty = 0.5 * penalty
    thresh_tiles = jnp.broadcast_to(half_penalty[:, :, None], (groups, PATCHES, LANES))
    own_thresh = lax.dynamic_index_in_dim(half_penalty, group_order[position], 0, False)[None, :, None]

    run = functools.partial(gradient_call, shards=devices, pairs=pairs, scalars=scalars, blocks=blocks, targets=targets)
    keep, send, start, thresh = run("first", near=near, far=far, extra=(thresh_tiles,))
    point = previous = start.astype(jnp.float32)
    for turn in range(ITERS - 1):
        if turn:
            keep, send = run("packed", near=near, far=far)
        current = shrink(point - 0.5 * reduce_shards(keep, send), thresh)
        point = current + momenta[turn] * (current - previous)
        previous = current
        near, far, _ = gather_shards(point.astype(jnp.bfloat16))
    keep, send, sent = run("final", near=near, far=far)
    gradient = reduce_shards(keep, send).reshape(SLOT_PAIRS, PATCHES, LANES)
    sent = sent.astype(jnp.float32)
    result = shrink(sent - 0.5 * gradient, own_thresh)
    result = result.reshape(SLOT_PAIRS, PATCHES, 2, BLOCK).transpose(0, 2, 1, 3)
    return result.reshape(1, SLOTS, PATCHES * BLOCK)


def solution(mesh):
    in_specs = (
        P("rows", None),
        P("rows", "groups"),
        P(("groups", "rows"), None, None),
        P("groups", None),
        P("groups"),
        P("groups"),
        P("groups", None),
    )
    out_specs = P(("groups", "rows"), None, None)
    return jax.shard_map(local, mesh=mesh, in_specs=in_specs, out_specs=out_specs, check_vma=False)
```

```python
import functools
import math

import jax
import jax.numpy as jnp
from jax import lax
from jax.experimental import pallas as pl
from jax.experimental.pallas import tpu as pltpu
from jax.sharding import PartitionSpec as P

BLOCK = 64
SLOTS = 16
PATCHES = 64
ITERS = 3
MEAN_LIVE = 10
LANES = 2 * BLOCK
SLOT_PAIRS = SLOTS // 2
SPARE = SLOT_PAIRS + 2
ROW_TILE = 16
SUPPORT_PARTS = 2
SUPPORT_STEP = 4
PIECE = 5
MATRIX_UNIT = 256
VMEM_MARGIN = 3 * 1024 * 1024
SUPPORT_VMEM = 40 * 1024 * 1024
HELD_BYTES = 65 * 1024 * 1024


def momentum_list():
    values = []
    tvalue = 1.0
    for turn in range(ITERS):
        tnext = (1.0 + (1.0 + 4.0 * tvalue * tvalue) ** 0.5) / 2.0
        values.append((tvalue - 1.0) / tnext)
        tvalue = tnext
    return values


def swap_halves(value):
    return jnp.concatenate([value[:, BLOCK:], value[:, :BLOCK]], axis=1)


def upper_half(shape):
    return lax.broadcasted_iota(jnp.int32, shape, 1) >= BLOCK


def group_at(index, seq, order, counts):
    position = seq[index]
    group = order[position]
    return position, group, counts[group]


def support_kernel(begin, seq, order, support, counts, dictionary, *refs):
    out, held, picks, ids, sems, out_sems = refs[-6:]
    entries, rows, _ = held.shape
    pairs = entries // 2

    def fetch(entry, block):
        start = pl.multiple_of((block // 2) * LANES, LANES)
        return pltpu.make_async_copy(dictionary.at[:, pl.ds(start, LANES)], held.at[entry], sems.at[entry])

    def start_group(index, offset):
        _, group, live = group_at(index, seq, order, counts)

        def start_slot(slot, carry):
            block = support[group, slot]
            ids[offset + slot] = block
            fetch(offset + slot, block).start()
            return carry

        lax.fori_loop(jnp.clip(-offset, 0, live), jnp.clip(entries - offset, 0, live), start_slot, 0)
        return offset + live

    lax.fori_loop(0, order.shape[0], start_group, jnp.int32(-begin))
    shape = (2 * LANES, LANES)
    source = lax.broadcasted_iota(jnp.int32, shape, 0)
    target = lax.broadcasted_iota(jnp.int32, shape, 1)
    for choice in range(4):
        wanted = jnp.where(target < BLOCK, (choice % 2) * BLOCK + target, LANES + (choice // 2) * BLOCK + target - BLOCK)
        picks[choice] = (source == wanted).astype(jnp.float32).astype(jnp.bfloat16)

    def store(pair):
        return pltpu.make_async_copy(held.at[2 * pair], out.at[begin // 2 + pair], out_sems.at[pair])

    def pack(step, carry):
        span = [SUPPORT_STEP * step + pair for pair in range(SUPPORT_STEP)]
        for pair in span:
            fetch(2 * pair, ids[2 * pair]).wait()
            fetch(2 * pair + 1, ids[2 * pair + 1]).wait()
        packed = []
        for pair in span:
            choice = ids[2 * pair] % 2 + 2 * (ids[2 * pair + 1] % 2)
            both = jnp.concatenate([held[2 * pair], held[2 * pair + 1]], axis=1)
            packed.append(jnp.dot(both, picks[choice], preferred_element_type=jnp.float32).astype(jnp.bfloat16))
        for pair, value in zip(span, packed):
            held[2 * pair] = value
            store(pair).start()
        return carry

    lax.fori_loop(0, pairs // SUPPORT_STEP, pack, 0)

    def drain(pair, carry):
        store(pair).wait()
        return carry

    lax.fori_loop(0, pairs, drain, 0)


def collect_support(seq, order, support, counts, dictionary, pairs, part, *before):
    rows = dictionary.shape[0]
    pairs = pairs // SUPPORT_PARTS
    entries = 2 * pairs
    return pl.pallas_call(
        functools.partial(support_kernel, part * entries),
        grid_spec=pltpu.PrefetchScalarGridSpec(
            num_scalar_prefetch=4,
            grid=(),
            in_specs=[pl.BlockSpec(memory_space=pltpu.HBM)] * (1 + len(before)),
            out_specs=pl.BlockSpec(memory_space=pltpu.HBM),
            scratch_shapes=[
                pltpu.VMEM((entries, rows, LANES), dictionary.dtype),
                pltpu.VMEM((4, 2 * LANES, LANES), jnp.bfloat16),
                pltpu.SMEM((entries,), jnp.int32),
                pltpu.SemaphoreType.DMA((entries,)),
                pltpu.SemaphoreType.DMA((pairs,)),
            ],
        ),
        out_shape=jax.ShapeDtypeStruct((HELD_BYTES // (rows * LANES * 2), rows, LANES), dictionary.dtype),
        compiler_params=pltpu.CompilerParams(vmem_limit_bytes=SUPPORT_VMEM),
        cost_estimate=pl.CostEstimate(flops=0, transcendentals=0, bytes_accessed=6 * pairs * rows * LANES * 2),
        input_output_aliases={5: 0} if before else {},
        name="collect_support",
    )(seq, order, support, counts, dictionary, *before)


def stage_orders(devices):
    distances = [2**bit for bit in range(devices.bit_length() - 1)]
    return distances, distances[:1] + distances[2:] + distances[1:2]


def slot_distance(slot, distances):
    bits = reversed(range(len(distances)))
    return sum(distance for bit, distance in zip(bits, distances) if slot >> bit & 1)


def gradient_kernel(mode, shards, pairs, seq, order, counts, own, blocks, near, far, targets, *refs):
    refs = list(refs)
    take = lambda: refs.pop(0)
    if mode in ("first", "final"):
        thresh = take()
    keep, send = take(), take()
    if mode == "first":
        start_out, thresh_out = take(), take()
    if mode == "final":
        sent, thresh_out = take(), take()
    held, codes, total = take(), take(), take()
    if mode == "first":
        starts, limits = take(), take()
    offsets, sems = refs

    groups = order.shape[0]
    pieces = pairs // PIECE
    me = own[0]

    def load(index):
        span = pl.ds(index * PIECE, PIECE)
        return pltpu.make_async_copy(blocks.at[span], held.at[span], sems.at[index])

    for index in range(pieces):
        load(index).start()
    held[pairs:] = jnp.zeros((SPARE,) + held.shape[1:], held.dtype)

    orders = stage_orders(shards)

    def holder(slot):
        far_half = slot >= shards // 2
        even = slot_distance(slot, orders[1 if far_half else 0])
        odd = slot_distance(slot, orders[0 if far_half else 1])
        return jnp.where(me % 2 == 0, even, odd) ^ me

    def shard_span(slot, size):
        return pl.ds(pl.multiple_of(holder(slot) * size, ROW_TILE), size)

    size_in = 2 * near.shape[0] // shards
    for slot in range(shards):
        source = near if slot < shards // 2 else far
        begin = slot % (shards // 2) * size_in
        codes[shard_span(slot, size_in), :] = source[begin : begin + size_in, :]

    def seat(index, offset):
        position, _, live = group_at(index, seq, order, counts)
        offsets[position] = offset
        return offset + live

    lax.fori_loop(0, groups, seat, jnp.int32(0))

    upper = upper_half((PATCHES, LANES))
    side = upper.astype(jnp.int32)

    def tile(pair):
        return pl.ds(pl.multiple_of(pair * PATCHES, PATCHES), PATCHES)

    def shifted(parts, count, odd, ahead):
        turned = [swap_halves(part) for part in parts]
        last = len(parts) - 1
        moved = []
        for pair in range(count):
            low, high = (pair, pair + 1) if ahead else (pair - 1, pair)
            low, high = min(max(low, 0), last), min(max(high, 0), last)
            value = jnp.where(upper[: turned[low].shape[0]], turned[high], turned[low])
            moved.append(jnp.where(odd, value, parts[min(pair, last)]))
        return moved

    def read_codes(position, offset, live, count):
        first = offset // 2
        if mode == "first":
            parts = [codes[tile(position * SLOT_PAIRS + pair), :] for pair in range(min(count, SLOT_PAIRS))]
            parts = shifted(parts, count, offset % 2 == 1, False)
        else:
            parts = [codes[tile(first + pair), :] for pair in range(count)]
        masked = []
        for pair, part in enumerate(parts):
            entry = 2 * (first + pair) + side
            mine = (entry >= offset) & (entry < offset + live)
            masked.append(jnp.where(mine, part, jnp.zeros_like(part)))
        return masked

    def write_packed(ref, parts, offset):
        first = offset // 2
        for pair, part in enumerate(parts):
            if pair == 0:
                part = jnp.where(upper | (offset % 2 == 0), part, ref[tile(first), :])
            ref[tile(first + pair), :] = part

    def one_group(position, group, offset, live, count):
        first = offset // 2
        parts = read_codes(position, offset, live, count)
        if mode == "first":
            write_packed(starts, parts, offset)
            write_packed(limits, [thresh[group]] * count, offset)
        matrix = jnp.concatenate([held[first + pair] for pair in range(count)], axis=1)
        point = jnp.concatenate(parts, axis=1)
        residual = lax.dot_general(point, matrix, (((1,), (1,)), ((), ())), preferred_element_type=jnp.float32)
        target = targets[tile(group), :].astype(jnp.float32)
        residual = (residual - target).astype(jnp.bfloat16)
        gradient = jnp.dot(residual, matrix, preferred_element_type=jnp.float32)
        write_packed(total, [gradient[:, pair * LANES : (pair + 1) * LANES] for pair in range(count)], offset)

    def wait_piece(index, carry):
        load(index).wait()
        return carry

    def two_groups(step, waited):
        picks = []
        chunks = 1
        for index in (2 * step, 2 * step + 1):
            position, group, live = group_at(index, seq, order, counts)
            offset = offsets[position]
            picks.append((position, group, offset, live))
            chunks = jnp.maximum(chunks, (live + offset % 2 + 3) // 4)
        reach = jnp.minimum(picks[1][2] // 2 + 2 * chunks - 1, pairs - 1)
        needed = jnp.maximum(reach // PIECE + 1, waited)
        lax.fori_loop(waited, needed, wait_piece, 0)
        for count in range(1, SLOTS // 4 + 2):

            @pl.when(chunks == count)
            def _(count=count):
                for pick in picks:
                    one_group(*pick, 2 * count)

        return needed

    waited = lax.fori_loop(0, groups // 2, two_groups, jnp.int32(0))
    lax.fori_loop(waited, pieces, wait_piece, 0)

    if mode != "final":
        size = 2 * keep.shape[0] // shards
        for slot in range(shards):
            begin = slot % (shards // 2) * size
            value = total[shard_span(slot, size), :]
            if slot < shards // 2:
                keep[begin : begin + size, :] = value
            else:
                send[begin : begin + size, :] = value.astype(send.dtype)
    if mode == "first":
        size = start_out.shape[0]
        span = pl.ds(pl.multiple_of(me * size, ROW_TILE), size)
        start_out[...] = starts[span, :]
        thresh_out[...] = limits[span, :]
    if mode == "final":
        offset = offsets[me]
        parts = read_codes(me, offset, counts[order[me]], SLOT_PAIRS + 1)
        for pair, part in enumerate(shifted(parts, SLOT_PAIRS, offset % 2 == 1, True)):
            sent[pair] = part
        thresh_out[...] = thresh[order[me]]
        for slot in range(shards):
            position = holder(slot)
            offset = offsets[position]
            live = counts[order[position]]
            parts = [total[tile(offset // 2 + pair), :] for pair in range(SLOT_PAIRS + 1)]
            begin = slot % (shards // 2) * SLOT_PAIRS * PATCHES
            for pair, part in enumerate(shifted(parts, SLOT_PAIRS, offset % 2 == 1, True)):
                value = jnp.where(2 * pair + side < live, part, 0.0)
                rows = slice(begin + pair * PATCHES, begin + (pair + 1) * PATCHES)
                if slot < shards // 2:
                    keep[rows, :] = value
                else:
                    send[rows, :] = value.astype(send.dtype)


def gradient_call(mode, shards, pairs, scalars, blocks, near, far, targets, extra=()):
    rows = blocks.shape[1]
    places = pairs + SPARE
    groups = scalars[1].shape[0]
    single, double = jnp.bfloat16, jnp.float32
    packed = (places * PATCHES, LANES)
    half_out = (groups * SLOT_PAIRS if mode == "final" else pairs) * PATCHES // 2
    shard = (2 * half_out // shards, LANES)
    outs = [((half_out, LANES), double), ((half_out, LANES), single)]
    if mode == "first":
        outs += [(shard, single), (shard, double)]
    if mode == "final":
        outs += [((SLOT_PAIRS, PATCHES, LANES), single), ((PATCHES, LANES), double)]
    codes = groups * SLOT_PAIRS * PATCHES if mode == "first" else packed[0]
    scratch = [((places, rows, LANES), single), ((codes, LANES), single), (packed, double)]
    if mode == "first":
        scratch += [(packed, single), (packed, double)]
    room = sum(math.prod(shape) * jnp.dtype(kind).itemsize for shape, kind in scratch)
    return pl.pallas_call(
        functools.partial(gradient_kernel, mode, shards, pairs),
        grid_spec=pltpu.PrefetchScalarGridSpec(
            num_scalar_prefetch=4,
            grid=(),
            in_specs=[pl.BlockSpec(memory_space=pltpu.HBM)]
            + [pl.BlockSpec(memory_space=pltpu.VMEM)] * (3 + len(extra)),
            out_specs=[pl.BlockSpec(memory_space=pltpu.VMEM)] * len(outs),
            scratch_shapes=[pltpu.VMEM(shape, kind) for shape, kind in scratch]
            + [pltpu.SMEM((groups,), jnp.int32), pltpu.SemaphoreType.DMA((pairs // PIECE,))],
        ),
        out_shape=[jax.ShapeDtypeStruct(shape, kind) for shape, kind in outs],
        compiler_params=pltpu.CompilerParams(vmem_limit_bytes=room + VMEM_MARGIN),
        cost_estimate=pl.CostEstimate(
            flops=4 * pairs * rows * LANES * MATRIX_UNIT, transcendentals=0, bytes_accessed=pairs * rows * LANES * 2
        ),
        name="gradient",
    )(*scalars, blocks, near, far, targets, *extra)


def exchange(value, distance, cores=(0, 1)):
    devices = lax.axis_size("rows")
    return lax.ppermute(value, "rows", [(i, i ^ distance) for i in range(devices) if i % 2 in cores])


def column_distances(devices):
    distances = stage_orders(devices)[0][2:]
    return [slot_distance(slot, distances) for slot in range(devices // 4)]


def by_core(even, odd):
    return jnp.where(lax.axis_index("rows") % 2 == 0, even, odd)


def gather_shards(own, beside=()):
    apart = column_distances(lax.axis_size("rows"))[1:]
    made = ()
    quarter = jnp.concatenate([own] + [exchange(own, distance, (0,)) for distance in apart], axis=0)
    couple = jnp.concatenate([own, exchange(own, 2, (1,))], axis=0)
    if beside:
        quarter, couple, *made = lax.optimization_barrier((quarter, couple, beside[0]()))
    even = jnp.concatenate([quarter, exchange(quarter, 2, (0,))], axis=0)
    odd = jnp.concatenate([couple] + [exchange(couple, distance, (1,)) for distance in apart], axis=0)
    near = by_core(even, odd)
    if beside:
        near, *made = lax.optimization_barrier((near, beside[1](*made)))
    return near, exchange(near, 1), made


def reduce_shards(keep, send):
    devices = lax.axis_size("rows")
    apart = column_distances(devices)
    size = 2 * keep.shape[0] // devices

    def arrived(value, distance, cores):
        return exchange(value.astype(jnp.bfloat16), distance, cores).astype(jnp.float32)

    total = keep + exchange(send, 1).astype(jnp.float32)
    middle = total.shape[0] // 2
    even = total[:middle] + arrived(total[middle:], 2, (0,))
    odd = total[: 2 * size]
    for place in range(1, len(apart)):
        odd = odd + arrived(total[2 * place * size : 2 * (place + 1) * size], apart[place], (1,))
    sums = even[:size]
    for place in range(1, len(apart)):
        sums = sums + arrived(even[place * size : (place + 1) * size], apart[place], (0,))
    return by_core(sums, odd[:size] + arrived(odd[size:], 2, (1,)))


def packed_order(live):
    index = jnp.arange(live.shape[0])
    ahead = (live[None, :] > live[:, None]) | ((live[None, :] == live[:, None]) & (index[None, :] < index[:, None]))
    rank = jnp.sum(ahead.astype(jnp.int32), axis=1)
    return jnp.sum(jnp.where(rank[:, None] == index[None, :], index[:, None], 0), axis=0).astype(jnp.int32)


def shrink(value, thresh):
    return value - jnp.clip(value, -thresh, thresh)


def local(dictionary, patches, initial_codes, support, counts, group_order, penalty):
    groups = group_order.shape[0]
    position = lax.axis_index("rows")
    devices = lax.axis_size("rows")
    momenta = momentum_list()
    pairs = MEAN_LIVE * groups // 2

    laid = initial_codes.reshape(SLOT_PAIRS, 2, PATCHES, BLOCK).transpose(0, 2, 1, 3)
    laid = laid.reshape(SLOT_PAIRS * PATCHES, LANES)
    seq = packed_order(jnp.take(counts, group_order))
    collect = functools.partial(collect_support, seq, group_order, support, counts, dictionary, pairs)
    near, far, (blocks,) = gather_shards(laid, [functools.partial(collect, part) for part in range(SUPPORT_PARTS)])

    scalars = (seq, group_order, counts, position.astype(jnp.int32).reshape(1))
    targets = patches.T
    half_penalty = 0.5 * penalty
    thresh_tiles = jnp.broadcast_to(half_penalty[:, :, None], (groups, PATCHES, LANES))

    run = functools.partial(gradient_call, shards=devices, pairs=pairs, scalars=scalars, blocks=blocks, targets=targets)
    keep, send, start, thresh = run("first", near=near, far=far, extra=(thresh_tiles,))
    point = previous = start.astype(jnp.float32)
    for turn in range(ITERS - 1):
        if turn:
            keep, send = run("packed", near=near, far=far)
        current = shrink(point - 0.5 * reduce_shards(keep, send), thresh)
        point = current + momenta[turn] * (current - previous)
        previous = current
        near, far, _ = gather_shards(point.astype(jnp.bfloat16))
    keep, send, sent, thresh = run("final", near=near, far=far, extra=(thresh_tiles,))
    gradient = reduce_shards(keep, send).reshape(SLOT_PAIRS, PATCHES, LANES)
    sent = sent.astype(jnp.float32)
    result = shrink(sent - 0.5 * gradient, thresh[None])
    result = result.reshape(SLOT_PAIRS, PATCHES, 2, BLOCK).transpose(0, 2, 1, 3)
    return result.reshape(1, SLOTS, PATCHES * BLOCK)


def solution(mesh):
    in_specs = (
        P("rows", None),
        P("rows", "groups"),
        P(("groups", "rows"), None, None),
        P("groups", None),
        P("groups"),
        P("groups"),
        P("groups", None),
    )
    out_specs = P(("groups", "rows"), None, None)
    return jax.shard_map(local, mesh=mesh, in_specs=in_specs, out_specs=out_specs, check_vma=False)
```

```python
import functools
import math

import jax
import jax.numpy as jnp
from jax import lax
from jax.experimental import pallas as pl
from jax.experimental.pallas import tpu as pltpu
from jax.sharding import PartitionSpec as P

BLOCK = 64
SLOTS = 16
PATCHES = 64
ITERS = 3
MEAN_LIVE = 10
LANES = 2 * BLOCK
SLOT_PAIRS = SLOTS // 2
SPARE = SLOT_PAIRS + 2
ROW_TILE = 16
SUPPORT_PARTS = 2
SUPPORT_STEP = 4
PIECE = 5
MATRIX_UNIT = 256
VMEM_MARGIN = 3 * 1024 * 1024
SUPPORT_VMEM = 40 * 1024 * 1024
HELD_BYTES = 65 * 1024 * 1024


def momentum_list():
    values = []
    tvalue = 1.0
    for turn in range(ITERS):
        tnext = (1.0 + (1.0 + 4.0 * tvalue * tvalue) ** 0.5) / 2.0
        values.append((tvalue - 1.0) / tnext)
        tvalue = tnext
    return values


def swap_halves(value):
    return jnp.concatenate([value[:, BLOCK:], value[:, :BLOCK]], axis=1)


def upper_half(shape):
    return lax.broadcasted_iota(jnp.int32, shape, 1) >= BLOCK


def group_at(index, seq, order, counts):
    position = seq[index]
    group = order[position]
    return position, group, counts[group]


def support_kernel(begin, seq, order, support, counts, dictionary, *refs):
    out, held, picks, ids, sems, out_sems = refs[-6:]
    entries, rows, _ = held.shape
    pairs = entries // 2

    def fetch(entry, block):
        start = pl.multiple_of((block // 2) * LANES, LANES)
        return pltpu.make_async_copy(dictionary.at[:, pl.ds(start, LANES)], held.at[entry], sems.at[entry])

    def start_group(index, offset):
        _, group, live = group_at(index, seq, order, counts)

        def start_slot(slot, carry):
            block = support[group, slot]
            ids[offset + slot] = block
            fetch(offset + slot, block).start()
            return carry

        lax.fori_loop(jnp.clip(-offset, 0, live), jnp.clip(entries - offset, 0, live), start_slot, 0)
        return offset + live

    lax.fori_loop(0, order.shape[0], start_group, jnp.int32(-begin))
    shape = (2 * LANES, LANES)
    source = lax.broadcasted_iota(jnp.int32, shape, 0)
    target = lax.broadcasted_iota(jnp.int32, shape, 1)
    for choice in range(4):
        wanted = jnp.where(target < BLOCK, (choice % 2) * BLOCK + target, LANES + (choice // 2) * BLOCK + target - BLOCK)
        picks[choice] = (source == wanted).astype(jnp.float32).astype(jnp.bfloat16)

    def store(pair):
        return pltpu.make_async_copy(held.at[2 * pair], out.at[begin // 2 + pair], out_sems.at[pair])

    def pack(step, carry):
        span = [SUPPORT_STEP * step + pair for pair in range(SUPPORT_STEP)]
        for pair in span:
            fetch(2 * pair, ids[2 * pair]).wait()
            fetch(2 * pair + 1, ids[2 * pair + 1]).wait()
        packed = []
        for pair in span:
            choice = ids[2 * pair] % 2 + 2 * (ids[2 * pair + 1] % 2)
            both = jnp.concatenate([held[2 * pair], held[2 * pair + 1]], axis=1)
            packed.append(jnp.dot(both, picks[choice], preferred_element_type=jnp.float32).astype(jnp.bfloat16))
        for pair, value in zip(span, packed):
            held[2 * pair] = value
            store(pair).start()
        return carry

    lax.fori_loop(0, pairs // SUPPORT_STEP, pack, 0)

    def drain(pair, carry):
        store(pair).wait()
        return carry

    lax.fori_loop(0, pairs, drain, 0)


def collect_support(seq, order, support, counts, dictionary, pairs, part, *before):
    rows = dictionary.shape[0]
    pairs = pairs // SUPPORT_PARTS
    entries = 2 * pairs
    return pl.pallas_call(
        functools.partial(support_kernel, part * entries),
        grid_spec=pltpu.PrefetchScalarGridSpec(
            num_scalar_prefetch=4,
            grid=(),
            in_specs=[pl.BlockSpec(memory_space=pltpu.HBM)] * (1 + len(before)),
            out_specs=pl.BlockSpec(memory_space=pltpu.HBM),
            scratch_shapes=[
                pltpu.VMEM((entries, rows, LANES), dictionary.dtype),
                pltpu.VMEM((4, 2 * LANES, LANES), jnp.bfloat16),
                pltpu.SMEM((entries,), jnp.int32),
                pltpu.SemaphoreType.DMA((entries,)),
                pltpu.SemaphoreType.DMA((pairs,)),
            ],
        ),
        out_shape=jax.ShapeDtypeStruct((HELD_BYTES // (rows * LANES * 2), rows, LANES), dictionary.dtype),
        compiler_params=pltpu.CompilerParams(vmem_limit_bytes=SUPPORT_VMEM),
        cost_estimate=pl.CostEstimate(flops=0, transcendentals=0, bytes_accessed=6 * pairs * rows * LANES * 2),
        input_output_aliases={5: 0} if before else {},
        name="collect_support",
    )(seq, order, support, counts, dictionary, *before)


def stage_distances(devices):
    return [2**bit for bit in range(devices.bit_length() - 1)]


def last_orders(devices):
    distances = stage_distances(devices)
    return distances, distances[:1] + distances[2:] + distances[1:2]


def slot_distance(slot, distances):
    bits = reversed(range(len(distances)))
    return sum(distance for bit, distance in zip(bits, distances) if slot >> bit & 1)


def gradient_kernel(mode, shards, pairs, seq, order, counts, own, blocks, near, far, targets, *refs):
    refs = list(refs)
    take = lambda: refs.pop(0)
    if mode in ("first", "final"):
        thresh = take()
    keep, send = take(), take()
    if mode == "first":
        start_out, thresh_out = take(), take()
    if mode == "final":
        sent, thresh_out = take(), take()
    held, codes, total = take(), take(), take()
    if mode == "first":
        starts, limits = take(), take()
    offsets, sems = refs

    groups = order.shape[0]
    pieces = pairs // PIECE
    me = own[0]

    def load(index):
        span = pl.ds(index * PIECE, PIECE)
        return pltpu.make_async_copy(blocks.at[span], held.at[span], sems.at[index])

    for index in range(pieces):
        load(index).start()
    held[pairs:] = jnp.zeros((SPARE,) + held.shape[1:], held.dtype)

    distances = stage_distances(shards)

    def shard_span(slot, size):
        return pl.ds(pl.multiple_of((slot_distance(slot, distances) ^ me) * size, ROW_TILE), size)

    def last_holder(slot):
        even, odd = (slot_distance(slot, order) for order in last_orders(shards))
        if slot >= shards // 2:
            even, odd = odd, even
        return jnp.where(me % 2 == 0, even, odd) ^ me

    size_in = 2 * near.shape[0] // shards
    for slot in range(shards):
        source = near if slot < shards // 2 else far
        begin = slot % (shards // 2) * size_in
        codes[shard_span(slot, size_in), :] = source[begin : begin + size_in, :]

    def seat(index, offset):
        position, _, live = group_at(index, seq, order, counts)
        offsets[position] = offset
        return offset + live

    lax.fori_loop(0, groups, seat, jnp.int32(0))

    upper = upper_half((PATCHES, LANES))
    side = upper.astype(jnp.int32)

    def tile(pair):
        return pl.ds(pl.multiple_of(pair * PATCHES, PATCHES), PATCHES)

    def shifted(parts, count, odd, ahead):
        turned = [swap_halves(part) for part in parts]
        last = len(parts) - 1
        moved = []
        for pair in range(count):
            low, high = (pair, pair + 1) if ahead else (pair - 1, pair)
            low, high = min(max(low, 0), last), min(max(high, 0), last)
            value = jnp.where(upper[: turned[low].shape[0]], turned[high], turned[low])
            moved.append(jnp.where(odd, value, parts[min(pair, last)]))
        return moved

    def read_codes(position, offset, live, count):
        first = offset // 2
        if mode == "first":
            parts = [codes[tile(position * SLOT_PAIRS + pair), :] for pair in range(min(count, SLOT_PAIRS))]
            parts = shifted(parts, count, offset % 2 == 1, False)
        else:
            parts = [codes[tile(first + pair), :] for pair in range(count)]
        masked = []
        for pair, part in enumerate(parts):
            entry = 2 * (first + pair) + side
            mine = (entry >= offset) & (entry < offset + live)
            masked.append(jnp.where(mine, part, jnp.zeros_like(part)))
        return masked

    def write_packed(ref, parts, offset):
        first = offset // 2
        for pair, part in enumerate(parts):
            if pair == 0:
                part = jnp.where(upper | (offset % 2 == 0), part, ref[tile(first), :])
            ref[tile(first + pair), :] = part

    def one_group(position, group, offset, live, count):
        first = offset // 2
        parts = read_codes(position, offset, live, count)
        if mode == "first":
            write_packed(starts, parts, offset)
            write_packed(limits, [thresh[group]] * count, offset)
        matrix = jnp.concatenate([held[first + pair] for pair in range(count)], axis=1)
        point = jnp.concatenate(parts, axis=1)
        residual = lax.dot_general(point, matrix, (((1,), (1,)), ((), ())), preferred_element_type=jnp.float32)
        target = targets[tile(group), :].astype(jnp.float32)
        residual = (residual - target).astype(jnp.bfloat16)
        gradient = jnp.dot(residual, matrix, preferred_element_type=jnp.float32)
        write_packed(total, [gradient[:, pair * LANES : (pair + 1) * LANES] for pair in range(count)], offset)

    def wait_piece(index, carry):
        load(index).wait()
        return carry

    def two_groups(step, waited):
        picks = []
        chunks = 1
        for index in (2 * step, 2 * step + 1):
            position, group, live = group_at(index, seq, order, counts)
            offset = offsets[position]
            picks.append((position, group, offset, live))
            chunks = jnp.maximum(chunks, (live + offset % 2 + 3) // 4)
        reach = jnp.minimum(picks[1][2] // 2 + 2 * chunks - 1, pairs - 1)
        needed = jnp.maximum(reach // PIECE + 1, waited)
        lax.fori_loop(waited, needed, wait_piece, 0)
        for count in range(1, SLOTS // 4 + 2):

            @pl.when(chunks == count)
            def _(count=count):
                for pick in picks:
                    one_group(*pick, 2 * count)

        return needed

    waited = lax.fori_loop(0, groups // 2, two_groups, jnp.int32(0))
    lax.fori_loop(waited, pieces, wait_piece, 0)

    if mode != "final":
        size = 2 * keep.shape[0] // shards
        for slot in range(shards):
            begin = slot % (shards // 2) * size
            value = total[shard_span(slot, size), :]
            if slot < shards // 2:
                keep[begin : begin + size, :] = value
            else:
                send[begin : begin + size, :] = value.astype(send.dtype)
    if mode == "first":
        size = start_out.shape[0]
        span = pl.ds(pl.multiple_of(me * size, ROW_TILE), size)
        start_out[...] = starts[span, :]
        thresh_out[...] = limits[span, :]
    if mode == "final":
        offset = offsets[me]
        parts = read_codes(me, offset, counts[order[me]], SLOT_PAIRS + 1)
        for pair, part in enumerate(shifted(parts, SLOT_PAIRS, offset % 2 == 1, True)):
            sent[pair] = part
        thresh_out[...] = thresh[order[me]]
        for slot in range(shards):
            position = last_holder(slot)
            offset = offsets[position]
            live = counts[order[position]]
            parts = [total[tile(offset // 2 + pair), :] for pair in range(SLOT_PAIRS + 1)]
            begin = slot % (shards // 2) * SLOT_PAIRS * PATCHES
            for pair, part in enumerate(shifted(parts, SLOT_PAIRS, offset % 2 == 1, True)):
                value = jnp.where(2 * pair + side < live, part, 0.0)
                rows = slice(begin + pair * PATCHES, begin + (pair + 1) * PATCHES)
                if slot < shards // 2:
                    keep[rows, :] = value
                else:
                    send[rows, :] = value.astype(send.dtype)


def gradient_call(mode, shards, pairs, scalars, blocks, near, far, targets, extra=()):
    rows = blocks.shape[1]
    places = pairs + SPARE
    groups = scalars[1].shape[0]
    single, double = jnp.bfloat16, jnp.float32
    packed = (places * PATCHES, LANES)
    half_out = (groups * SLOT_PAIRS if mode == "final" else pairs) * PATCHES // 2
    shard = (2 * half_out // shards, LANES)
    outs = [((half_out, LANES), double), ((half_out, LANES), single)]
    if mode == "first":
        outs += [(shard, single), (shard, double)]
    if mode == "final":
        outs += [((SLOT_PAIRS, PATCHES, LANES), single), ((PATCHES, LANES), double)]
    codes = groups * SLOT_PAIRS * PATCHES if mode == "first" else packed[0]
    scratch = [((places, rows, LANES), single), ((codes, LANES), single), (packed, double)]
    if mode == "first":
        scratch += [(packed, single), (packed, double)]
    room = sum(math.prod(shape) * jnp.dtype(kind).itemsize for shape, kind in scratch)
    return pl.pallas_call(
        functools.partial(gradient_kernel, mode, shards, pairs),
        grid_spec=pltpu.PrefetchScalarGridSpec(
            num_scalar_prefetch=4,
            grid=(),
            in_specs=[pl.BlockSpec(memory_space=pltpu.HBM)]
            + [pl.BlockSpec(memory_space=pltpu.VMEM)] * (3 + len(extra)),
            out_specs=[pl.BlockSpec(memory_space=pltpu.VMEM)] * len(outs),
            scratch_shapes=[pltpu.VMEM(shape, kind) for shape, kind in scratch]
            + [pltpu.SMEM((groups,), jnp.int32), pltpu.SemaphoreType.DMA((pairs // PIECE,))],
        ),
        out_shape=[jax.ShapeDtypeStruct(shape, kind) for shape, kind in outs],
        compiler_params=pltpu.CompilerParams(vmem_limit_bytes=room + VMEM_MARGIN),
        cost_estimate=pl.CostEstimate(
            flops=4 * pairs * rows * LANES * MATRIX_UNIT, transcendentals=0, bytes_accessed=pairs * rows * LANES * 2
        ),
        name="gradient",
    )(*scalars, blocks, near, far, targets, *extra)


def exchange(value, even, odd=None):
    devices = lax.axis_size("rows")
    apart = (even, even if odd is None else odd)
    return lax.ppermute(value, "rows", [(i, i ^ apart[i % 2]) for i in range(devices)])


def gather_shards(own, beside=()):
    distances = stage_distances(lax.axis_size("rows"))
    apart = [slot_distance(slot, distances[2:]) for slot in range(lax.axis_size("rows") // 4)]
    made = ()
    value = jnp.concatenate([own] + [exchange(own, distance) for distance in apart[1:]], axis=0)
    if beside:
        value, *made = lax.optimization_barrier((value, beside[0]()))
    value = jnp.concatenate([value, exchange(value, distances[1])], axis=0)
    if beside:
        value, *made = lax.optimization_barrier((value, beside[1](*made)))
    return value, exchange(value, distances[0]), made


def reduce_shards(keep, send):
    devices = lax.axis_size("rows")
    distances = stage_distances(devices)
    half = keep + exchange(send, distances[0]).astype(jnp.float32)
    size = 2 * keep.shape[0] // devices
    sent = half.astype(jnp.bfloat16)
    total = half[:size]
    for slot in range(1, devices // 2):
        share = exchange(sent[slot * size : (slot + 1) * size], slot_distance(slot, distances[1:]))
        total = total + share.astype(jnp.float32)
    return total


def last_reduce(keep, send):
    total = keep + exchange(send, 1).astype(jnp.float32)
    for even, odd in list(zip(*last_orders(lax.axis_size("rows"))))[1:]:
        middle = total.shape[0] // 2
        total = total[:middle] + exchange(total[middle:].astype(jnp.bfloat16), even, odd).astype(jnp.float32)
    return total


def packed_order(live):
    index = jnp.arange(live.shape[0])
    ahead = (live[None, :] > live[:, None]) | ((live[None, :] == live[:, None]) & (index[None, :] < index[:, None]))
    rank = jnp.sum(ahead.astype(jnp.int32), axis=1)
    return jnp.sum(jnp.where(rank[:, None] == index[None, :], index[:, None], 0), axis=0).astype(jnp.int32)


def shrink(value, thresh):
    return value - jnp.clip(value, -thresh, thresh)


def local(dictionary, patches, initial_codes, support, counts, group_order, penalty):
    groups = group_order.shape[0]
    position = lax.axis_index("rows")
    devices = lax.axis_size("rows")
    momenta = momentum_list()
    pairs = MEAN_LIVE * groups // 2

    laid = initial_codes.reshape(SLOT_PAIRS, 2, PATCHES, BLOCK).transpose(0, 2, 1, 3)
    laid = laid.reshape(SLOT_PAIRS * PATCHES, LANES)
    seq = packed_order(jnp.take(counts, group_order))
    collect = functools.partial(collect_support, seq, group_order, support, counts, dictionary, pairs)
    near, far, (blocks,) = gather_shards(laid, [functools.partial(collect, part) for part in range(SUPPORT_PARTS)])

    scalars = (seq, group_order, counts, position.astype(jnp.int32).reshape(1))
    targets = patches.T
    half_penalty = 0.5 * penalty
    thresh_tiles = jnp.broadcast_to(half_penalty[:, :, None], (groups, PATCHES, LANES))

    run = functools.partial(gradient_call, shards=devices, pairs=pairs, scalars=scalars, blocks=blocks, targets=targets)
    keep, send, start, thresh = run("first", near=near, far=far, extra=(thresh_tiles,))
    point = previous = start.astype(jnp.float32)
    for turn in range(ITERS - 1):
        if turn:
            keep, send = run("packed", near=near, far=far)
        current = shrink(point - 0.5 * reduce_shards(keep, send), thresh)
        point = current + momenta[turn] * (current - previous)
        previous = current
        near, far, _ = gather_shards(point.astype(jnp.bfloat16))
    keep, send, sent, thresh = run("final", near=near, far=far, extra=(thresh_tiles,))
    gradient = last_reduce(keep, send).reshape(SLOT_PAIRS, PATCHES, LANES)
    sent = sent.astype(jnp.float32)
    result = shrink(sent - 0.5 * gradient, thresh[None])
    result = result.reshape(SLOT_PAIRS, PATCHES, 2, BLOCK).transpose(0, 2, 1, 3)
    return result.reshape(1, SLOTS, PATCHES * BLOCK)


def solution(mesh):
    in_specs = (
        P("rows", None),
        P("rows", "groups"),
        P(("groups", "rows"), None, None),
        P("groups", None),
        P("groups"),
        P("groups"),
        P("groups", None),
    )
    out_specs = P(("groups", "rows"), None, None)
    return jax.shard_map(local, mesh=mesh, in_specs=in_specs, out_specs=out_specs, check_vma=False)
```

```python
import functools
import math

import jax
import jax.numpy as jnp
from jax import lax
from jax.experimental import pallas as pl
from jax.experimental.pallas import tpu as pltpu
from jax.sharding import PartitionSpec as P

BLOCK = 64
SLOTS = 16
PATCHES = 64
ITERS = 3
MEAN_LIVE = 10
LANES = 2 * BLOCK
SLOT_PAIRS = SLOTS // 2
SPARE = SLOT_PAIRS + 2
ROW_TILE = 16
SUPPORT_PARTS = 2
SUPPORT_STEP = 4
PIECE = 5
MATRIX_UNIT = 256
VMEM_MARGIN = 3 * 1024 * 1024
SUPPORT_VMEM = 40 * 1024 * 1024
HELD_BYTES = 65 * 1024 * 1024


def momentum_list():
    values = []
    tvalue = 1.0
    for turn in range(ITERS):
        tnext = (1.0 + (1.0 + 4.0 * tvalue * tvalue) ** 0.5) / 2.0
        values.append((tvalue - 1.0) / tnext)
        tvalue = tnext
    return values


def swap_halves(value):
    return jnp.concatenate([value[:, BLOCK:], value[:, :BLOCK]], axis=1)


def upper_half(shape):
    return lax.broadcasted_iota(jnp.int32, shape, 1) >= BLOCK


class Part:
    def __init__(self, ref, begin, width=1):
        self.ref, self.begin, self.width = ref, begin, width

    def __getitem__(self, index):
        if isinstance(index, tuple):
            index = index[0] * self.width + index[1]
        return self.ref[self.begin + index]


def scalar_parts(scalars, groups):
    seq, order, counts = (Part(scalars, part * groups) for part in range(3))
    return seq, order, counts, Part(scalars, 3 * groups, SLOTS), scalars[groups * (3 + SLOTS)]


def group_at(index, seq, order, counts):
    position = seq[index]
    group = order[position]
    return position, group, counts[group]


def support_kernel(begin, groups, scalars, dictionary, *refs):
    out, held, picks, ids, sems, out_sems = refs[-6:]
    seq, order, counts, support, _ = scalar_parts(scalars, groups)
    entries, rows, _ = held.shape
    pairs = entries // 2

    def fetch(entry, block):
        start = pl.multiple_of((block // 2) * LANES, LANES)
        return pltpu.make_async_copy(dictionary.at[:, pl.ds(start, LANES)], held.at[entry], sems.at[entry])

    def start_group(index, offset):
        _, group, live = group_at(index, seq, order, counts)

        def start_slot(slot, carry):
            block = support[group, slot]
            ids[offset + slot] = block
            fetch(offset + slot, block).start()
            return carry

        lax.fori_loop(jnp.clip(-offset, 0, live), jnp.clip(entries - offset, 0, live), start_slot, 0)
        return offset + live

    lax.fori_loop(0, groups, start_group, jnp.int32(-begin))
    shape = (2 * LANES, LANES)
    source = lax.broadcasted_iota(jnp.int32, shape, 0)
    target = lax.broadcasted_iota(jnp.int32, shape, 1)
    for choice in range(4):
        wanted = jnp.where(target < BLOCK, (choice % 2) * BLOCK + target, LANES + (choice // 2) * BLOCK + target - BLOCK)
        picks[choice] = (source == wanted).astype(jnp.float32).astype(jnp.bfloat16)

    def store(pair):
        return pltpu.make_async_copy(held.at[2 * pair], out.at[begin // 2 + pair], out_sems.at[pair])

    def pack(step, carry):
        span = [SUPPORT_STEP * step + pair for pair in range(SUPPORT_STEP)]
        for pair in span:
            fetch(2 * pair, ids[2 * pair]).wait()
            fetch(2 * pair + 1, ids[2 * pair + 1]).wait()
        packed = []
        for pair in span:
            choice = ids[2 * pair] % 2 + 2 * (ids[2 * pair + 1] % 2)
            both = jnp.concatenate([held[2 * pair], held[2 * pair + 1]], axis=1)
            packed.append(jnp.dot(both, picks[choice], preferred_element_type=jnp.float32).astype(jnp.bfloat16))
        for pair, value in zip(span, packed):
            held[2 * pair] = value
            store(pair).start()
        return carry

    lax.fori_loop(0, pairs // SUPPORT_STEP, pack, 0)

    def drain(pair, carry):
        store(pair).wait()
        return carry

    lax.fori_loop(0, pairs, drain, 0)


def collect_support(scalars, groups, dictionary, pairs, part, *before):
    rows = dictionary.shape[0]
    pairs = pairs // SUPPORT_PARTS
    entries = 2 * pairs
    return pl.pallas_call(
        functools.partial(support_kernel, part * entries, groups),
        grid_spec=pltpu.PrefetchScalarGridSpec(
            num_scalar_prefetch=1,
            grid=(),
            in_specs=[pl.BlockSpec(memory_space=pltpu.HBM)] * (1 + len(before)),
            out_specs=pl.BlockSpec(memory_space=pltpu.HBM),
            scratch_shapes=[
                pltpu.VMEM((entries, rows, LANES), dictionary.dtype),
                pltpu.VMEM((4, 2 * LANES, LANES), jnp.bfloat16),
                pltpu.SMEM((entries,), jnp.int32),
                pltpu.SemaphoreType.DMA((entries,)),
                pltpu.SemaphoreType.DMA((pairs,)),
            ],
        ),
        out_shape=jax.ShapeDtypeStruct((HELD_BYTES // (rows * LANES * 2), rows, LANES), dictionary.dtype),
        compiler_params=pltpu.CompilerParams(vmem_limit_bytes=SUPPORT_VMEM),
        cost_estimate=pl.CostEstimate(flops=0, transcendentals=0, bytes_accessed=6 * pairs * rows * LANES * 2),
        input_output_aliases={2: 0} if before else {},
        name="collect_support",
    )(scalars, dictionary, *before)


def stage_distances(devices):
    return [2**bit for bit in range(devices.bit_length() - 1)]


def last_orders(devices):
    distances = stage_distances(devices)
    return distances, distances[:1] + distances[2:] + distances[1:2]


def slot_distance(slot, distances):
    bits = reversed(range(len(distances)))
    return sum(distance for bit, distance in zip(bits, distances) if slot >> bit & 1)


def gradient_kernel(mode, shards, pairs, groups, scalars, blocks, *refs):
    seq, order, counts, _, me = scalar_parts(scalars, groups)
    refs = list(refs)
    take = lambda: refs.pop(0)
    gathered, targets = [take() for _ in range(4)], take()
    if mode in ("first", "final"):
        thresh = take()
    keep, send = take(), (take(), take())
    if mode == "first":
        start_out, thresh_out = take(), take()
    if mode == "final":
        sent, thresh_out = take(), take()
    held, codes, total = take(), take(), take()
    if mode == "first":
        starts, limits = take(), take()
    offsets, sems = refs

    pieces = pairs // PIECE

    def load(index):
        span = pl.ds(index * PIECE, PIECE)
        return pltpu.make_async_copy(blocks.at[span], held.at[span], sems.at[index])

    for index in range(pieces):
        load(index).start()
    held[pairs:] = jnp.zeros((SPARE,) + held.shape[1:], held.dtype)

    distances = stage_distances(shards)

    def shard_span(slot, size):
        return pl.ds(pl.multiple_of((slot_distance(slot, distances) ^ me) * size, ROW_TILE), size)

    def last_holder(slot):
        even, odd = (slot_distance(slot, order) for order in last_orders(shards))
        if slot >= shards // 2:
            even, odd = odd, even
        return jnp.where(me % 2 == 0, even, odd) ^ me

    quarter = shards // 4
    size_in = gathered[0].shape[0] // quarter
    for slot in range(shards):
        begin = slot % quarter * size_in
        codes[shard_span(slot, size_in), :] = gathered[slot // quarter][begin : begin + size_in, :]

    def put(slot, size, begin, value):
        rows = slice(slot % quarter * size + begin, slot % quarter * size + begin + value.shape[0])
        if slot < 2 * quarter:
            first = slot // quarter * quarter * size
            keep[first + rows.start : first + rows.stop, :] = value
        else:
            send[slot // quarter - 2][rows, :] = value.astype(jnp.bfloat16)

    def seat(index, offset):
        position, _, live = group_at(index, seq, order, counts)
        offsets[position] = offset
        return offset + live

    lax.fori_loop(0, groups, seat, jnp.int32(0))

    upper = upper_half((PATCHES, LANES))
    side = upper.astype(jnp.int32)

    def tile(pair):
        return pl.ds(pl.multiple_of(pair * PATCHES, PATCHES), PATCHES)

    def shifted(parts, count, odd, ahead):
        turned = [swap_halves(part) for part in parts]
        last = len(parts) - 1
        moved = []
        for pair in range(count):
            low, high = (pair, pair + 1) if ahead else (pair - 1, pair)
            low, high = min(max(low, 0), last), min(max(high, 0), last)
            value = jnp.where(upper[: turned[low].shape[0]], turned[high], turned[low])
            moved.append(jnp.where(odd, value, parts[min(pair, last)]))
        return moved

    def read_codes(position, offset, live, count):
        first = offset // 2
        if mode == "first":
            parts = [codes[tile(position * SLOT_PAIRS + pair), :] for pair in range(min(count, SLOT_PAIRS))]
            parts = shifted(parts, count, offset % 2 == 1, False)
        else:
            parts = [codes[tile(first + pair), :] for pair in range(count)]
        masked = []
        for pair, part in enumerate(parts):
            entry = 2 * (first + pair) + side
            mine = (entry >= offset) & (entry < offset + live)
            masked.append(jnp.where(mine, part, jnp.zeros_like(part)))
        return masked

    def write_packed(ref, parts, offset):
        first = offset // 2
        for pair, part in enumerate(parts):
            if pair == 0:
                part = jnp.where(upper | (offset % 2 == 0), part, ref[tile(first), :])
            ref[tile(first + pair), :] = part

    def one_group(position, group, offset, live, count):
        first = offset // 2
        parts = read_codes(position, offset, live, count)
        if mode == "first":
            write_packed(starts, parts, offset)
            write_packed(limits, [thresh[group]] * count, offset)
        matrix = jnp.concatenate([held[first + pair] for pair in range(count)], axis=1)
        point = jnp.concatenate(parts, axis=1)
        residual = lax.dot_general(point, matrix, (((1,), (1,)), ((), ())), preferred_element_type=jnp.float32)
        target = targets[tile(group), :].astype(jnp.float32)
        residual = (residual - target).astype(jnp.bfloat16)
        gradient = jnp.dot(residual, matrix, preferred_element_type=jnp.float32)
        write_packed(total, [gradient[:, pair * LANES : (pair + 1) * LANES] for pair in range(count)], offset)

    def wait_piece(index, carry):
        load(index).wait()
        return carry

    def two_groups(step, waited):
        picks = []
        count_needed = 1
        for index in (2 * step, 2 * step + 1):
            position, group, live = group_at(index, seq, order, counts)
            offset = offsets[position]
            picks.append((position, group, offset, live))
            count_needed = jnp.maximum(count_needed, (live + offset % 2 + 1) // 2)
        reach = jnp.minimum(picks[1][2] // 2 + count_needed - 1, pairs - 1)
        needed = jnp.maximum(reach // PIECE + 1, waited)
        lax.fori_loop(waited, needed, wait_piece, 0)
        for count in range(1, SLOT_PAIRS + 2):

            @pl.when(count_needed == count)
            def _(count=count):
                for pick in picks:
                    one_group(*pick, count)

        return needed

    waited = lax.fori_loop(0, groups // 2, two_groups, jnp.int32(0))
    lax.fori_loop(waited, pieces, wait_piece, 0)

    if mode != "final":
        size = 2 * keep.shape[0] // shards
        for slot in range(shards):
            put(slot, size, 0, total[shard_span(slot, size), :])
    if mode == "first":
        size = start_out.shape[0]
        span = pl.ds(pl.multiple_of(me * size, ROW_TILE), size)
        start_out[...] = starts[span, :]
        thresh_out[...] = limits[span, :]
    if mode == "final":
        offset = offsets[me]
        parts = read_codes(me, offset, counts[order[me]], SLOT_PAIRS + 1)
        for pair, part in enumerate(shifted(parts, SLOT_PAIRS, offset % 2 == 1, True)):
            sent[pair] = part
        thresh_out[...] = thresh[order[me]]
        for slot in range(shards):
            position = last_holder(slot)
            offset = offsets[position]
            live = counts[order[position]]
            parts = [total[tile(offset // 2 + pair), :] for pair in range(SLOT_PAIRS + 1)]
            for pair, part in enumerate(shifted(parts, SLOT_PAIRS, offset % 2 == 1, True)):
                value = jnp.where(2 * pair + side < live, part, 0.0)
                put(slot, SLOT_PAIRS * PATCHES, pair * PATCHES, value)


def gradient_call(mode, shards, pairs, groups, scalars, blocks, gathered, targets, extra=()):
    rows = blocks.shape[1]
    places = pairs + SPARE
    single, double = jnp.bfloat16, jnp.float32
    packed = (places * PATCHES, LANES)
    half_out = (groups * SLOT_PAIRS if mode == "final" else pairs) * PATCHES // 2
    shard = (2 * half_out // shards, LANES)
    outs = [((half_out, LANES), double)] + [((half_out // 2, LANES), single)] * 2
    if mode == "first":
        outs += [(shard, single), (shard, double)]
    if mode == "final":
        outs += [((SLOT_PAIRS, PATCHES, LANES), single), ((PATCHES, LANES), double)]
    codes = groups * SLOT_PAIRS * PATCHES if mode == "first" else packed[0]
    scratch = [((places, rows, LANES), single), ((codes, LANES), single), (packed, double)]
    if mode == "first":
        scratch += [(packed, single), (packed, double)]
    room = sum(math.prod(shape) * jnp.dtype(kind).itemsize for shape, kind in scratch)
    return pl.pallas_call(
        functools.partial(gradient_kernel, mode, shards, pairs, groups),
        grid_spec=pltpu.PrefetchScalarGridSpec(
            num_scalar_prefetch=1,
            grid=(),
            in_specs=[pl.BlockSpec(memory_space=pltpu.HBM)]
            + [pl.BlockSpec(memory_space=pltpu.VMEM)] * (5 + len(extra)),
            out_specs=[pl.BlockSpec(memory_space=pltpu.VMEM)] * len(outs),
            scratch_shapes=[pltpu.VMEM(shape, kind) for shape, kind in scratch]
            + [pltpu.SMEM((groups,), jnp.int32), pltpu.SemaphoreType.DMA((pairs // PIECE,))],
        ),
        out_shape=[jax.ShapeDtypeStruct(shape, kind) for shape, kind in outs],
        compiler_params=pltpu.CompilerParams(vmem_limit_bytes=room + VMEM_MARGIN),
        cost_estimate=pl.CostEstimate(
            flops=4 * pairs * rows * LANES * MATRIX_UNIT, transcendentals=0, bytes_accessed=pairs * rows * LANES * 2
        ),
        name="gradient",
    )(scalars, blocks, *gathered, targets, *extra)


def exchange(value, even, odd=None):
    devices = lax.axis_size("rows")
    apart = (even, even if odd is None else odd)
    return lax.ppermute(value, "rows", [(i, i ^ apart[i % 2]) for i in range(devices)])


def gather_shards(own, beside=()):
    core, row, *columns = stage_distances(lax.axis_size("rows"))
    apart = [slot_distance(slot, columns) for slot in range(lax.axis_size("rows") // 4)]
    made = ()
    near = jnp.concatenate([own] + [exchange(own, distance) for distance in apart[1:]], axis=0)
    if beside:
        near, *made = lax.optimization_barrier((near, beside[0]()))
    other = exchange(near, row)
    far = exchange(near, core)
    if beside:
        other, *made = lax.optimization_barrier((other, beside[1](*made)))
    return (near, other, far, exchange(other, core)), made


def add_cores(keep, *send):
    middle = keep.shape[0] // 2
    arrived = [exchange(part, 1).astype(jnp.float32) for part in send]
    return [part + share for part, share in zip((keep[:middle], keep[middle:]), arrived)]


def reduce_shards(keep, *send):
    devices = lax.axis_size("rows")
    distances = stage_distances(devices)
    quarters = add_cores(keep, *send)
    size = 2 * keep.shape[0] // devices
    sent = [quarter.astype(jnp.bfloat16) for quarter in quarters]
    total = quarters[0][:size]
    for slot in range(1, devices // 2):
        begin = slot % (devices // 4) * size
        share = sent[slot // (devices // 4)][begin : begin + size]
        total = total + exchange(share, slot_distance(slot, distances[1:])).astype(jnp.float32)
    return total


def last_reduce(keep, *send):
    near, other = add_cores(keep, *send)
    for even, odd in list(zip(*last_orders(lax.axis_size("rows"))))[1:]:
        total = near + exchange(other.astype(jnp.bfloat16), even, odd).astype(jnp.float32)
        near, other = total[: total.shape[0] // 2], total[total.shape[0] // 2 :]
    return total


def packed_order(live):
    index = jnp.arange(live.shape[0])
    ahead = (live[None, :] > live[:, None]) | ((live[None, :] == live[:, None]) & (index[None, :] < index[:, None]))
    rank = jnp.sum(ahead.astype(jnp.int32), axis=1)
    return jnp.sum(jnp.where(rank[:, None] == index[None, :], index[:, None], 0), axis=0).astype(jnp.int32)


def shrink(value, thresh):
    return value - jnp.clip(value, -thresh, thresh)


def local(dictionary, patches, initial_codes, support, counts, group_order, penalty):
    groups = group_order.shape[0]
    position = lax.axis_index("rows")
    devices = lax.axis_size("rows")
    momenta = momentum_list()
    pairs = MEAN_LIVE * groups // 2

    laid = initial_codes.reshape(SLOT_PAIRS, 2, PATCHES, BLOCK).transpose(0, 2, 1, 3)
    laid = laid.reshape(SLOT_PAIRS * PATCHES, LANES)
    live = jnp.sum(jnp.where(group_order[:, None] == jnp.arange(groups)[None, :], counts[None, :], 0), axis=1)
    own = position.astype(jnp.int32).reshape(1)
    scalars = jnp.concatenate([packed_order(live), group_order, counts, support.reshape(groups * SLOTS), own])
    collect = functools.partial(collect_support, scalars, groups, dictionary, pairs)
    gathered, (blocks,) = gather_shards(laid, [functools.partial(collect, part) for part in range(SUPPORT_PARTS)])

    targets = patches.T
    half_penalty = 0.5 * penalty
    thresh_tiles = jnp.broadcast_to(half_penalty[:, :, None], (groups, PATCHES, LANES))

    run = functools.partial(
        gradient_call, shards=devices, pairs=pairs, groups=groups, scalars=scalars, blocks=blocks, targets=targets
    )
    *shares, start, thresh = run("first", gathered=gathered, extra=(thresh_tiles,))
    point = previous = start.astype(jnp.float32)
    for turn in range(ITERS - 1):
        if turn:
            shares = run("packed", gathered=gathered)
        current = shrink(point - 0.5 * reduce_shards(*shares), thresh)
        point = current + momenta[turn] * (current - previous)
        previous = current
        gathered, _ = gather_shards(point.astype(jnp.bfloat16))
    *shares, sent, thresh = run("final", gathered=gathered, extra=(thresh_tiles,))
    gradient = last_reduce(*shares).reshape(SLOT_PAIRS, PATCHES, LANES)
    sent = sent.astype(jnp.float32)
    result = shrink(sent - 0.5 * gradient, thresh[None])
    result = result.reshape(SLOT_PAIRS, PATCHES, 2, BLOCK).transpose(0, 2, 1, 3)
    return result.reshape(1, SLOTS, PATCHES * BLOCK)


def solution(mesh):
    in_specs = (
        P("rows", None),
        P("rows", "groups"),
        P(("groups", "rows"), None, None),
        P("groups", None),
        P("groups"),
        P("groups"),
        P("groups", None),
    )
    out_specs = P(("groups", "rows"), None, None)
    return jax.shard_map(local, mesh=mesh, in_specs=in_specs, out_specs=out_specs, check_vma=False)
```

```python
import functools
import math

import jax
import jax.numpy as jnp
from jax import lax
from jax.experimental import pallas as pl
from jax.experimental.pallas import tpu as pltpu
from jax.sharding import PartitionSpec as P

BLOCK = 64
SLOTS = 16
PATCHES = 64
ITERS = 3
MEAN_LIVE = 10
LANES = 2 * BLOCK
SLOT_PAIRS = SLOTS // 2
SPARE = SLOT_PAIRS + 2
ROW_TILE = 16
SUPPORT_PARTS = 2
SUPPORT_STEP = 4
PIECE = 5
MATRIX_UNIT = 256
VMEM_MARGIN = 3 * 1024 * 1024
SUPPORT_VMEM = 40 * 1024 * 1024
HELD_BYTES = 65 * 1024 * 1024


def momentum_list():
    values = []
    tvalue = 1.0
    for turn in range(ITERS):
        tnext = (1.0 + (1.0 + 4.0 * tvalue * tvalue) ** 0.5) / 2.0
        values.append((tvalue - 1.0) / tnext)
        tvalue = tnext
    return values


def swap_halves(value):
    return jnp.concatenate([value[:, BLOCK:], value[:, :BLOCK]], axis=1)


def upper_half(shape):
    return lax.broadcasted_iota(jnp.int32, shape, 1) >= BLOCK


class Part:
    def __init__(self, ref, begin, width=1):
        self.ref, self.begin, self.width = ref, begin, width

    def __getitem__(self, index):
        if isinstance(index, tuple):
            index = index[0] * self.width + index[1]
        return self.ref[self.begin + index]


def scalar_parts(scalars, groups):
    seq, order, counts = (Part(scalars, part * groups) for part in range(3))
    return seq, order, counts, Part(scalars, 3 * groups, SLOTS), scalars[groups * (3 + SLOTS)]


def group_at(index, seq, order, counts):
    position = seq[index]
    group = order[position]
    return position, group, counts[group]


def support_kernel(begin, groups, scalars, dictionary, *refs):
    out, held, picks, ids, sems, out_sems = refs[-6:]
    seq, order, counts, support, _ = scalar_parts(scalars, groups)
    entries, rows, _ = held.shape
    pairs = entries // 2

    def fetch(entry, block):
        start = pl.multiple_of((block // 2) * LANES, LANES)
        return pltpu.make_async_copy(dictionary.at[:, pl.ds(start, LANES)], held.at[entry], sems.at[entry])

    def start_group(index, offset):
        _, group, live = group_at(index, seq, order, counts)

        def start_slot(slot, carry):
            block = support[group, slot]
            ids[offset + slot] = block
            fetch(offset + slot, block).start()
            return carry

        lax.fori_loop(jnp.clip(-offset, 0, live), jnp.clip(entries - offset, 0, live), start_slot, 0)
        return offset + live

    lax.fori_loop(0, groups, start_group, jnp.int32(-begin))
    shape = (2 * LANES, LANES)
    source = lax.broadcasted_iota(jnp.int32, shape, 0)
    target = lax.broadcasted_iota(jnp.int32, shape, 1)
    for choice in range(4):
        wanted = jnp.where(target < BLOCK, (choice % 2) * BLOCK + target, LANES + (choice // 2) * BLOCK + target - BLOCK)
        picks[choice] = (source == wanted).astype(jnp.float32).astype(jnp.bfloat16)

    def store(pair):
        return pltpu.make_async_copy(held.at[2 * pair], out.at[begin // 2 + pair], out_sems.at[pair])

    def pack(step, carry):
        span = [SUPPORT_STEP * step + pair for pair in range(SUPPORT_STEP)]
        for pair in span:
            fetch(2 * pair, ids[2 * pair]).wait()
            fetch(2 * pair + 1, ids[2 * pair + 1]).wait()
        packed = []
        for pair in span:
            choice = ids[2 * pair] % 2 + 2 * (ids[2 * pair + 1] % 2)
            both = jnp.concatenate([held[2 * pair], held[2 * pair + 1]], axis=1)
            packed.append(jnp.dot(both, picks[choice], preferred_element_type=jnp.float32).astype(jnp.bfloat16))
        for pair, value in zip(span, packed):
            held[2 * pair] = value
            store(pair).start()
        return carry

    lax.fori_loop(0, pairs // SUPPORT_STEP, pack, 0)

    def drain(pair, carry):
        store(pair).wait()
        return carry

    lax.fori_loop(0, pairs, drain, 0)


def collect_support(scalars, groups, dictionary, pairs, part, *before):
    rows = dictionary.shape[0]
    pairs = pairs // SUPPORT_PARTS
    entries = 2 * pairs
    return pl.pallas_call(
        functools.partial(support_kernel, part * entries, groups),
        grid_spec=pltpu.PrefetchScalarGridSpec(
            num_scalar_prefetch=1,
            grid=(),
            in_specs=[pl.BlockSpec(memory_space=pltpu.HBM)] * (1 + len(before)),
            out_specs=pl.BlockSpec(memory_space=pltpu.HBM),
            scratch_shapes=[
                pltpu.VMEM((entries, rows, LANES), dictionary.dtype),
                pltpu.VMEM((4, 2 * LANES, LANES), jnp.bfloat16),
                pltpu.SMEM((entries,), jnp.int32),
                pltpu.SemaphoreType.DMA((entries,)),
                pltpu.SemaphoreType.DMA((pairs,)),
            ],
        ),
        out_shape=jax.ShapeDtypeStruct((HELD_BYTES // (rows * LANES * 2), rows, LANES), dictionary.dtype),
        compiler_params=pltpu.CompilerParams(vmem_limit_bytes=SUPPORT_VMEM),
        cost_estimate=pl.CostEstimate(flops=0, transcendentals=0, bytes_accessed=6 * pairs * rows * LANES * 2),
        input_output_aliases={2: 0} if before else {},
        name="collect_support",
    )(scalars, dictionary, *before)


def stage_distances(devices):
    return [2**bit for bit in range(devices.bit_length() - 1)]


def last_orders(devices):
    distances = stage_distances(devices)
    return distances, distances[:1] + distances[2:] + distances[1:2]


def slot_distance(slot, distances):
    bits = reversed(range(len(distances)))
    return sum(distance for bit, distance in zip(bits, distances) if slot >> bit & 1)


def gradient_kernel(mode, shards, pairs, groups, scalars, blocks, *refs):
    seq, order, counts, _, me = scalar_parts(scalars, groups)
    refs = list(refs)
    take = lambda: refs.pop(0)
    gathered, targets = [take() for _ in range(4)], take()
    if mode in ("first", "final"):
        thresh = take()
    keep, send = take(), (take(), take())
    if mode == "first":
        start_out, thresh_out = take(), take()
    if mode == "final":
        sent, thresh_out = take(), take()
    held, codes, total = take(), take(), take()
    if mode == "first":
        starts, limits = take(), take()
    offsets, sems = refs

    pieces = pairs // PIECE

    def load(index):
        span = pl.ds(index * PIECE, PIECE)
        return pltpu.make_async_copy(blocks.at[span], held.at[span], sems.at[index])

    for index in range(pieces):
        load(index).start()
    held[pairs:] = jnp.zeros((SPARE,) + held.shape[1:], held.dtype)

    distances = stage_distances(shards)

    def shard_span(slot, size):
        return pl.ds(pl.multiple_of((slot_distance(slot, distances) ^ me) * size, ROW_TILE), size)

    def last_holder(slot):
        even, odd = (slot_distance(slot, order) for order in last_orders(shards))
        if slot >= shards // 2:
            even, odd = odd, even
        return jnp.where(me % 2 == 0, even, odd) ^ me

    quarter = shards // 4
    size_in = gathered[0].shape[0] // (quarter + 1)
    for slot in range(shards):
        half, inside = divmod(slot, 2 * quarter)
        second = inside > quarter
        begin = (inside - (quarter + 1) * second) * size_in
        codes[shard_span(slot, size_in), :] = gathered[2 * half + second][begin : begin + size_in, :]

    def put(slot, size, begin, value):
        rows = slice(slot % quarter * size + begin, slot % quarter * size + begin + value.shape[0])
        if slot < 2 * quarter:
            first = slot // quarter * quarter * size
            keep[first + rows.start : first + rows.stop, :] = value
        else:
            send[slot // quarter - 2][rows, :] = value.astype(jnp.bfloat16)

    def seat(index, offset):
        position, _, live = group_at(index, seq, order, counts)
        offsets[position] = offset
        return offset + live

    lax.fori_loop(0, groups, seat, jnp.int32(0))

    upper = upper_half((PATCHES, LANES))
    side = upper.astype(jnp.int32)

    def tile(pair):
        return pl.ds(pl.multiple_of(pair * PATCHES, PATCHES), PATCHES)

    def shifted(parts, count, odd, ahead):
        turned = [swap_halves(part) for part in parts]
        last = len(parts) - 1
        moved = []
        for pair in range(count):
            low, high = (pair, pair + 1) if ahead else (pair - 1, pair)
            low, high = min(max(low, 0), last), min(max(high, 0), last)
            value = jnp.where(upper[: turned[low].shape[0]], turned[high], turned[low])
            moved.append(jnp.where(odd, value, parts[min(pair, last)]))
        return moved

    def read_codes(position, offset, live, count):
        first = offset // 2
        if mode == "first":
            parts = [codes[tile(position * SLOT_PAIRS + pair), :] for pair in range(min(count, SLOT_PAIRS))]
            parts = shifted(parts, count, offset % 2 == 1, False)
        else:
            parts = [codes[tile(first + pair), :] for pair in range(count)]
        masked = []
        for pair, part in enumerate(parts):
            entry = 2 * (first + pair) + side
            mine = (entry >= offset) & (entry < offset + live)
            masked.append(jnp.where(mine, part, jnp.zeros_like(part)))
        return masked

    def write_packed(ref, parts, offset):
        first = offset // 2
        for pair, part in enumerate(parts):
            if pair == 0:
                part = jnp.where(upper | (offset % 2 == 0), part, ref[tile(first), :])
            ref[tile(first + pair), :] = part

    def one_group(position, group, offset, live, count):
        first = offset // 2
        parts = read_codes(position, offset, live, count)
        if mode == "first":
            write_packed(starts, parts, offset)
            write_packed(limits, [thresh[group]] * count, offset)
        matrix = jnp.concatenate([held[first + pair] for pair in range(count)], axis=1)
        point = jnp.concatenate(parts, axis=1)
        residual = lax.dot_general(matrix, point, (((1,), (1,)), ((), ())), preferred_element_type=jnp.float32).T
        target = targets[tile(group), :].astype(jnp.float32)
        residual = (residual - target).astype(jnp.bfloat16)
        gradient = jnp.dot(residual, matrix, preferred_element_type=jnp.float32)
        write_packed(total, [gradient[:, pair * LANES : (pair + 1) * LANES] for pair in range(count)], offset)

    def wait_piece(index, carry):
        load(index).wait()
        return carry

    def two_groups(step, waited):
        picks = []
        count_needed = 1
        for index in (2 * step, 2 * step + 1):
            position, group, live = group_at(index, seq, order, counts)
            offset = offsets[position]
            picks.append((position, group, offset, live))
            count_needed = jnp.maximum(count_needed, (live + offset % 2 + 1) // 2)
        reach = jnp.minimum(picks[1][2] // 2 + count_needed - 1, pairs - 1)
        needed = jnp.maximum(reach // PIECE + 1, waited)
        lax.fori_loop(waited, needed, wait_piece, 0)
        for count in range(1, SLOT_PAIRS + 2):

            @pl.when(count_needed == count)
            def _(count=count):
                for pick in picks:
                    one_group(*pick, count)

        return needed

    waited = lax.fori_loop(0, groups // 2, two_groups, jnp.int32(0))
    lax.fori_loop(waited, pieces, wait_piece, 0)

    if mode != "final":
        size = 2 * keep.shape[0] // shards
        for slot in range(shards):
            put(slot, size, 0, total[shard_span(slot, size), :])
    if mode == "first":
        size = start_out.shape[0]
        span = pl.ds(pl.multiple_of(me * size, ROW_TILE), size)
        start_out[...] = starts[span, :]
        thresh_out[...] = limits[span, :]
    if mode == "final":
        offset = offsets[me]
        parts = read_codes(me, offset, counts[order[me]], SLOT_PAIRS + 1)
        for pair, part in enumerate(shifted(parts, SLOT_PAIRS, offset % 2 == 1, True)):
            sent[pair] = part
        thresh_out[...] = thresh[order[me]]
        for slot in range(shards):
            position = last_holder(slot)
            offset = offsets[position]
            live = counts[order[position]]
            parts = [total[tile(offset // 2 + pair), :] for pair in range(SLOT_PAIRS + 1)]
            for pair, part in enumerate(shifted(parts, SLOT_PAIRS, offset % 2 == 1, True)):
                value = jnp.where(2 * pair + side < live, part, 0.0)
                put(slot, SLOT_PAIRS * PATCHES, pair * PATCHES, value)


def gradient_call(mode, shards, pairs, groups, scalars, blocks, gathered, targets, extra=()):
    rows = blocks.shape[1]
    places = pairs + SPARE
    single, double = jnp.bfloat16, jnp.float32
    packed = (places * PATCHES, LANES)
    half_out = (groups * SLOT_PAIRS if mode == "final" else pairs) * PATCHES // 2
    shard = (2 * half_out // shards, LANES)
    outs = [((half_out, LANES), double)] + [((half_out // 2, LANES), single)] * 2
    if mode == "first":
        outs += [(shard, single), (shard, double)]
    if mode == "final":
        outs += [((SLOT_PAIRS, PATCHES, LANES), single), ((PATCHES, LANES), double)]
    codes = groups * SLOT_PAIRS * PATCHES if mode == "first" else packed[0]
    scratch = [((places, rows, LANES), single), ((codes, LANES), single), (packed, double)]
    if mode == "first":
        scratch += [(packed, single), (packed, double)]
    room = sum(math.prod(shape) * jnp.dtype(kind).itemsize for shape, kind in scratch)
    return pl.pallas_call(
        functools.partial(gradient_kernel, mode, shards, pairs, groups),
        grid_spec=pltpu.PrefetchScalarGridSpec(
            num_scalar_prefetch=1,
            grid=(),
            in_specs=[pl.BlockSpec(memory_space=pltpu.HBM)]
            + [pl.BlockSpec(memory_space=pltpu.VMEM)] * (5 + len(extra)),
            out_specs=[pl.BlockSpec(memory_space=pltpu.VMEM)] * len(outs),
            scratch_shapes=[pltpu.VMEM(shape, kind) for shape, kind in scratch]
            + [pltpu.SMEM((groups,), jnp.int32), pltpu.SemaphoreType.DMA((pairs // PIECE,))],
        ),
        out_shape=[jax.ShapeDtypeStruct(shape, kind) for shape, kind in outs],
        compiler_params=pltpu.CompilerParams(vmem_limit_bytes=room + VMEM_MARGIN),
        cost_estimate=pl.CostEstimate(
            flops=4 * pairs * rows * LANES * MATRIX_UNIT, transcendentals=0, bytes_accessed=pairs * rows * LANES * 2
        ),
        name="gradient",
    )(scalars, blocks, *gathered, targets, *extra)


def exchange(value, even, odd=None):
    devices = lax.axis_size("rows")
    apart = (even, even if odd is None else odd)
    return lax.ppermute(value, "rows", [(i, i ^ apart[i % 2]) for i in range(devices)])


def gather_shards(own, beside=()):
    core, row, *columns = stage_distances(lax.axis_size("rows"))
    apart = [slot_distance(slot, columns) for slot in range(lax.axis_size("rows") // 4)]
    made = ()
    near = jnp.concatenate([own] + [exchange(own, distance) for distance in apart[1:] + [row]], axis=0)
    if beside:
        near, *made = lax.optimization_barrier((near, beside[0]()))
    other = exchange(near[own.shape[0] : len(apart) * own.shape[0]], row)
    far = exchange(near, core)
    if beside:
        other, *made = lax.optimization_barrier((other, beside[1](*made)))
    return (near, other, far, exchange(other, core)), made


def add_cores(keep, *send):
    middle = keep.shape[0] // 2
    arrived = [exchange(part, 1).astype(jnp.float32) for part in send]
    return [part + share for part, share in zip((keep[:middle], keep[middle:]), arrived)]


def reduce_shards(keep, *send):
    devices = lax.axis_size("rows")
    distances = stage_distances(devices)
    quarters = add_cores(keep, *send)
    size = 2 * keep.shape[0] // devices
    sent = [quarter.astype(jnp.bfloat16) for quarter in quarters]
    total = quarters[0][:size]
    for slot in range(1, devices // 2):
        begin = slot % (devices // 4) * size
        share = sent[slot // (devices // 4)][begin : begin + size]
        total = total + exchange(share, slot_distance(slot, distances[1:])).astype(jnp.float32)
    return total


def last_reduce(keep, *send):
    near, other = add_cores(keep, *send)
    for even, odd in list(zip(*last_orders(lax.axis_size("rows"))))[1:]:
        total = near + exchange(other.astype(jnp.bfloat16), even, odd).astype(jnp.float32)
        near, other = total[: total.shape[0] // 2], total[total.shape[0] // 2 :]
    return total


def packed_order(live):
    index = jnp.arange(live.shape[0])
    ahead = (live[None, :] > live[:, None]) | ((live[None, :] == live[:, None]) & (index[None, :] < index[:, None]))
    rank = jnp.sum(ahead.astype(jnp.int32), axis=1)
    return jnp.sum(jnp.where(rank[:, None] == index[None, :], index[:, None], 0), axis=0).astype(jnp.int32)


def shrink(value, thresh):
    return value - jnp.clip(value, -thresh, thresh)


def local(dictionary, patches, initial_codes, support, counts, group_order, penalty):
    groups = group_order.shape[0]
    position = lax.axis_index("rows")
    devices = lax.axis_size("rows")
    momenta = momentum_list()
    pairs = MEAN_LIVE * groups // 2

    laid = initial_codes.reshape(SLOT_PAIRS, 2, PATCHES, BLOCK).transpose(0, 2, 1, 3)
    laid = laid.reshape(SLOT_PAIRS * PATCHES, LANES)
    live = jnp.sum(jnp.where(group_order[:, None] == jnp.arange(groups)[None, :], counts[None, :], 0), axis=1)
    own = position.astype(jnp.int32).reshape(1)
    scalars = jnp.concatenate([packed_order(live), group_order, counts, support.reshape(groups * SLOTS), own])
    collect = functools.partial(collect_support, scalars, groups, dictionary, pairs)
    gathered, (blocks,) = gather_shards(laid, [functools.partial(collect, part) for part in range(SUPPORT_PARTS)])

    targets = patches.T
    half_penalty = 0.5 * penalty
    thresh_tiles = jnp.broadcast_to(half_penalty[:, :, None], (groups, PATCHES, LANES))

    run = functools.partial(
        gradient_call, shards=devices, pairs=pairs, groups=groups, scalars=scalars, blocks=blocks, targets=targets
    )
    *shares, start, thresh = run("first", gathered=gathered, extra=(thresh_tiles,))
    point = previous = start.astype(jnp.float32)
    for turn in range(ITERS - 1):
        if turn:
            shares = run("packed", gathered=gathered)
        current = shrink(point - 0.5 * reduce_shards(*shares), thresh)
        point = current + momenta[turn] * (current - previous)
        previous = current
        gathered, _ = gather_shards(point.astype(jnp.bfloat16))
    *shares, sent, thresh = run("final", gathered=gathered, extra=(thresh_tiles,))
    gradient = last_reduce(*shares).reshape(SLOT_PAIRS, PATCHES, LANES)
    sent = sent.astype(jnp.float32)
    result = shrink(sent - 0.5 * gradient, thresh[None])
    result = result.reshape(SLOT_PAIRS, PATCHES, 2, BLOCK).transpose(0, 2, 1, 3)
    return result.reshape(1, SLOTS, PATCHES * BLOCK)


def solution(mesh):
    in_specs = (
        P("rows", None),
        P("rows", "groups"),
        P(("groups", "rows"), None, None),
        P("groups", None),
        P("groups"),
        P("groups"),
        P("groups", None),
    )
    out_specs = P(("groups", "rows"), None, None)
    return jax.shard_map(local, mesh=mesh, in_specs=in_specs, out_specs=out_specs, check_vma=False)
```

```python
import functools
import math

import jax
import jax.numpy as jnp
from jax import lax
from jax.experimental import pallas as pl
from jax.experimental.pallas import tpu as pltpu
from jax.sharding import PartitionSpec as P

BLOCK = 64
SLOTS = 16
PATCHES = 64
ITERS = 3
MEAN_LIVE = 10
LANES = 2 * BLOCK
SLOT_PAIRS = SLOTS // 2
SPARE = SLOT_PAIRS + 2
ROW_TILE = 16
SUPPORT_PARTS = 2
SUPPORT_STEP = 4
SUPPORT_AHEAD = 3
PIECE = 5
MATRIX_UNIT = 256
VMEM_MARGIN = 3 * 1024 * 1024
SUPPORT_VMEM = 40 * 1024 * 1024
HELD_BYTES = 65 * 1024 * 1024


def momentum_list():
    values = []
    tvalue = 1.0
    for turn in range(ITERS):
        tnext = (1.0 + (1.0 + 4.0 * tvalue * tvalue) ** 0.5) / 2.0
        values.append((tvalue - 1.0) / tnext)
        tvalue = tnext
    return values


def swap_halves(value):
    return jnp.concatenate([value[:, BLOCK:], value[:, :BLOCK]], axis=1)


def upper_half(shape):
    return lax.broadcasted_iota(jnp.int32, shape, 1) >= BLOCK


class Part:
    def __init__(self, ref, begin, width=1):
        self.ref, self.begin, self.width = ref, begin, width

    def __getitem__(self, index):
        if isinstance(index, tuple):
            index = index[0] * self.width + index[1]
        return self.ref[self.begin + index]


def scalar_parts(scalars, groups):
    seq, order, counts = (Part(scalars, part * groups) for part in range(3))
    return seq, order, counts, Part(scalars, 3 * groups, SLOTS), scalars[groups * (3 + SLOTS)]


def group_at(index, seq, order, counts):
    position = seq[index]
    group = order[position]
    return position, group, counts[group]


def support_kernel(begin, groups, scalars, dictionary, *refs):
    out, held, picks, ids, sems, out_sems = refs[-6:]
    seq, order, counts, support, _ = scalar_parts(scalars, groups)
    entries, rows, _ = held.shape
    pairs = entries // 2

    def fetch(entry, block):
        start = pl.multiple_of((block // 2) * LANES, LANES)
        return pltpu.make_async_copy(dictionary.at[:, pl.ds(start, LANES)], held.at[entry], sems.at[entry])

    def start_group(index, offset):
        _, group, live = group_at(index, seq, order, counts)

        def start_slot(slot, carry):
            ids[offset + slot] = support[group, slot]
            return carry

        lax.fori_loop(jnp.clip(-offset, 0, live), jnp.clip(entries - offset, 0, live), start_slot, 0)
        return offset + live

    lax.fori_loop(0, groups, start_group, jnp.int32(-begin))
    steps = pairs // SUPPORT_STEP

    def start_step(step):
        for entry in range(2 * SUPPORT_STEP):
            index = 2 * SUPPORT_STEP * step + entry
            fetch(index, ids[index]).start()

    for step in range(min(SUPPORT_AHEAD, steps)):
        start_step(step)
    shape = (2 * LANES, LANES)
    source = lax.broadcasted_iota(jnp.int32, shape, 0)
    target = lax.broadcasted_iota(jnp.int32, shape, 1)
    for choice in range(4):
        wanted = jnp.where(target < BLOCK, (choice % 2) * BLOCK + target, LANES + (choice // 2) * BLOCK + target - BLOCK)
        picks[choice] = (source == wanted).astype(jnp.float32).astype(jnp.bfloat16)

    def store(pair):
        return pltpu.make_async_copy(held.at[2 * pair], out.at[begin // 2 + pair], out_sems.at[pair])

    def pack(step, carry):
        @pl.when(step + SUPPORT_AHEAD < steps)
        def _():
            start_step(step + SUPPORT_AHEAD)

        span = [SUPPORT_STEP * step + pair for pair in range(SUPPORT_STEP)]
        for pair in span:
            fetch(2 * pair, ids[2 * pair]).wait()
            fetch(2 * pair + 1, ids[2 * pair + 1]).wait()
        packed = []
        for pair in span:
            choice = ids[2 * pair] % 2 + 2 * (ids[2 * pair + 1] % 2)
            both = jnp.concatenate([held[2 * pair], held[2 * pair + 1]], axis=1)
            packed.append(jnp.dot(both, picks[choice], preferred_element_type=jnp.float32).astype(jnp.bfloat16))
        for pair, value in zip(span, packed):
            held[2 * pair] = value
            store(pair).start()
        return carry

    lax.fori_loop(0, steps, pack, 0)

    def drain(pair, carry):
        store(pair).wait()
        return carry

    lax.fori_loop(0, pairs, drain, 0)


def collect_support(scalars, groups, dictionary, pairs, part, *before):
    rows = dictionary.shape[0]
    pairs = pairs // SUPPORT_PARTS
    entries = 2 * pairs
    return pl.pallas_call(
        functools.partial(support_kernel, part * entries, groups),
        grid_spec=pltpu.PrefetchScalarGridSpec(
            num_scalar_prefetch=1,
            grid=(),
            in_specs=[pl.BlockSpec(memory_space=pltpu.HBM)] * (1 + len(before)),
            out_specs=pl.BlockSpec(memory_space=pltpu.HBM),
            scratch_shapes=[
                pltpu.VMEM((entries, rows, LANES), dictionary.dtype),
                pltpu.VMEM((4, 2 * LANES, LANES), jnp.bfloat16),
                pltpu.SMEM((entries,), jnp.int32),
                pltpu.SemaphoreType.DMA((entries,)),
                pltpu.SemaphoreType.DMA((pairs,)),
            ],
        ),
        out_shape=jax.ShapeDtypeStruct((HELD_BYTES // (rows * LANES * 2), rows, LANES), dictionary.dtype),
        compiler_params=pltpu.CompilerParams(vmem_limit_bytes=SUPPORT_VMEM),
        cost_estimate=pl.CostEstimate(flops=0, transcendentals=0, bytes_accessed=6 * pairs * rows * LANES * 2),
        input_output_aliases={2: 0} if before else {},
        name="collect_support",
    )(scalars, dictionary, *before)


def stage_distances(devices):
    return [2**bit for bit in range(devices.bit_length() - 1)]


def last_orders(devices):
    distances = stage_distances(devices)
    return distances, distances[:1] + distances[2:] + distances[1:2]


def slot_distance(slot, distances):
    bits = reversed(range(len(distances)))
    return sum(distance for bit, distance in zip(bits, distances) if slot >> bit & 1)


def gradient_kernel(mode, shards, pairs, groups, scalars, blocks, *refs):
    seq, order, counts, _, me = scalar_parts(scalars, groups)
    refs = list(refs)
    take = lambda: refs.pop(0)
    gathered, targets = [take() for _ in range(4)], take()
    if mode in ("first", "final"):
        thresh = take()
    keep, send = take(), (take(), take())
    if mode == "first":
        start_out, thresh_out = take(), take()
    if mode == "final":
        sent, thresh_out = take(), take()
    held, codes, total = take(), take(), take()
    if mode == "first":
        starts, limits = take(), take()
    offsets, sems = refs

    pieces = pairs // PIECE

    def load(index):
        span = pl.ds(index * PIECE, PIECE)
        return pltpu.make_async_copy(blocks.at[span], held.at[span], sems.at[index])

    for index in range(pieces):
        load(index).start()
    held[pairs:] = jnp.zeros((SPARE,) + held.shape[1:], held.dtype)

    distances = stage_distances(shards)

    def shard_span(slot, size):
        return pl.ds(pl.multiple_of((slot_distance(slot, distances) ^ me) * size, ROW_TILE), size)

    def last_holder(slot):
        even, odd = (slot_distance(slot, order) for order in last_orders(shards))
        if slot >= shards // 2:
            even, odd = odd, even
        return jnp.where(me % 2 == 0, even, odd) ^ me

    quarter = shards // 4
    size_in = gathered[0].shape[0] // (quarter + 1)
    for slot in range(shards):
        half, inside = divmod(slot, 2 * quarter)
        second = inside > quarter
        begin = (inside - (quarter + 1) * second) * size_in
        codes[shard_span(slot, size_in), :] = gathered[2 * half + second][begin : begin + size_in, :]

    def put(slot, size, begin, value):
        rows = slice(slot % quarter * size + begin, slot % quarter * size + begin + value.shape[0])
        if slot < 2 * quarter:
            first = slot // quarter * quarter * size
            keep[first + rows.start : first + rows.stop, :] = value
        else:
            send[slot // quarter - 2][rows, :] = value.astype(jnp.bfloat16)

    def seat(index, offset):
        position, _, live = group_at(index, seq, order, counts)
        offsets[position] = offset
        return offset + live

    lax.fori_loop(0, groups, seat, jnp.int32(0))

    upper = upper_half((PATCHES, LANES))
    side = upper.astype(jnp.int32)

    def tile(pair):
        return pl.ds(pl.multiple_of(pair * PATCHES, PATCHES), PATCHES)

    def shifted(parts, count, odd, ahead):
        turned = [swap_halves(part) for part in parts]
        last = len(parts) - 1
        moved = []
        for pair in range(count):
            low, high = (pair, pair + 1) if ahead else (pair - 1, pair)
            low, high = min(max(low, 0), last), min(max(high, 0), last)
            value = jnp.where(upper[: turned[low].shape[0]], turned[high], turned[low])
            moved.append(jnp.where(odd, value, parts[min(pair, last)]))
        return moved

    def read_codes(position, offset, live, count):
        first = offset // 2
        if mode == "first":
            parts = [codes[tile(position * SLOT_PAIRS + pair), :] for pair in range(min(count, SLOT_PAIRS))]
            parts = shifted(parts, count, offset % 2 == 1, False)
        else:
            parts = [codes[tile(first + pair), :] for pair in range(count)]
        masked = []
        for pair, part in enumerate(parts):
            entry = 2 * (first + pair) + side
            mine = (entry >= offset) & (entry < offset + live)
            masked.append(jnp.where(mine, part, jnp.zeros_like(part)))
        return masked

    def write_packed(ref, parts, offset):
        first = offset // 2
        for pair, part in enumerate(parts):
            if pair == 0:
                part = jnp.where(upper | (offset % 2 == 0), part, ref[tile(first), :])
            ref[tile(first + pair), :] = part

    def one_group(position, group, offset, live, count):
        first = offset // 2
        parts = read_codes(position, offset, live, count)
        if mode == "first":
            write_packed(starts, parts, offset)
            write_packed(limits, [thresh[group]] * count, offset)
        matrix = jnp.concatenate([held[first + pair] for pair in range(count)], axis=1)
        point = jnp.concatenate(parts, axis=1)
        residual = lax.dot_general(point, matrix, (((1,), (1,)), ((), ())), preferred_element_type=jnp.float32)
        target = targets[tile(group), :].astype(jnp.float32)
        residual = (residual - target).astype(jnp.bfloat16)
        gradient = jnp.dot(residual, matrix, preferred_element_type=jnp.float32)
        write_packed(total, [gradient[:, pair * LANES : (pair + 1) * LANES] for pair in range(count)], offset)

    def wait_piece(index, carry):
        load(index).wait()
        return carry

    def two_groups(step, waited):
        picks = []
        count_needed = 1
        for index in (2 * step, 2 * step + 1):
            position, group, live = group_at(index, seq, order, counts)
            offset = offsets[position]
            picks.append((position, group, offset, live))
            count_needed = jnp.maximum(count_needed, (live + offset % 2 + 1) // 2)
        reach = jnp.minimum(picks[1][2] // 2 + count_needed - 1, pairs - 1)
        needed = jnp.maximum(reach // PIECE + 1, waited)
        lax.fori_loop(waited, needed, wait_piece, 0)
        for count in range(1, SLOT_PAIRS + 2):

            @pl.when(count_needed == count)
            def _(count=count):
                for pick in picks:
                    one_group(*pick, count)

        return needed

    waited = lax.fori_loop(0, groups // 2, two_groups, jnp.int32(0))
    lax.fori_loop(waited, pieces, wait_piece, 0)

    if mode != "final":
        size = 2 * keep.shape[0] // shards
        for slot in range(shards):
            put(slot, size, 0, total[shard_span(slot, size), :])
    if mode == "first":
        size = start_out.shape[0]
        span = pl.ds(pl.multiple_of(me * size, ROW_TILE), size)
        start_out[...] = starts[span, :]
        thresh_out[...] = limits[span, :]
    if mode == "final":
        offset = offsets[me]
        parts = read_codes(me, offset, counts[order[me]], SLOT_PAIRS + 1)
        for pair, part in enumerate(shifted(parts, SLOT_PAIRS, offset % 2 == 1, True)):
            sent[pair] = part
        thresh_out[...] = thresh[order[me]]
        for slot in range(shards):
            position = last_holder(slot)
            offset = offsets[position]
            live = counts[order[position]]
            parts = [total[tile(offset // 2 + pair), :] for pair in range(SLOT_PAIRS + 1)]
            for pair, part in enumerate(shifted(parts, SLOT_PAIRS, offset % 2 == 1, True)):
                value = jnp.where(2 * pair + side < live, part, 0.0)
                put(slot, SLOT_PAIRS * PATCHES, pair * PATCHES, value)


def gradient_call(mode, shards, pairs, groups, scalars, blocks, gathered, targets, extra=()):
    rows = blocks.shape[1]
    places = pairs + SPARE
    single, double = jnp.bfloat16, jnp.float32
    packed = (places * PATCHES, LANES)
    half_out = (groups * SLOT_PAIRS if mode == "final" else pairs) * PATCHES // 2
    shard = (2 * half_out // shards, LANES)
    outs = [((half_out, LANES), double)] + [((half_out // 2, LANES), single)] * 2
    if mode == "first":
        outs += [(shard, single), (shard, double)]
    if mode == "final":
        outs += [((SLOT_PAIRS, PATCHES, LANES), single), ((PATCHES, LANES), double)]
    codes = groups * SLOT_PAIRS * PATCHES if mode == "first" else packed[0]
    scratch = [((places, rows, LANES), single), ((codes, LANES), single), (packed, double)]
    if mode == "first":
        scratch += [(packed, single), (packed, double)]
    room = sum(math.prod(shape) * jnp.dtype(kind).itemsize for shape, kind in scratch)
    return pl.pallas_call(
        functools.partial(gradient_kernel, mode, shards, pairs, groups),
        grid_spec=pltpu.PrefetchScalarGridSpec(
            num_scalar_prefetch=1,
            grid=(),
            in_specs=[pl.BlockSpec(memory_space=pltpu.HBM)]
            + [pl.BlockSpec(memory_space=pltpu.VMEM)] * (5 + len(extra)),
            out_specs=[pl.BlockSpec(memory_space=pltpu.VMEM)] * len(outs),
            scratch_shapes=[pltpu.VMEM(shape, kind) for shape, kind in scratch]
            + [pltpu.SMEM((groups,), jnp.int32), pltpu.SemaphoreType.DMA((pairs // PIECE,))],
        ),
        out_shape=[jax.ShapeDtypeStruct(shape, kind) for shape, kind in outs],
        compiler_params=pltpu.CompilerParams(vmem_limit_bytes=room + VMEM_MARGIN),
        cost_estimate=pl.CostEstimate(
            flops=4 * pairs * rows * LANES * MATRIX_UNIT, transcendentals=0, bytes_accessed=pairs * rows * LANES * 2
        ),
        name="gradient",
    )(scalars, blocks, *gathered, targets, *extra)


def exchange(value, even, odd=None):
    devices = lax.axis_size("rows")
    apart = (even, even if odd is None else odd)
    return lax.ppermute(value, "rows", [(i, i ^ apart[i % 2]) for i in range(devices)])


def gather_shards(own, beside=()):
    core, row, *columns = stage_distances(lax.axis_size("rows"))
    apart = [slot_distance(slot, columns) for slot in range(lax.axis_size("rows") // 4)]
    made = ()
    near = jnp.concatenate([own] + [exchange(own, distance) for distance in apart[1:] + [row]], axis=0)
    if beside:
        near, *made = lax.optimization_barrier((near, beside[0]()))
    other = exchange(near[own.shape[0] : len(apart) * own.shape[0]], row)
    far = exchange(near, core)
    if beside:
        other, *made = lax.optimization_barrier((other, beside[1](*made)))
    return (near, other, far, exchange(other, core)), made


def add_cores(keep, *send):
    middle = keep.shape[0] // 2
    arrived = [exchange(part, 1).astype(jnp.float32) for part in send]
    return [part + share for part, share in zip((keep[:middle], keep[middle:]), arrived)]


def reduce_shards(keep, *send):
    devices = lax.axis_size("rows")
    _, row, *columns = stage_distances(devices)
    near, other = add_cores(keep, *send)
    size = near.shape[0] // (devices // 4)
    sums = near[size:] + exchange(other[size:].astype(jnp.bfloat16), row).astype(jnp.float32)
    last, sums = lax.optimization_barrier((other[:size].astype(jnp.bfloat16), sums.astype(jnp.bfloat16)))
    total = near[:size] + exchange(last, row).astype(jnp.float32)
    for slot in range(1, devices // 4):
        share = exchange(sums[(slot - 1) * size : slot * size], slot_distance(slot, columns))
        total = total + share.astype(jnp.float32)
    return total


def last_reduce(keep, *send):
    near, other = add_cores(keep, *send)
    for even, odd in list(zip(*last_orders(lax.axis_size("rows"))))[1:]:
        total = near + exchange(other.astype(jnp.bfloat16), even, odd).astype(jnp.float32)
        near, other = total[: total.shape[0] // 2], total[total.shape[0] // 2 :]
    return total


def packed_order(live):
    index = jnp.arange(live.shape[0])
    ahead = (live[None, :] > live[:, None]) | ((live[None, :] == live[:, None]) & (index[None, :] < index[:, None]))
    rank = jnp.sum(ahead.astype(jnp.int32), axis=1)
    return jnp.sum(jnp.where(rank[:, None] == index[None, :], index[:, None], 0), axis=0).astype(jnp.int32)


def shrink(value, thresh):
    return value - jnp.clip(value, -thresh, thresh)


def local(dictionary, patches, initial_codes, support, counts, group_order, penalty):
    groups = group_order.shape[0]
    position = lax.axis_index("rows")
    devices = lax.axis_size("rows")
    momenta = momentum_list()
    pairs = MEAN_LIVE * groups // 2

    laid = initial_codes.reshape(SLOT_PAIRS, 2, PATCHES, BLOCK).transpose(0, 2, 1, 3)
    laid = laid.reshape(SLOT_PAIRS * PATCHES, LANES)
    live = jnp.sum(jnp.where(group_order[:, None] == jnp.arange(groups)[None, :], counts[None, :], 0), axis=1)
    own = position.astype(jnp.int32).reshape(1)
    scalars = jnp.concatenate([packed_order(live), group_order, counts, support.reshape(groups * SLOTS), own])
    collect = functools.partial(collect_support, scalars, groups, dictionary, pairs)
    gathered, (blocks,) = gather_shards(laid, [functools.partial(collect, part) for part in range(SUPPORT_PARTS)])

    targets = patches.T
    half_penalty = 0.5 * penalty
    thresh_tiles = jnp.broadcast_to(half_penalty[:, :, None], (groups, PATCHES, LANES))

    run = functools.partial(
        gradient_call, shards=devices, pairs=pairs, groups=groups, scalars=scalars, blocks=blocks, targets=targets
    )
    *shares, start, thresh = run("first", gathered=gathered, extra=(thresh_tiles,))
    point = previous = start.astype(jnp.float32)
    for turn in range(ITERS - 1):
        if turn:
            shares = run("packed", gathered=gathered)
        current = shrink(point - 0.5 * reduce_shards(*shares), thresh)
        point = current + momenta[turn] * (current - previous)
        previous = current
        gathered, _ = gather_shards(point.astype(jnp.bfloat16))
    *shares, sent, thresh = run("final", gathered=gathered, extra=(thresh_tiles,))
    gradient = last_reduce(*shares).reshape(SLOT_PAIRS, PATCHES, LANES)
    sent = sent.astype(jnp.float32)
    result = shrink(sent - 0.5 * gradient, thresh[None])
    result = result.reshape(SLOT_PAIRS, PATCHES, 2, BLOCK).transpose(0, 2, 1, 3)
    return result.reshape(1, SLOTS, PATCHES * BLOCK)


def solution(mesh):
    in_specs = (
        P("rows", None),
        P("rows", "groups"),
        P(("groups", "rows"), None, None),
        P("groups", None),
        P("groups"),
        P("groups"),
        P("groups", None),
    )
    out_specs = P(("groups", "rows"), None, None)
    return jax.shard_map(local, mesh=mesh, in_specs=in_specs, out_specs=out_specs, check_vma=False)
```

```python
import functools
import math

import jax
import jax.numpy as jnp
from jax import lax
from jax.experimental import pallas as pl
from jax.experimental.pallas import tpu as pltpu
from jax.sharding import PartitionSpec as P

BLOCK = 64
SLOTS = 16
PATCHES = 64
ITERS = 3
MEAN_LIVE = 10
LANES = 2 * BLOCK
SLOT_PAIRS = SLOTS // 2
SPARE = SLOT_PAIRS + 2
ROW_TILE = 16
SUPPORT_PARTS = 2
SUPPORT_STEP = 4
PIECE = 5
MATRIX_UNIT = 256
VMEM_MARGIN = 3 * 1024 * 1024
SUPPORT_VMEM = 40 * 1024 * 1024
HELD_BYTES = 65 * 1024 * 1024


def momentum_list():
    values = []
    tvalue = 1.0
    for turn in range(ITERS):
        tnext = (1.0 + (1.0 + 4.0 * tvalue * tvalue) ** 0.5) / 2.0
        values.append((tvalue - 1.0) / tnext)
        tvalue = tnext
    return values


def swap_halves(value):
    return jnp.concatenate([value[:, BLOCK:], value[:, :BLOCK]], axis=1)


def upper_half(shape):
    return lax.broadcasted_iota(jnp.int32, shape, 1) >= BLOCK


class Part:
    def __init__(self, ref, begin, width=1):
        self.ref, self.begin, self.width = ref, begin, width

    def __getitem__(self, index):
        if isinstance(index, tuple):
            index = index[0] * self.width + index[1]
        return self.ref[self.begin + index]


def scalar_parts(scalars, groups):
    seq, order, counts = (Part(scalars, part * groups) for part in range(3))
    return seq, order, counts, Part(scalars, 3 * groups, SLOTS), scalars[groups * (3 + SLOTS)]


def group_at(index, seq, order, counts):
    position = seq[index]
    group = order[position]
    return position, group, counts[group]


def support_kernel(begin, groups, scalars, dictionary, *refs):
    out, held, picks, ids, sems, out_sems = refs[-6:]
    seq, order, counts, support, _ = scalar_parts(scalars, groups)
    entries, rows, _ = held.shape
    pairs = entries // 2

    def fetch(entry, block):
        start = pl.multiple_of((block // 2) * LANES, LANES)
        return pltpu.make_async_copy(dictionary.at[:, pl.ds(start, LANES)], held.at[entry], sems.at[entry])

    def start_group(index, offset):
        _, group, live = group_at(index, seq, order, counts)

        def start_slot(slot, carry):
            ids[offset + slot] = support[group, slot]
            return carry

        lax.fori_loop(jnp.clip(-offset, 0, live), jnp.clip(entries - offset, 0, live), start_slot, 0)
        return offset + live

    lax.fori_loop(0, groups, start_group, jnp.int32(-begin))
    steps = pairs // SUPPORT_STEP

    def start_step(step):
        for entry in range(2 * SUPPORT_STEP):
            index = 2 * SUPPORT_STEP * step + entry
            fetch(index, ids[index]).start()

    def start_all(step, carry):
        start_step(step)
        return carry

    lax.fori_loop(0, steps, start_all, 0)
    shape = (2 * LANES, LANES)
    source = lax.broadcasted_iota(jnp.int32, shape, 0)
    target = lax.broadcasted_iota(jnp.int32, shape, 1)
    for choice in range(4):
        wanted = jnp.where(target < BLOCK, (choice % 2) * BLOCK + target, LANES + (choice // 2) * BLOCK + target - BLOCK)
        picks[choice] = (source == wanted).astype(jnp.float32).astype(jnp.bfloat16)

    def store(pair):
        return pltpu.make_async_copy(held.at[2 * pair], out.at[begin // 2 + pair], out_sems.at[pair])

    def pack(step, carry):
        span = [SUPPORT_STEP * step + pair for pair in range(SUPPORT_STEP)]
        for pair in span:
            fetch(2 * pair, ids[2 * pair]).wait()
            fetch(2 * pair + 1, ids[2 * pair + 1]).wait()
        packed = []
        for pair in span:
            choice = ids[2 * pair] % 2 + 2 * (ids[2 * pair + 1] % 2)
            both = jnp.concatenate([held[2 * pair], held[2 * pair + 1]], axis=1)
            packed.append(jnp.dot(both, picks[choice], preferred_element_type=jnp.float32).astype(jnp.bfloat16))
        for pair, value in zip(span, packed):
            held[2 * pair] = value
            store(pair).start()
        return carry

    lax.fori_loop(0, steps, pack, 0)

    def drain(pair, carry):
        store(pair).wait()
        return carry

    lax.fori_loop(0, pairs, drain, 0)


def collect_support(scalars, groups, dictionary, pairs, part, *before):
    rows = dictionary.shape[0]
    pairs = pairs // SUPPORT_PARTS
    entries = 2 * pairs
    return pl.pallas_call(
        functools.partial(support_kernel, part * entries, groups),
        grid_spec=pltpu.PrefetchScalarGridSpec(
            num_scalar_prefetch=1,
            grid=(),
            in_specs=[pl.BlockSpec(memory_space=pltpu.HBM)] * (1 + len(before)),
            out_specs=pl.BlockSpec(memory_space=pltpu.HBM),
            scratch_shapes=[
                pltpu.VMEM((entries, rows, LANES), dictionary.dtype),
                pltpu.VMEM((4, 2 * LANES, LANES), jnp.bfloat16),
                pltpu.SMEM((entries,), jnp.int32),
                pltpu.SemaphoreType.DMA((entries,)),
                pltpu.SemaphoreType.DMA((pairs,)),
            ],
        ),
        out_shape=jax.ShapeDtypeStruct((HELD_BYTES // (rows * LANES * 2), rows, LANES), dictionary.dtype),
        compiler_params=pltpu.CompilerParams(vmem_limit_bytes=SUPPORT_VMEM),
        cost_estimate=pl.CostEstimate(flops=0, transcendentals=0, bytes_accessed=6 * pairs * rows * LANES * 2),
        input_output_aliases={2: 0} if before else {},
        name="collect_support",
    )(scalars, dictionary, *before)


def stage_distances(devices):
    return [2**bit for bit in range(devices.bit_length() - 1)]


def last_orders(devices):
    distances = stage_distances(devices)
    return distances, distances[:1] + distances[2:] + distances[1:2]


def slot_distance(slot, distances):
    bits = reversed(range(len(distances)))
    return sum(distance for bit, distance in zip(bits, distances) if slot >> bit & 1)


def gradient_kernel(mode, shards, pairs, groups, scalars, blocks, *refs):
    seq, order, counts, _, me = scalar_parts(scalars, groups)
    refs = list(refs)
    take = lambda: refs.pop(0)
    gathered, targets = [take() for _ in range(4)], take()
    if mode in ("first", "final"):
        thresh = take()
    keep, send = take(), (take(), take())
    if mode == "first":
        start_out, thresh_out = take(), take()
    if mode == "final":
        sent, thresh_out = take(), take()
    held, codes, total = take(), take(), take()
    if mode == "first":
        starts, limits = take(), take()
    offsets, sems = refs

    pieces = pairs // PIECE

    def load(index):
        span = pl.ds(index * PIECE, PIECE)
        return pltpu.make_async_copy(blocks.at[span], held.at[span], sems.at[index])

    for index in range(pieces):
        load(index).start()
    held[pairs:] = jnp.zeros((SPARE,) + held.shape[1:], held.dtype)

    distances = stage_distances(shards)

    def shard_span(slot, size):
        return pl.ds(pl.multiple_of((slot_distance(slot, distances) ^ me) * size, ROW_TILE), size)

    def last_holder(slot):
        even, odd = (slot_distance(slot, order) for order in last_orders(shards))
        if slot >= shards // 2:
            even, odd = odd, even
        return jnp.where(me % 2 == 0, even, odd) ^ me

    quarter = shards // 4
    size_in = gathered[0].shape[0] // (quarter + 1)
    for slot in range(shards):
        half, inside = divmod(slot, 2 * quarter)
        second = inside > quarter
        begin = (inside - (quarter + 1) * second) * size_in
        codes[shard_span(slot, size_in), :] = gathered[2 * half + second][begin : begin + size_in, :]

    def put(slot, size, begin, value):
        far, inside = divmod(slot, 2 * quarter)
        if far:
            ahead = send[0].shape[0] // size
            second = inside >= ahead
            start = (inside - ahead * second) * size + begin
            send[second][start : start + value.shape[0], :] = value.astype(jnp.bfloat16)
        else:
            start = inside * size + begin
            keep[start : start + value.shape[0], :] = value

    def seat(index, offset):
        position, _, live = group_at(index, seq, order, counts)
        offsets[position] = offset
        return offset + live

    lax.fori_loop(0, groups, seat, jnp.int32(0))

    upper = upper_half((PATCHES, LANES))
    side = upper.astype(jnp.int32)

    def tile(pair):
        return pl.ds(pl.multiple_of(pair * PATCHES, PATCHES), PATCHES)

    def shifted(parts, count, odd, ahead):
        turned = [swap_halves(part) for part in parts]
        last = len(parts) - 1
        moved = []
        for pair in range(count):
            low, high = (pair, pair + 1) if ahead else (pair - 1, pair)
            low, high = min(max(low, 0), last), min(max(high, 0), last)
            value = jnp.where(upper[: turned[low].shape[0]], turned[high], turned[low])
            moved.append(jnp.where(odd, value, parts[min(pair, last)]))
        return moved

    def read_codes(position, offset, live, count):
        first = offset // 2
        if mode == "first":
            parts = [codes[tile(position * SLOT_PAIRS + pair), :] for pair in range(min(count, SLOT_PAIRS))]
            parts = shifted(parts, count, offset % 2 == 1, False)
        else:
            parts = [codes[tile(first + pair), :] for pair in range(count)]
        masked = []
        for pair, part in enumerate(parts):
            entry = 2 * (first + pair) + side
            mine = (entry >= offset) & (entry < offset + live)
            masked.append(jnp.where(mine, part, jnp.zeros_like(part)))
        return masked

    def write_packed(ref, parts, offset):
        first = offset // 2
        for pair, part in enumerate(parts):
            if pair == 0:
                part = jnp.where(upper | (offset % 2 == 0), part, ref[tile(first), :])
            ref[tile(first + pair), :] = part

    def one_group(position, group, offset, live, count):
        first = offset // 2
        parts = read_codes(position, offset, live, count)
        if mode == "first":
            write_packed(starts, parts, offset)
            write_packed(limits, [thresh[group]] * count, offset)
        matrix = jnp.concatenate([held[first + pair] for pair in range(count)], axis=1)
        point = jnp.concatenate(parts, axis=1)
        residual = lax.dot_general(point, matrix, (((1,), (1,)), ((), ())), preferred_element_type=jnp.float32)
        target = targets[tile(group), :].astype(jnp.float32)
        residual = (residual - target).astype(jnp.bfloat16)
        gradient = jnp.dot(residual, matrix, preferred_element_type=jnp.float32)
        write_packed(total, [gradient[:, pair * LANES : (pair + 1) * LANES] for pair in range(count)], offset)

    def wait_piece(index, carry):
        load(index).wait()
        return carry

    def two_groups(step, waited):
        picks = []
        count_needed = 1
        for index in (2 * step, 2 * step + 1):
            position, group, live = group_at(index, seq, order, counts)
            offset = offsets[position]
            picks.append((position, group, offset, live))
            count_needed = jnp.maximum(count_needed, (live + offset % 2 + 1) // 2)
        reach = jnp.minimum(picks[1][2] // 2 + count_needed - 1, pairs - 1)
        needed = jnp.maximum(reach // PIECE + 1, waited)
        lax.fori_loop(waited, needed, wait_piece, 0)
        for count in range(1, SLOT_PAIRS + 2):

            @pl.when(count_needed == count)
            def _(count=count):
                for pick in picks:
                    one_group(*pick, count)

        return needed

    waited = lax.fori_loop(0, groups // 2, two_groups, jnp.int32(0))
    lax.fori_loop(waited, pieces, wait_piece, 0)

    if mode != "final":
        size = 2 * keep.shape[0] // shards
        for slot in range(shards):
            put(slot, size, 0, total[shard_span(slot, size), :])
    if mode == "first":
        size = start_out.shape[0]
        span = pl.ds(pl.multiple_of(me * size, ROW_TILE), size)
        start_out[...] = starts[span, :]
        thresh_out[...] = limits[span, :]
    if mode == "final":
        offset = offsets[me]
        parts = read_codes(me, offset, counts[order[me]], SLOT_PAIRS + 1)
        for pair, part in enumerate(shifted(parts, SLOT_PAIRS, offset % 2 == 1, True)):
            sent[pair] = part
        thresh_out[...] = thresh[order[me]]
        for slot in range(shards):
            position = last_holder(slot)
            offset = offsets[position]
            live = counts[order[position]]
            parts = [total[tile(offset // 2 + pair), :] for pair in range(SLOT_PAIRS + 1)]
            for pair, part in enumerate(shifted(parts, SLOT_PAIRS, offset % 2 == 1, True)):
                value = jnp.where(2 * pair + side < live, part, 0.0)
                put(slot, SLOT_PAIRS * PATCHES, pair * PATCHES, value)


def gradient_call(mode, shards, pairs, groups, scalars, blocks, gathered, targets, extra=()):
    rows = blocks.shape[1]
    places = pairs + SPARE
    single, double = jnp.bfloat16, jnp.float32
    packed = (places * PATCHES, LANES)
    half_out = (groups * SLOT_PAIRS if mode == "final" else pairs) * PATCHES // 2
    shard = (2 * half_out // shards, LANES)
    ahead = half_out // 2 + (0 if mode == "final" else shard[0])
    outs = [((half_out, LANES), double), ((ahead, LANES), single), ((half_out - ahead, LANES), single)]
    if mode == "first":
        outs += [(shard, single), (shard, double)]
    if mode == "final":
        outs += [((SLOT_PAIRS, PATCHES, LANES), single), ((PATCHES, LANES), double)]
    codes = groups * SLOT_PAIRS * PATCHES if mode == "first" else packed[0]
    scratch = [((places, rows, LANES), single), ((codes, LANES), single), (packed, double)]
    if mode == "first":
        scratch += [(packed, single), (packed, double)]
    room = sum(math.prod(shape) * jnp.dtype(kind).itemsize for shape, kind in scratch)
    return pl.pallas_call(
        functools.partial(gradient_kernel, mode, shards, pairs, groups),
        grid_spec=pltpu.PrefetchScalarGridSpec(
            num_scalar_prefetch=1,
            grid=(),
            in_specs=[pl.BlockSpec(memory_space=pltpu.HBM)]
            + [pl.BlockSpec(memory_space=pltpu.VMEM)] * (5 + len(extra)),
            out_specs=[pl.BlockSpec(memory_space=pltpu.VMEM)] * len(outs),
            scratch_shapes=[pltpu.VMEM(shape, kind) for shape, kind in scratch]
            + [pltpu.SMEM((groups,), jnp.int32), pltpu.SemaphoreType.DMA((pairs // PIECE,))],
        ),
        out_shape=[jax.ShapeDtypeStruct(shape, kind) for shape, kind in outs],
        compiler_params=pltpu.CompilerParams(vmem_limit_bytes=room + VMEM_MARGIN),
        cost_estimate=pl.CostEstimate(
            flops=4 * pairs * rows * LANES * MATRIX_UNIT, transcendentals=0, bytes_accessed=pairs * rows * LANES * 2
        ),
        name="gradient",
    )(scalars, blocks, *gathered, targets, *extra)


def exchange(value, even, odd=None):
    devices = lax.axis_size("rows")
    apart = (even, even if odd is None else odd)
    return lax.ppermute(value, "rows", [(i, i ^ apart[i % 2]) for i in range(devices)])


def gather_shards(own, beside=()):
    core, row, *columns = stage_distances(lax.axis_size("rows"))
    apart = [slot_distance(slot, columns) for slot in range(lax.axis_size("rows") // 4)]
    made = ()
    near = jnp.concatenate([own] + [exchange(own, distance) for distance in apart[1:] + [row]], axis=0)
    if beside:
        near, *made = lax.optimization_barrier((near, beside[0]()))
    other = exchange(near[own.shape[0] : len(apart) * own.shape[0]], row)
    far = exchange(near, core)
    if beside:
        other, *made = lax.optimization_barrier((other, beside[1](*made)))
    return (near, other, far, exchange(other, core)), made


def add_cores(keep, *send):
    ahead = send[0].shape[0]
    after = keep[ahead:] + exchange(send[1], 1).astype(jnp.float32)
    return keep[:ahead] + exchange(send[0], 1).astype(jnp.float32), after


def reduce_shards(keep, *send):
    devices = lax.axis_size("rows")
    _, row, *columns = stage_distances(devices)
    size = 2 * keep.shape[0] // devices
    near, other = add_cores(keep, *send)
    sums = near[size:-size] + exchange(other.astype(jnp.bfloat16), row).astype(jnp.float32)
    last, sums = lax.optimization_barrier((near[-size:].astype(jnp.bfloat16), sums.astype(jnp.bfloat16)))
    total = near[:size] + exchange(last, row).astype(jnp.float32)
    for slot in range(1, devices // 4):
        share = exchange(sums[(slot - 1) * size : slot * size], slot_distance(slot, columns))
        total = total + share.astype(jnp.float32)
    return total


def last_reduce(keep, *send):
    near, other = add_cores(keep, *send)
    for even, odd in list(zip(*last_orders(lax.axis_size("rows"))))[1:]:
        total = near + exchange(other.astype(jnp.bfloat16), even, odd).astype(jnp.float32)
        near, other = total[: total.shape[0] // 2], total[total.shape[0] // 2 :]
    return total


def packed_order(live):
    index = jnp.arange(live.shape[0])
    ahead = (live[None, :] < live[:, None]) | ((live[None, :] == live[:, None]) & (index[None, :] < index[:, None]))
    rank = jnp.sum(ahead.astype(jnp.int32), axis=1)
    return jnp.sum(jnp.where(rank[:, None] == index[None, :], index[:, None], 0), axis=0).astype(jnp.int32)


def shrink(value, thresh):
    return value - jnp.clip(value, -thresh, thresh)


def local(dictionary, patches, initial_codes, support, counts, group_order, penalty):
    groups = group_order.shape[0]
    position = lax.axis_index("rows")
    devices = lax.axis_size("rows")
    momenta = momentum_list()
    pairs = MEAN_LIVE * groups // 2

    laid = initial_codes.reshape(SLOT_PAIRS, 2, PATCHES, BLOCK).transpose(0, 2, 1, 3)
    laid = laid.reshape(SLOT_PAIRS * PATCHES, LANES)
    live = jnp.sum(jnp.where(group_order[:, None] == jnp.arange(groups)[None, :], counts[None, :], 0), axis=1)
    own = position.astype(jnp.int32).reshape(1)
    scalars = jnp.concatenate([packed_order(live), group_order, counts, support.reshape(groups * SLOTS), own])
    collect = functools.partial(collect_support, scalars, groups, dictionary, pairs)
    gathered, (blocks,) = gather_shards(laid, [functools.partial(collect, part) for part in range(SUPPORT_PARTS)])

    targets = patches.T
    half_penalty = 0.5 * penalty
    thresh_tiles = jnp.broadcast_to(half_penalty[:, :, None], (groups, PATCHES, LANES))

    run = functools.partial(
        gradient_call, shards=devices, pairs=pairs, groups=groups, scalars=scalars, blocks=blocks, targets=targets
    )
    *shares, start, thresh = run("first", gathered=gathered, extra=(thresh_tiles,))
    point = previous = start.astype(jnp.float32)
    for turn in range(ITERS - 1):
        if turn:
            shares = run("packed", gathered=gathered)
        current = shrink(point - 0.5 * reduce_shards(*shares), thresh)
        point = current + momenta[turn] * (current - previous)
        previous = current
        gathered, _ = gather_shards(point.astype(jnp.bfloat16))
    *shares, sent, thresh = run("final", gathered=gathered, extra=(thresh_tiles,))
    gradient = last_reduce(*shares).reshape(SLOT_PAIRS, PATCHES, LANES)
    sent = sent.astype(jnp.float32)
    result = shrink(sent - 0.5 * gradient, thresh[None])
    result = result.reshape(SLOT_PAIRS, PATCHES, 2, BLOCK).transpose(0, 2, 1, 3)
    return result.reshape(1, SLOTS, PATCHES * BLOCK)


def solution(mesh):
    in_specs = (
        P("rows", None),
        P("rows", "groups"),
        P(("groups", "rows"), None, None),
        P("groups", None),
        P("groups"),
        P("groups"),
        P("groups", None),
    )
    out_specs = P(("groups", "rows"), None, None)
    return jax.shard_map(local, mesh=mesh, in_specs=in_specs, out_specs=out_specs, check_vma=False)
```

```python
import functools
import math

import jax
import jax.numpy as jnp
from jax import lax
from jax.experimental import pallas as pl
from jax.experimental.pallas import tpu as pltpu
from jax.sharding import PartitionSpec as P

BLOCK = 64
SLOTS = 16
PATCHES = 64
ITERS = 3
MEAN_LIVE = 10
LANES = 2 * BLOCK
SLOT_PAIRS = SLOTS // 2
SPARE = SLOT_PAIRS + 2
ROW_TILE = 16
SUPPORT_PARTS = 2
SUPPORT_STEP = 4
PIECE = 5
MATRIX_UNIT = 256
VMEM_MARGIN = 3 * 1024 * 1024
SUPPORT_VMEM = 40 * 1024 * 1024
HELD_BYTES = 65 * 1024 * 1024


def momentum_list():
    values = []
    tvalue = 1.0
    for turn in range(ITERS):
        tnext = (1.0 + (1.0 + 4.0 * tvalue * tvalue) ** 0.5) / 2.0
        values.append((tvalue - 1.0) / tnext)
        tvalue = tnext
    return values


def swap_halves(value):
    return jnp.concatenate([value[:, BLOCK:], value[:, :BLOCK]], axis=1)


def upper_half(shape):
    return lax.broadcasted_iota(jnp.int32, shape, 1) >= BLOCK


class Part:
    def __init__(self, ref, begin, width=1):
        self.ref, self.begin, self.width = ref, begin, width

    def __getitem__(self, index):
        if isinstance(index, tuple):
            index = index[0] * self.width + index[1]
        return self.ref[self.begin + index]


def scalar_parts(scalars, groups):
    seq, order, counts = (Part(scalars, part * groups) for part in range(3))
    return seq, order, counts, Part(scalars, 3 * groups, SLOTS), scalars[groups * (3 + SLOTS)]


def group_at(index, seq, order, counts):
    position = seq[index]
    group = order[position]
    return position, group, counts[group]


def support_kernel(begin, groups, scalars, dictionary, *refs):
    out, held, picks, ids, sems, out_sems = refs[-6:]
    seq, order, counts, support, _ = scalar_parts(scalars, groups)
    entries, rows, _ = held.shape
    pairs = entries // 2

    def fetch(entry, block):
        start = pl.multiple_of((block // 2) * LANES, LANES)
        return pltpu.make_async_copy(dictionary.at[:, pl.ds(start, LANES)], held.at[entry], sems.at[entry])

    def start_group(index, offset):
        _, group, live = group_at(index, seq, order, counts)

        def start_slot(slot, carry):
            block = support[group, slot]
            ids[offset + slot] = block
            fetch(offset + slot, block).start()
            return carry

        lax.fori_loop(jnp.clip(-offset, 0, live), jnp.clip(entries - offset, 0, live), start_slot, 0)
        return offset + live

    lax.fori_loop(0, groups, start_group, jnp.int32(-begin))
    steps = pairs // SUPPORT_STEP
    shape = (2 * LANES, LANES)
    source = lax.broadcasted_iota(jnp.int32, shape, 0)
    target = lax.broadcasted_iota(jnp.int32, shape, 1)
    for choice in range(4):
        wanted = jnp.where(target < BLOCK, (choice % 2) * BLOCK + target, LANES + (choice // 2) * BLOCK + target - BLOCK)
        picks[choice] = (source == wanted).astype(jnp.float32).astype(jnp.bfloat16)

    def store(pair):
        return pltpu.make_async_copy(held.at[2 * pair], out.at[begin // 2 + pair], out_sems.at[pair])

    def pack(step, carry):
        span = [SUPPORT_STEP * step + pair for pair in range(SUPPORT_STEP)]
        for pair in span:
            fetch(2 * pair, ids[2 * pair]).wait()
            fetch(2 * pair + 1, ids[2 * pair + 1]).wait()
        packed = []
        for pair in span:
            choice = ids[2 * pair] % 2 + 2 * (ids[2 * pair + 1] % 2)
            both = jnp.concatenate([held[2 * pair], held[2 * pair + 1]], axis=1)
            packed.append(jnp.dot(both, picks[choice], preferred_element_type=jnp.float32).astype(jnp.bfloat16))
        for pair, value in zip(span, packed):
            held[2 * pair] = value
            store(pair).start()
        return carry

    lax.fori_loop(0, steps, pack, 0)

    def drain(pair, carry):
        store(pair).wait()
        return carry

    lax.fori_loop(0, pairs, drain, 0)


def collect_support(scalars, groups, dictionary, pairs, part, *before):
    rows = dictionary.shape[0]
    pairs = pairs // SUPPORT_PARTS
    entries = 2 * pairs
    return pl.pallas_call(
        functools.partial(support_kernel, part * entries, groups),
        grid_spec=pltpu.PrefetchScalarGridSpec(
            num_scalar_prefetch=1,
            grid=(),
            in_specs=[pl.BlockSpec(memory_space=pltpu.HBM)] * (1 + len(before)),
            out_specs=pl.BlockSpec(memory_space=pltpu.HBM),
            scratch_shapes=[
                pltpu.VMEM((entries, rows, LANES), dictionary.dtype),
                pltpu.VMEM((4, 2 * LANES, LANES), jnp.bfloat16),
                pltpu.SMEM((entries,), jnp.int32),
                pltpu.SemaphoreType.DMA((entries,)),
                pltpu.SemaphoreType.DMA((pairs,)),
            ],
        ),
        out_shape=jax.ShapeDtypeStruct((HELD_BYTES // (rows * LANES * 2), rows, LANES), dictionary.dtype),
        compiler_params=pltpu.CompilerParams(vmem_limit_bytes=SUPPORT_VMEM),
        cost_estimate=pl.CostEstimate(flops=0, transcendentals=0, bytes_accessed=6 * pairs * rows * LANES * 2),
        input_output_aliases={2: 0} if before else {},
        name="collect_support",
    )(scalars, dictionary, *before)


def stage_distances(devices):
    return [2**bit for bit in range(devices.bit_length() - 1)]


def last_orders(devices):
    distances = stage_distances(devices)
    return distances, distances[:1] + distances[2:] + distances[1:2]


def slot_distance(slot, distances):
    bits = reversed(range(len(distances)))
    return sum(distance for bit, distance in zip(bits, distances) if slot >> bit & 1)


def gradient_kernel(mode, shards, pairs, groups, scalars, blocks, *refs):
    seq, order, counts, _, me = scalar_parts(scalars, groups)
    refs = list(refs)
    take = lambda: refs.pop(0)
    gathered, targets = [take() for _ in range(4)], take()
    if mode in ("first", "final"):
        thresh = take()
    keep, send = take(), (take(), take())
    if mode == "first":
        start_out, thresh_out = take(), take()
    if mode == "final":
        sent, thresh_out = take(), take()
    held, codes, total = take(), take(), take()
    if mode == "first":
        starts, limits = take(), take()
    offsets, sems = refs

    pieces = pairs // PIECE

    def load(index):
        span = pl.ds(index * PIECE, PIECE)
        return pltpu.make_async_copy(blocks.at[span], held.at[span], sems.at[index])

    for index in range(pieces):
        load(index).start()
    held[pairs:] = jnp.zeros((SPARE,) + held.shape[1:], held.dtype)

    distances = stage_distances(shards)

    def shard_span(slot, size):
        return pl.ds(pl.multiple_of((slot_distance(slot, distances) ^ me) * size, ROW_TILE), size)

    def last_holder(slot):
        even, odd = (slot_distance(slot, order) for order in last_orders(shards))
        if slot >= shards // 2:
            even, odd = odd, even
        return jnp.where(me % 2 == 0, even, odd) ^ me

    quarter = shards // 4
    size_in = gathered[0].shape[0] // (quarter + 1)
    for slot in range(shards):
        half, inside = divmod(slot, 2 * quarter)
        second = inside > quarter
        begin = (inside - (quarter + 1) * second) * size_in
        codes[shard_span(slot, size_in), :] = gathered[2 * half + second][begin : begin + size_in, :]

    def put(slot, size, begin, value):
        far, inside = divmod(slot, 2 * quarter)
        if far:
            ahead = send[0].shape[0] // size
            second = inside >= ahead
            start = (inside - ahead * second) * size + begin
            send[second][start : start + value.shape[0], :] = value.astype(jnp.bfloat16)
        else:
            start = inside * size + begin
            keep[start : start + value.shape[0], :] = value

    def seat(index, offset):
        position, _, live = group_at(index, seq, order, counts)
        offsets[position] = offset
        return offset + live

    lax.fori_loop(0, groups, seat, jnp.int32(0))

    upper = upper_half((PATCHES, LANES))
    side = upper.astype(jnp.int32)

    def tile(pair):
        return pl.ds(pl.multiple_of(pair * PATCHES, PATCHES), PATCHES)

    def shifted(parts, count, odd, ahead):
        turned = [swap_halves(part) for part in parts]
        last = len(parts) - 1
        moved = []
        for pair in range(count):
            low, high = (pair, pair + 1) if ahead else (pair - 1, pair)
            low, high = min(max(low, 0), last), min(max(high, 0), last)
            value = jnp.where(upper[: turned[low].shape[0]], turned[high], turned[low])
            moved.append(jnp.where(odd, value, parts[min(pair, last)]))
        return moved

    def read_codes(position, offset, live, count):
        first = offset // 2
        if mode == "first":
            parts = [codes[tile(position * SLOT_PAIRS + pair), :] for pair in range(min(count, SLOT_PAIRS))]
            parts = shifted(parts, count, offset % 2 == 1, False)
        else:
            parts = [codes[tile(first + pair), :] for pair in range(count)]
        masked = []
        for pair, part in enumerate(parts):
            entry = 2 * (first + pair) + side
            mine = (entry >= offset) & (entry < offset + live)
            masked.append(jnp.where(mine, part, jnp.zeros_like(part)))
        return masked

    def write_packed(ref, parts, offset):
        first = offset // 2
        for pair, part in enumerate(parts):
            if pair == 0:
                part = jnp.where(upper | (offset % 2 == 0), part, ref[tile(first), :])
            ref[tile(first + pair), :] = part

    def one_group(position, group, offset, live, count):
        first = offset // 2
        parts = read_codes(position, offset, live, count)
        if mode == "first":
            write_packed(starts, parts, offset)
            write_packed(limits, [thresh[group]] * count, offset)
        matrix = jnp.concatenate([held[first + pair] for pair in range(count)], axis=1)
        point = jnp.concatenate(parts, axis=1)
        residual = lax.dot_general(point, matrix, (((1,), (1,)), ((), ())), preferred_element_type=jnp.float32)
        target = targets[tile(group), :].astype(jnp.float32)
        residual = (residual - target).astype(jnp.bfloat16)
        gradient = jnp.dot(residual, matrix, preferred_element_type=jnp.float32)
        write_packed(total, [gradient[:, pair * LANES : (pair + 1) * LANES] for pair in range(count)], offset)

    def wait_piece(index, carry):
        load(index).wait()
        return carry

    def two_groups(step, waited):
        picks = []
        count_needed = 1
        for index in (2 * step, 2 * step + 1):
            position, group, live = group_at(index, seq, order, counts)
            offset = offsets[position]
            picks.append((position, group, offset, live))
            count_needed = jnp.maximum(count_needed, (live + offset % 2 + 1) // 2)
        reach = jnp.minimum(picks[1][2] // 2 + count_needed - 1, pairs - 1)
        needed = jnp.maximum(reach // PIECE + 1, waited)
        lax.fori_loop(waited, needed, wait_piece, 0)
        for count in range(1, SLOT_PAIRS + 2):

            @pl.when(count_needed == count)
            def _(count=count):
                for pick in picks:
                    one_group(*pick, count)

        return needed

    waited = lax.fori_loop(0, groups // 2, two_groups, jnp.int32(0))
    lax.fori_loop(waited, pieces, wait_piece, 0)

    if mode != "final":
        size = 2 * keep.shape[0] // shards
        for slot in range(shards):
            put(slot, size, 0, total[shard_span(slot, size), :])
    if mode == "first":
        size = start_out.shape[0]
        span = pl.ds(pl.multiple_of(me * size, ROW_TILE), size)
        start_out[...] = starts[span, :]
        thresh_out[...] = limits[span, :]
    if mode == "final":
        offset = offsets[me]
        parts = read_codes(me, offset, counts[order[me]], SLOT_PAIRS + 1)
        for pair, part in enumerate(shifted(parts, SLOT_PAIRS, offset % 2 == 1, True)):
            sent[pair] = part
        thresh_out[...] = thresh[order[me]]
        for slot in range(shards):
            position = last_holder(slot)
            offset = offsets[position]
            live = counts[order[position]]
            parts = [total[tile(offset // 2 + pair), :] for pair in range(SLOT_PAIRS + 1)]
            for pair, part in enumerate(shifted(parts, SLOT_PAIRS, offset % 2 == 1, True)):
                value = jnp.where(2 * pair + side < live, part, 0.0)
                put(slot, SLOT_PAIRS * PATCHES, pair * PATCHES, value)


def gradient_call(mode, shards, pairs, groups, scalars, blocks, gathered, targets, extra=()):
    rows = blocks.shape[1]
    places = pairs + SPARE
    single, double = jnp.bfloat16, jnp.float32
    packed = (places * PATCHES, LANES)
    half_out = (groups * SLOT_PAIRS if mode == "final" else pairs) * PATCHES // 2
    shard = (2 * half_out // shards, LANES)
    ahead = half_out // 2 + (0 if mode == "final" else shard[0])
    outs = [((half_out, LANES), double), ((ahead, LANES), single), ((half_out - ahead, LANES), single)]
    if mode == "first":
        outs += [(shard, single), (shard, double)]
    if mode == "final":
        outs += [((SLOT_PAIRS, PATCHES, LANES), single), ((PATCHES, LANES), double)]
    codes = groups * SLOT_PAIRS * PATCHES if mode == "first" else packed[0]
    scratch = [((places, rows, LANES), single), ((codes, LANES), single), (packed, double)]
    if mode == "first":
        scratch += [(packed, single), (packed, double)]
    room = sum(math.prod(shape) * jnp.dtype(kind).itemsize for shape, kind in scratch)
    return pl.pallas_call(
        functools.partial(gradient_kernel, mode, shards, pairs, groups),
        grid_spec=pltpu.PrefetchScalarGridSpec(
            num_scalar_prefetch=1,
            grid=(),
            in_specs=[pl.BlockSpec(memory_space=pltpu.HBM)]
            + [pl.BlockSpec(memory_space=pltpu.VMEM)] * (5 + len(extra)),
            out_specs=[pl.BlockSpec(memory_space=pltpu.VMEM)] * len(outs),
            scratch_shapes=[pltpu.VMEM(shape, kind) for shape, kind in scratch]
            + [pltpu.SMEM((groups,), jnp.int32), pltpu.SemaphoreType.DMA((pairs // PIECE,))],
        ),
        out_shape=[jax.ShapeDtypeStruct(shape, kind) for shape, kind in outs],
        compiler_params=pltpu.CompilerParams(vmem_limit_bytes=room + VMEM_MARGIN),
        cost_estimate=pl.CostEstimate(
            flops=4 * pairs * rows * LANES * MATRIX_UNIT, transcendentals=0, bytes_accessed=pairs * rows * LANES * 2
        ),
        name="gradient",
    )(scalars, blocks, *gathered, targets, *extra)


def exchange(value, even, odd=None):
    devices = lax.axis_size("rows")
    apart = (even, even if odd is None else odd)
    return lax.ppermute(value, "rows", [(i, i ^ apart[i % 2]) for i in range(devices)])


def gather_shards(own, beside=()):
    core, row, *columns = stage_distances(lax.axis_size("rows"))
    apart = [slot_distance(slot, columns) for slot in range(lax.axis_size("rows") // 4)]
    made = ()
    near = jnp.concatenate([own] + [exchange(own, distance) for distance in apart[1:] + [row]], axis=0)
    if beside:
        near, *made = lax.optimization_barrier((near, beside[0]()))
    other = exchange(near[own.shape[0] : len(apart) * own.shape[0]], row)
    far = exchange(near, core)
    if beside:
        other, *made = lax.optimization_barrier((other, beside[1](*made)))
    return (near, other, far, exchange(other, core)), made


def add_cores(keep, *send):
    ahead = send[0].shape[0]
    after = keep[ahead:] + exchange(send[1], 1).astype(jnp.float32)
    return keep[:ahead] + exchange(send[0], 1).astype(jnp.float32), after


def reduce_shards(keep, *send):
    devices = lax.axis_size("rows")
    _, row, *columns = stage_distances(devices)
    size = 2 * keep.shape[0] // devices
    near, other = add_cores(keep, *send)
    sums = near[size:-size] + exchange(other.astype(jnp.bfloat16), row).astype(jnp.float32)
    last, sums = lax.optimization_barrier((near[-size:].astype(jnp.bfloat16), sums.astype(jnp.bfloat16)))
    total = near[:size] + exchange(last, row).astype(jnp.float32)
    for slot in range(1, devices // 4):
        share = exchange(sums[(slot - 1) * size : slot * size], slot_distance(slot, columns))
        total = total + share.astype(jnp.float32)
    return total


def last_reduce(keep, *send):
    devices = lax.axis_size("rows")
    even, odd = last_orders(devices)
    near, other = add_cores(keep, *send)
    sums = near + exchange(other.astype(jnp.bfloat16), even[1], odd[1]).astype(jnp.float32)
    size = 2 * keep.shape[0] // devices
    sent = sums.astype(jnp.bfloat16)
    total = sums[:size]
    for slot in range(1, devices // 4):
        share = sent[slot * size : (slot + 1) * size]
        total = total + exchange(share, slot_distance(slot, even[2:]), slot_distance(slot, odd[2:])).astype(jnp.float32)
    return total


def packed_order(live):
    index = jnp.arange(live.shape[0])
    key = (live + live % 2 * (SLOTS + 1)) * live.shape[0] + index
    ahead = key[None, :] < key[:, None]
    rank = jnp.sum(ahead.astype(jnp.int32), axis=1)
    return jnp.sum(jnp.where(rank[:, None] == index[None, :], index[:, None], 0), axis=0).astype(jnp.int32)


def shrink(value, thresh):
    return value - jnp.clip(value, -thresh, thresh)


def local(dictionary, patches, initial_codes, support, counts, group_order, penalty):
    groups = group_order.shape[0]
    position = lax.axis_index("rows")
    devices = lax.axis_size("rows")
    momenta = momentum_list()
    pairs = MEAN_LIVE * groups // 2

    laid = initial_codes.reshape(SLOT_PAIRS, 2, PATCHES, BLOCK).transpose(0, 2, 1, 3)
    laid = laid.reshape(SLOT_PAIRS * PATCHES, LANES)
    live = jnp.sum(jnp.where(group_order[:, None] == jnp.arange(groups)[None, :], counts[None, :], 0), axis=1)
    own = position.astype(jnp.int32).reshape(1)
    scalars = jnp.concatenate([packed_order(live), group_order, counts, support.reshape(groups * SLOTS), own])
    collect = functools.partial(collect_support, scalars, groups, dictionary, pairs)
    gathered, (blocks,) = gather_shards(laid, [functools.partial(collect, part) for part in range(SUPPORT_PARTS)])

    targets = patches.T
    half_penalty = 0.5 * penalty
    thresh_tiles = jnp.broadcast_to(half_penalty[:, :, None], (groups, PATCHES, LANES))

    run = functools.partial(
        gradient_call, shards=devices, pairs=pairs, groups=groups, scalars=scalars, blocks=blocks, targets=targets
    )
    *shares, start, thresh = run("first", gathered=gathered, extra=(thresh_tiles,))
    point = previous = start.astype(jnp.float32)
    for turn in range(ITERS - 1):
        if turn:
            shares = run("packed", gathered=gathered)
        current = shrink(point - 0.5 * reduce_shards(*shares), thresh)
        point = current + momenta[turn] * (current - previous)
        previous = current
        gathered, _ = gather_shards(point.astype(jnp.bfloat16))
    *shares, sent, thresh = run("final", gathered=gathered, extra=(thresh_tiles,))
    gradient = last_reduce(*shares).reshape(SLOT_PAIRS, PATCHES, LANES)
    sent = sent.astype(jnp.float32)
    result = shrink(sent - 0.5 * gradient, thresh[None])
    result = result.reshape(SLOT_PAIRS, PATCHES, 2, BLOCK).transpose(0, 2, 1, 3)
    return result.reshape(1, SLOTS, PATCHES * BLOCK)


def solution(mesh):
    in_specs = (
        P("rows", None),
        P("rows", "groups"),
        P(("groups", "rows"), None, None),
        P("groups", None),
        P("groups"),
        P("groups"),
        P("groups", None),
    )
    out_specs = P(("groups", "rows"), None, None)
    return jax.shard_map(local, mesh=mesh, in_specs=in_specs, out_specs=out_specs, check_vma=False)
```

```python
import functools
import math

import jax
import jax.numpy as jnp
from jax import lax
from jax.experimental import pallas as pl
from jax.experimental.pallas import tpu as pltpu
from jax.sharding import PartitionSpec as P

BLOCK = 64
SLOTS = 16
PATCHES = 64
ITERS = 3
MEAN_LIVE = 10
LANES = 2 * BLOCK
SLOT_PAIRS = SLOTS // 2
SPARE = SLOT_PAIRS + 2
ROW_TILE = 16
SUPPORT_PARTS = 2
SUPPORT_STEP = 4
PIECE = 5
MATRIX_UNIT = 256
VMEM_MARGIN = 3 * 1024 * 1024
SUPPORT_VMEM = 40 * 1024 * 1024
HELD_BYTES = 65 * 1024 * 1024


def momentum_list():
    values = []
    tvalue = 1.0
    for turn in range(ITERS):
        tnext = (1.0 + (1.0 + 4.0 * tvalue * tvalue) ** 0.5) / 2.0
        values.append((tvalue - 1.0) / tnext)
        tvalue = tnext
    return values


def swap_halves(value):
    return jnp.concatenate([value[:, BLOCK:], value[:, :BLOCK]], axis=1)


def upper_half(shape):
    return lax.broadcasted_iota(jnp.int32, shape, 1) >= BLOCK


class Part:
    def __init__(self, ref, begin, width=1):
        self.ref, self.begin, self.width = ref, begin, width

    def __getitem__(self, index):
        if isinstance(index, tuple):
            index = index[0] * self.width + index[1]
        return self.ref[self.begin + index]


def scalar_parts(scalars, groups):
    seq, order, counts = (Part(scalars, part * groups) for part in range(3))
    return seq, order, counts, Part(scalars, 3 * groups, SLOTS), scalars[groups * (3 + SLOTS)]


def group_at(index, seq, order, counts):
    position = seq[index]
    group = order[position]
    return position, group, counts[group]


def support_kernel(begin, groups, scalars, dictionary, *refs):
    out, held, picks, ids, sems, out_sems = refs[-6:]
    seq, order, counts, support, _ = scalar_parts(scalars, groups)
    entries, rows, _ = held.shape
    pairs = entries // 2

    def fetch(entry, block):
        start = pl.multiple_of((block // 2) * LANES, LANES)
        return pltpu.make_async_copy(dictionary.at[:, pl.ds(start, LANES)], held.at[entry], sems.at[entry])

    def start_group(index, offset):
        _, group, live = group_at(index, seq, order, counts)

        def start_slot(slot, carry):
            block = support[group, slot]
            ids[offset + slot] = block
            fetch(offset + slot, block).start()
            return carry

        lax.fori_loop(jnp.clip(-offset, 0, live), jnp.clip(entries - offset, 0, live), start_slot, 0)
        return offset + live

    lax.fori_loop(0, groups, start_group, jnp.int32(-begin))
    steps = pairs // SUPPORT_STEP
    shape = (2 * LANES, LANES)
    source = lax.broadcasted_iota(jnp.int32, shape, 0)
    target = lax.broadcasted_iota(jnp.int32, shape, 1)
    for choice in range(4):
        wanted = jnp.where(target < BLOCK, (choice % 2) * BLOCK + target, LANES + (choice // 2) * BLOCK + target - BLOCK)
        picks[choice] = (source == wanted).astype(jnp.float32).astype(jnp.bfloat16)

    def store(pair):
        return pltpu.make_async_copy(held.at[2 * pair], out.at[begin // 2 + pair], out_sems.at[pair])

    def pack(step, carry):
        span = [SUPPORT_STEP * step + pair for pair in range(SUPPORT_STEP)]
        for pair in span:
            fetch(2 * pair, ids[2 * pair]).wait()
            fetch(2 * pair + 1, ids[2 * pair + 1]).wait()
        packed = []
        for pair in span:
            choice = ids[2 * pair] % 2 + 2 * (ids[2 * pair + 1] % 2)
            both = jnp.concatenate([held[2 * pair], held[2 * pair + 1]], axis=1)
            packed.append(jnp.dot(both, picks[choice], preferred_element_type=jnp.float32).astype(jnp.bfloat16))
        for pair, value in zip(span, packed):
            held[2 * pair] = value
            store(pair).start()
        return carry

    lax.fori_loop(0, steps, pack, 0)

    def drain(pair, carry):
        store(pair).wait()
        return carry

    lax.fori_loop(0, pairs, drain, 0)


def collect_support(scalars, groups, dictionary, pairs, part, *before):
    rows = dictionary.shape[0]
    pairs = pairs // SUPPORT_PARTS
    entries = 2 * pairs
    return pl.pallas_call(
        functools.partial(support_kernel, part * entries, groups),
        grid_spec=pltpu.PrefetchScalarGridSpec(
            num_scalar_prefetch=1,
            grid=(),
            in_specs=[pl.BlockSpec(memory_space=pltpu.HBM)] * (1 + len(before)),
            out_specs=pl.BlockSpec(memory_space=pltpu.HBM),
            scratch_shapes=[
                pltpu.VMEM((entries, rows, LANES), dictionary.dtype),
                pltpu.VMEM((4, 2 * LANES, LANES), jnp.bfloat16),
                pltpu.SMEM((entries,), jnp.int32),
                pltpu.SemaphoreType.DMA((entries,)),
                pltpu.SemaphoreType.DMA((pairs,)),
            ],
        ),
        out_shape=jax.ShapeDtypeStruct((HELD_BYTES // (rows * LANES * 2), rows, LANES), dictionary.dtype),
        compiler_params=pltpu.CompilerParams(vmem_limit_bytes=SUPPORT_VMEM),
        cost_estimate=pl.CostEstimate(flops=0, transcendentals=0, bytes_accessed=6 * pairs * rows * LANES * 2),
        input_output_aliases={2: 0} if before else {},
        name="collect_support",
    )(scalars, dictionary, *before)


def stage_distances(devices):
    return [2**bit for bit in range(devices.bit_length() - 1)]


def reduce_orders(devices):
    distances = stage_distances(devices)
    return distances, distances[:1] + distances[2:] + distances[1:2]


def slot_distance(slot, distances):
    bits = reversed(range(len(distances)))
    return sum(distance for bit, distance in zip(bits, distances) if slot >> bit & 1)


def gradient_kernel(mode, shards, pairs, groups, scalars, blocks, *refs):
    seq, order, counts, _, me = scalar_parts(scalars, groups)
    refs = list(refs)
    take = lambda: refs.pop(0)
    gathered, targets = [take() for _ in range(4)], take()
    if mode in ("first", "final"):
        thresh = take()
    keep, send = take(), (take(), take())
    if mode == "first":
        start_out, thresh_out = take(), take()
    if mode == "final":
        sent, thresh_out = take(), take()
    held, codes, total = take(), take(), take()
    if mode == "first":
        starts, limits = take(), take()
    offsets, sems = refs

    pieces = pairs // PIECE

    def load(index):
        span = pl.ds(index * PIECE, PIECE)
        return pltpu.make_async_copy(blocks.at[span], held.at[span], sems.at[index])

    for index in range(pieces):
        load(index).start()
    held[pairs:] = jnp.zeros((SPARE,) + held.shape[1:], held.dtype)

    distances = stage_distances(shards)

    def shard_span(slot, size):
        return pl.ds(pl.multiple_of((slot_distance(slot, distances) ^ me) * size, ROW_TILE), size)

    def reduce_holder(slot):
        even, odd = (slot_distance(slot, order) for order in reduce_orders(shards))
        if slot >= shards // 2:
            even, odd = odd, even
        return jnp.where(me % 2 == 0, even, odd) ^ me

    quarter = shards // 4
    size_in = gathered[0].shape[0] // (quarter + 1)
    for slot in range(shards):
        half, inside = divmod(slot, 2 * quarter)
        second = inside > quarter
        begin = (inside - (quarter + 1) * second) * size_in
        codes[shard_span(slot, size_in), :] = gathered[2 * half + second][begin : begin + size_in, :]

    def put(slot, size, begin, value):
        far, inside = divmod(slot, 2 * quarter)
        if far:
            ahead = send[0].shape[0] // size
            second = inside >= ahead
            start = (inside - ahead * second) * size + begin
            send[second][start : start + value.shape[0], :] = value.astype(jnp.bfloat16)
        else:
            start = inside * size + begin
            keep[start : start + value.shape[0], :] = value

    def seat(index, offset):
        position, _, live = group_at(index, seq, order, counts)
        offsets[position] = offset
        return offset + live

    lax.fori_loop(0, groups, seat, jnp.int32(0))

    upper = upper_half((PATCHES, LANES))
    side = upper.astype(jnp.int32)

    def tile(pair):
        return pl.ds(pl.multiple_of(pair * PATCHES, PATCHES), PATCHES)

    def shifted(parts, count, odd, ahead):
        turned = [swap_halves(part) for part in parts]
        last = len(parts) - 1
        moved = []
        for pair in range(count):
            low, high = (pair, pair + 1) if ahead else (pair - 1, pair)
            low, high = min(max(low, 0), last), min(max(high, 0), last)
            value = jnp.where(upper[: turned[low].shape[0]], turned[high], turned[low])
            moved.append(jnp.where(odd, value, parts[min(pair, last)]))
        return moved

    def read_codes(position, offset, live, count):
        first = offset // 2
        if mode == "first":
            parts = [codes[tile(position * SLOT_PAIRS + pair), :] for pair in range(min(count, SLOT_PAIRS))]
            parts = shifted(parts, count, offset % 2 == 1, False)
        else:
            parts = [codes[tile(first + pair), :] for pair in range(count)]
        masked = []
        for pair, part in enumerate(parts):
            entry = 2 * (first + pair) + side
            mine = (entry >= offset) & (entry < offset + live)
            masked.append(jnp.where(mine, part, jnp.zeros_like(part)))
        return masked

    def write_packed(ref, parts, offset):
        first = offset // 2
        for pair, part in enumerate(parts):
            if pair == 0:
                part = jnp.where(upper | (offset % 2 == 0), part, ref[tile(first), :])
            ref[tile(first + pair), :] = part

    def one_group(position, group, offset, live, count):
        first = offset // 2
        parts = read_codes(position, offset, live, count)
        if mode == "first":
            write_packed(starts, parts, offset)
            write_packed(limits, [thresh[group]] * count, offset)
        matrix = jnp.concatenate([held[first + pair] for pair in range(count)], axis=1)
        point = jnp.concatenate(parts, axis=1)
        residual = lax.dot_general(point, matrix, (((1,), (1,)), ((), ())), preferred_element_type=jnp.float32)
        target = targets[tile(group), :].astype(jnp.float32)
        residual = (residual - target).astype(jnp.bfloat16)
        gradient = jnp.dot(residual, matrix, preferred_element_type=jnp.float32)
        write_packed(total, [gradient[:, pair * LANES : (pair + 1) * LANES] for pair in range(count)], offset)

    def wait_piece(index, carry):
        load(index).wait()
        return carry

    def two_groups(step, waited):
        picks = []
        count_needed = 1
        for index in (2 * step, 2 * step + 1):
            position, group, live = group_at(index, seq, order, counts)
            offset = offsets[position]
            picks.append((position, group, offset, live))
            count_needed = jnp.maximum(count_needed, (live + offset % 2 + 1) // 2)
        reach = jnp.minimum(picks[1][2] // 2 + count_needed - 1, pairs - 1)
        needed = jnp.maximum(reach // PIECE + 1, waited)
        lax.fori_loop(waited, needed, wait_piece, 0)
        for count in range(1, SLOT_PAIRS + 2):

            @pl.when(count_needed == count)
            def _(count=count):
                for pick in picks:
                    one_group(*pick, count)

        return needed

    waited = lax.fori_loop(0, groups // 2, two_groups, jnp.int32(0))
    lax.fori_loop(waited, pieces, wait_piece, 0)

    if mode != "final":
        size = 2 * keep.shape[0] // shards
        for slot in range(shards):
            put(slot, size, 0, total[pl.ds(pl.multiple_of(reduce_holder(slot) * size, ROW_TILE), size), :])
    if mode == "first":
        size = start_out.shape[0]
        span = pl.ds(pl.multiple_of(me * size, ROW_TILE), size)
        start_out[...] = starts[span, :]
        thresh_out[...] = limits[span, :]
    if mode == "final":
        offset = offsets[me]
        parts = read_codes(me, offset, counts[order[me]], SLOT_PAIRS + 1)
        for pair, part in enumerate(shifted(parts, SLOT_PAIRS, offset % 2 == 1, True)):
            sent[pair] = part
        thresh_out[...] = thresh[order[me]]
        for slot in range(shards):
            position = reduce_holder(slot)
            offset = offsets[position]
            live = counts[order[position]]
            parts = [total[tile(offset // 2 + pair), :] for pair in range(SLOT_PAIRS + 1)]
            for pair, part in enumerate(shifted(parts, SLOT_PAIRS, offset % 2 == 1, True)):
                value = jnp.where(2 * pair + side < live, part, 0.0)
                put(slot, SLOT_PAIRS * PATCHES, pair * PATCHES, value)


def gradient_call(mode, shards, pairs, groups, scalars, blocks, gathered, targets, extra=()):
    rows = blocks.shape[1]
    places = pairs + SPARE
    single, double = jnp.bfloat16, jnp.float32
    packed = (places * PATCHES, LANES)
    half_out = (groups * SLOT_PAIRS if mode == "final" else pairs) * PATCHES // 2
    shard = (2 * half_out // shards, LANES)
    outs = [((half_out, LANES), double)] + [((half_out // 2, LANES), single)] * 2
    if mode == "first":
        outs += [(shard, single), (shard, double)]
    if mode == "final":
        outs += [((SLOT_PAIRS, PATCHES, LANES), single), ((PATCHES, LANES), double)]
    codes = groups * SLOT_PAIRS * PATCHES if mode == "first" else packed[0]
    scratch = [((places, rows, LANES), single), ((codes, LANES), single), (packed, double)]
    if mode == "first":
        scratch += [(packed, single), (packed, double)]
    room = sum(math.prod(shape) * jnp.dtype(kind).itemsize for shape, kind in scratch)
    return pl.pallas_call(
        functools.partial(gradient_kernel, mode, shards, pairs, groups),
        grid_spec=pltpu.PrefetchScalarGridSpec(
            num_scalar_prefetch=1,
            grid=(),
            in_specs=[pl.BlockSpec(memory_space=pltpu.HBM)]
            + [pl.BlockSpec(memory_space=pltpu.VMEM)] * (5 + len(extra)),
            out_specs=[pl.BlockSpec(memory_space=pltpu.VMEM)] * len(outs),
            scratch_shapes=[pltpu.VMEM(shape, kind) for shape, kind in scratch]
            + [pltpu.SMEM((groups,), jnp.int32), pltpu.SemaphoreType.DMA((pairs // PIECE,))],
        ),
        out_shape=[jax.ShapeDtypeStruct(shape, kind) for shape, kind in outs],
        compiler_params=pltpu.CompilerParams(vmem_limit_bytes=room + VMEM_MARGIN),
        cost_estimate=pl.CostEstimate(
            flops=4 * pairs * rows * LANES * MATRIX_UNIT, transcendentals=0, bytes_accessed=pairs * rows * LANES * 2
        ),
        name="gradient",
    )(scalars, blocks, *gathered, targets, *extra)


def exchange(value, even, odd=None):
    devices = lax.axis_size("rows")
    apart = (even, even if odd is None else odd)
    return lax.ppermute(value, "rows", [(i, i ^ apart[i % 2]) for i in range(devices)])


def gather_shards(own, beside=()):
    core, row, *columns = stage_distances(lax.axis_size("rows"))
    apart = [slot_distance(slot, columns) for slot in range(lax.axis_size("rows") // 4)]
    made = ()
    near = jnp.concatenate([own] + [exchange(own, distance) for distance in apart[1:] + [row]], axis=0)
    if beside:
        near, *made = lax.optimization_barrier((near, beside[0]()))
    other = exchange(near[own.shape[0] : len(apart) * own.shape[0]], row)
    far = exchange(near, core)
    if beside:
        other, *made = lax.optimization_barrier((other, beside[1](*made)))
    return (near, other, far, exchange(other, core)), made


def add_cores(keep, *send):
    ahead = send[0].shape[0]
    after = keep[ahead:] + exchange(send[1], 1).astype(jnp.float32)
    return keep[:ahead] + exchange(send[0], 1).astype(jnp.float32), after


def reduce_shards(keep, *send):
    devices = lax.axis_size("rows")
    even, odd = reduce_orders(devices)
    near, other = add_cores(keep, *send)
    sums = near + exchange(other.astype(jnp.bfloat16), even[1], odd[1]).astype(jnp.float32)
    size = 2 * keep.shape[0] // devices
    sent = sums.astype(jnp.bfloat16)
    total = sums[:size]
    for slot in range(1, devices // 4):
        share = sent[slot * size : (slot + 1) * size]
        total = total + exchange(share, slot_distance(slot, even[2:]), slot_distance(slot, odd[2:])).astype(jnp.float32)
    return total


def packed_order(live):
    index = jnp.arange(live.shape[0])
    key = (live + live % 2 * (SLOTS + 1)) * live.shape[0] + index
    ahead = key[None, :] < key[:, None]
    rank = jnp.sum(ahead.astype(jnp.int32), axis=1)
    return jnp.sum(jnp.where(rank[:, None] == index[None, :], index[:, None], 0), axis=0).astype(jnp.int32)


def shrink(value, thresh):
    return value - jnp.clip(value, -thresh, thresh)


def local(dictionary, patches, initial_codes, support, counts, group_order, penalty):
    groups = group_order.shape[0]
    position = lax.axis_index("rows")
    devices = lax.axis_size("rows")
    momenta = momentum_list()
    pairs = MEAN_LIVE * groups // 2

    laid = initial_codes.reshape(SLOT_PAIRS, 2, PATCHES, BLOCK).transpose(0, 2, 1, 3)
    laid = laid.reshape(SLOT_PAIRS * PATCHES, LANES)
    live = jnp.sum(jnp.where(group_order[:, None] == jnp.arange(groups)[None, :], counts[None, :], 0), axis=1)
    own = position.astype(jnp.int32).reshape(1)
    scalars = jnp.concatenate([packed_order(live), group_order, counts, support.reshape(groups * SLOTS), own])
    collect = functools.partial(collect_support, scalars, groups, dictionary, pairs)
    gathered, (blocks,) = gather_shards(laid, [functools.partial(collect, part) for part in range(SUPPORT_PARTS)])

    targets = patches.T
    half_penalty = 0.5 * penalty
    thresh_tiles = jnp.broadcast_to(half_penalty[:, :, None], (groups, PATCHES, LANES))

    run = functools.partial(
        gradient_call, shards=devices, pairs=pairs, groups=groups, scalars=scalars, blocks=blocks, targets=targets
    )
    *shares, start, thresh = run("first", gathered=gathered, extra=(thresh_tiles,))
    point = previous = start.astype(jnp.float32)
    for turn in range(ITERS - 1):
        if turn:
            shares = run("packed", gathered=gathered)
        current = shrink(point - 0.5 * reduce_shards(*shares), thresh)
        point = current + momenta[turn] * (current - previous)
        previous = current
        gathered, _ = gather_shards(point.astype(jnp.bfloat16))
    *shares, sent, thresh = run("final", gathered=gathered, extra=(thresh_tiles,))
    gradient = reduce_shards(*shares).reshape(SLOT_PAIRS, PATCHES, LANES)
    sent = sent.astype(jnp.float32)
    result = shrink(sent - 0.5 * gradient, thresh[None])
    result = result.reshape(SLOT_PAIRS, PATCHES, 2, BLOCK).transpose(0, 2, 1, 3)
    return result.reshape(1, SLOTS, PATCHES * BLOCK)


def solution(mesh):
    in_specs = (
        P("rows", None),
        P("rows", "groups"),
        P(("groups", "rows"), None, None),
        P("groups", None),
        P("groups"),
        P("groups"),
        P("groups", None),
    )
    out_specs = P(("groups", "rows"), None, None)
    return jax.shard_map(local, mesh=mesh, in_specs=in_specs, out_specs=out_specs, check_vma=False)
```

```python
import functools
import math

import jax
import jax.numpy as jnp
from jax import lax
from jax.experimental import pallas as pl
from jax.experimental.pallas import tpu as pltpu
from jax.sharding import PartitionSpec as P

BLOCK = 64
SLOTS = 16
PATCHES = 64
ITERS = 3
MEAN_LIVE = 10
LANES = 2 * BLOCK
SLOT_PAIRS = SLOTS // 2
SPARE = SLOT_PAIRS + 2
ROW_TILE = 16
SUPPORT_PARTS = 2
SUPPORT_STEP = 4
PIECE = 5
MATRIX_UNIT = 256
VMEM_MARGIN = 3 * 1024 * 1024
SUPPORT_VMEM = 40 * 1024 * 1024
HELD_BYTES = 65 * 1024 * 1024


def momentum_list():
    values = []
    tvalue = 1.0
    for turn in range(ITERS):
        tnext = (1.0 + (1.0 + 4.0 * tvalue * tvalue) ** 0.5) / 2.0
        values.append((tvalue - 1.0) / tnext)
        tvalue = tnext
    return values


def swap_halves(value):
    return jnp.concatenate([value[:, BLOCK:], value[:, :BLOCK]], axis=1)


def upper_half(shape):
    return lax.broadcasted_iota(jnp.int32, shape, 1) >= BLOCK


class Part:
    def __init__(self, ref, begin, width=1):
        self.ref, self.begin, self.width = ref, begin, width

    def __getitem__(self, index):
        if isinstance(index, tuple):
            index = index[0] * self.width + index[1]
        return self.ref[self.begin + index]


def scalar_parts(scalars, groups):
    seq, order, counts = (Part(scalars, part * groups) for part in range(3))
    return seq, order, counts, Part(scalars, 3 * groups, SLOTS), scalars[groups * (3 + SLOTS)]


def group_at(index, seq, order, counts):
    position = seq[index]
    group = order[position]
    return position, group, counts[group]


def support_kernel(begin, groups, scalars, dictionary, *refs):
    out, held, picks, ids, sems, out_sems = refs[-6:]
    seq, order, counts, support, _ = scalar_parts(scalars, groups)
    entries, rows, _ = held.shape
    pairs = entries // 2

    def fetch(entry, block):
        start = pl.multiple_of((block // 2) * LANES, LANES)
        return pltpu.make_async_copy(dictionary.at[:, pl.ds(start, LANES)], held.at[entry], sems.at[entry])

    def start_group(index, offset):
        _, group, live = group_at(index, seq, order, counts)

        def start_slot(slot, carry):
            block = support[group, slot]
            ids[offset + slot] = block
            fetch(offset + slot, block).start()
            return carry

        lax.fori_loop(jnp.clip(-offset, 0, live), jnp.clip(entries - offset, 0, live), start_slot, 0)
        return offset + live

    lax.fori_loop(0, groups, start_group, jnp.int32(-begin))
    steps = pairs // SUPPORT_STEP
    shape = (2 * LANES, LANES)
    source = lax.broadcasted_iota(jnp.int32, shape, 0)
    target = lax.broadcasted_iota(jnp.int32, shape, 1)
    for choice in range(4):
        wanted = jnp.where(target < BLOCK, (choice % 2) * BLOCK + target, LANES + (choice // 2) * BLOCK + target - BLOCK)
        picks[choice] = (source == wanted).astype(jnp.float32).astype(jnp.bfloat16)

    def store(pair):
        return pltpu.make_async_copy(held.at[2 * pair], out.at[begin // 2 + pair], out_sems.at[pair])

    def pack(step, carry):
        span = [SUPPORT_STEP * step + pair for pair in range(SUPPORT_STEP)]
        for pair in span:
            fetch(2 * pair, ids[2 * pair]).wait()
            fetch(2 * pair + 1, ids[2 * pair + 1]).wait()
        packed = []
        for pair in span:
            choice = ids[2 * pair] % 2 + 2 * (ids[2 * pair + 1] % 2)
            both = jnp.concatenate([held[2 * pair], held[2 * pair + 1]], axis=1)
            packed.append(jnp.dot(both, picks[choice], preferred_element_type=jnp.float32).astype(jnp.bfloat16))
        for pair, value in zip(span, packed):
            held[2 * pair] = value
            store(pair).start()
        return carry

    lax.fori_loop(0, steps, pack, 0)

    def drain(pair, carry):
        store(pair).wait()
        return carry

    lax.fori_loop(0, pairs, drain, 0)


def collect_support(scalars, groups, dictionary, pairs, part, *before):
    rows = dictionary.shape[0]
    pairs = pairs // SUPPORT_PARTS
    entries = 2 * pairs
    return pl.pallas_call(
        functools.partial(support_kernel, part * entries, groups),
        grid_spec=pltpu.PrefetchScalarGridSpec(
            num_scalar_prefetch=1,
            grid=(),
            in_specs=[pl.BlockSpec(memory_space=pltpu.HBM)] * (1 + len(before)),
            out_specs=pl.BlockSpec(memory_space=pltpu.HBM),
            scratch_shapes=[
                pltpu.VMEM((entries, rows, LANES), dictionary.dtype),
                pltpu.VMEM((4, 2 * LANES, LANES), jnp.bfloat16),
                pltpu.SMEM((entries,), jnp.int32),
                pltpu.SemaphoreType.DMA((entries,)),
                pltpu.SemaphoreType.DMA((pairs,)),
            ],
        ),
        out_shape=jax.ShapeDtypeStruct((HELD_BYTES // (rows * LANES * 2), rows, LANES), dictionary.dtype),
        compiler_params=pltpu.CompilerParams(vmem_limit_bytes=SUPPORT_VMEM),
        cost_estimate=pl.CostEstimate(flops=0, transcendentals=0, bytes_accessed=6 * pairs * rows * LANES * 2),
        input_output_aliases={2: 0} if before else {},
        name="collect_support",
    )(scalars, dictionary, *before)


def stage_distances(devices):
    return [2**bit for bit in range(devices.bit_length() - 1)]


def last_orders(devices):
    distances = stage_distances(devices)
    return distances, distances[:1] + distances[2:] + distances[1:2]


def slot_distance(slot, distances):
    bits = reversed(range(len(distances)))
    return sum(distance for bit, distance in zip(bits, distances) if slot >> bit & 1)


def gradient_kernel(mode, shards, pairs, groups, scalars, blocks, *refs):
    seq, order, counts, _, me = scalar_parts(scalars, groups)
    refs = list(refs)
    take = lambda: refs.pop(0)
    gathered, targets = [take() for _ in range(4)], take()
    if mode in ("first", "final"):
        thresh = take()
    keep, send = take(), (take(), take())
    if mode == "first":
        start_out, thresh_out = take(), take()
    if mode == "final":
        sent, thresh_out = take(), take()
    held, codes, total = take(), take(), take()
    if mode == "first":
        starts, limits = take(), take()
    offsets, sems = refs

    pieces = pairs // PIECE

    def load(index):
        span = pl.ds(index * PIECE, PIECE)
        return pltpu.make_async_copy(blocks.at[span], held.at[span], sems.at[index])

    for index in range(pieces):
        load(index).start()
    held[pairs:] = jnp.zeros((SPARE,) + held.shape[1:], held.dtype)

    distances = stage_distances(shards)

    def shard_span(slot, size):
        return pl.ds(pl.multiple_of((slot_distance(slot, distances) ^ me) * size, ROW_TILE), size)

    def last_holder(slot):
        even, odd = (slot_distance(slot, order) for order in last_orders(shards))
        if slot >= shards // 2:
            even, odd = odd, even
        return jnp.where(me % 2 == 0, even, odd) ^ me

    quarter = shards // 4
    size_in = gathered[0].shape[0] // (quarter + 1)
    for slot in range(shards):
        half, inside = divmod(slot, 2 * quarter)
        second = inside > quarter
        begin = (inside - (quarter + 1) * second) * size_in
        codes[shard_span(slot, size_in), :] = gathered[2 * half + second][begin : begin + size_in, :]

    def put(slot, size, begin, value):
        far, inside = divmod(slot, 2 * quarter)
        if far:
            ahead = send[0].shape[0] // size
            second = inside >= ahead
            start = (inside - ahead * second) * size + begin
            send[second][start : start + value.shape[0], :] = value.astype(jnp.bfloat16)
        else:
            start = inside * size + begin
            keep[start : start + value.shape[0], :] = value

    def seat(index, offset):
        position, _, live = group_at(index, seq, order, counts)
        offsets[position] = offset
        return offset + live

    lax.fori_loop(0, groups, seat, jnp.int32(0))

    upper = upper_half((PATCHES, LANES))
    side = upper.astype(jnp.int32)

    def tile(pair):
        return pl.ds(pl.multiple_of(pair * PATCHES, PATCHES), PATCHES)

    def shifted(parts, count, odd, ahead):
        turned = [swap_halves(part) for part in parts]
        last = len(parts) - 1
        moved = []
        for pair in range(count):
            low, high = (pair, pair + 1) if ahead else (pair - 1, pair)
            low, high = min(max(low, 0), last), min(max(high, 0), last)
            value = jnp.where(upper[: turned[low].shape[0]], turned[high], turned[low])
            moved.append(jnp.where(odd, value, parts[min(pair, last)]))
        return moved

    def read_codes(position, offset, live, count):
        first = offset // 2
        if mode == "first":
            parts = [codes[tile(position * SLOT_PAIRS + pair), :] for pair in range(min(count, SLOT_PAIRS))]
            parts = shifted(parts, count, offset % 2 == 1, False)
        else:
            parts = [codes[tile(first + pair), :] for pair in range(count)]
        masked = []
        for pair, part in enumerate(parts):
            entry = 2 * (first + pair) + side
            mine = (entry >= offset) & (entry < offset + live)
            masked.append(jnp.where(mine, part, jnp.zeros_like(part)))
        return masked

    def write_packed(ref, parts, offset):
        first = offset // 2
        for pair, part in enumerate(parts):
            if pair == 0:
                part = jnp.where(upper | (offset % 2 == 0), part, ref[tile(first), :])
            ref[tile(first + pair), :] = part

    def one_group(position, group, offset, live, count):
        first = offset // 2
        parts = read_codes(position, offset, live, count)
        if mode == "first":
            write_packed(starts, parts, offset)
            write_packed(limits, [thresh[group]] * count, offset)
        matrix = jnp.concatenate([held[first + pair] for pair in range(count)], axis=1)
        point = jnp.concatenate(parts, axis=1)
        residual = lax.dot_general(point, matrix, (((1,), (1,)), ((), ())), preferred_element_type=jnp.float32)
        target = targets[tile(group), :].astype(jnp.float32)
        residual = (residual - target).astype(jnp.bfloat16)
        gradient = jnp.dot(residual, matrix, preferred_element_type=jnp.float32)
        write_packed(total, [gradient[:, pair * LANES : (pair + 1) * LANES] for pair in range(count)], offset)

    def wait_piece(index, carry):
        load(index).wait()
        return carry

    def two_groups(step, waited):
        picks = []
        count_needed = 1
        for index in (2 * step, 2 * step + 1):
            position, group, live = group_at(index, seq, order, counts)
            offset = offsets[position]
            picks.append((position, group, offset, live))
            count_needed = jnp.maximum(count_needed, (live + offset % 2 + 1) // 2)
        reach = jnp.minimum(picks[1][2] // 2 + count_needed - 1, pairs - 1)
        needed = jnp.maximum(reach // PIECE + 1, waited)
        lax.fori_loop(waited, needed, wait_piece, 0)
        for count in range(1, SLOT_PAIRS + 2):

            @pl.when(count_needed == count)
            def _(count=count):
                for pick in picks:
                    one_group(*pick, count)

        return needed

    waited = lax.fori_loop(0, groups // 2, two_groups, jnp.int32(0))
    lax.fori_loop(waited, pieces, wait_piece, 0)

    if mode != "final":
        size = 2 * keep.shape[0] // shards
        for slot in range(shards):
            put(slot, size, 0, total[shard_span(slot, size), :])
    if mode == "first":
        size = start_out.shape[0]
        span = pl.ds(pl.multiple_of(me * size, ROW_TILE), size)
        start_out[...] = starts[span, :]
        thresh_out[...] = limits[span, :]
    if mode == "final":
        offset = offsets[me]
        parts = read_codes(me, offset, counts[order[me]], SLOT_PAIRS + 1)
        for pair, part in enumerate(shifted(parts, SLOT_PAIRS, offset % 2 == 1, True)):
            sent[pair] = part
        thresh_out[...] = thresh[order[me]]
        for slot in range(shards):
            position = last_holder(slot)
            offset = offsets[position]
            live = counts[order[position]]
            parts = [total[tile(offset // 2 + pair), :] for pair in range(SLOT_PAIRS + 1)]
            for pair, part in enumerate(shifted(parts, SLOT_PAIRS, offset % 2 == 1, True)):
                value = jnp.where(2 * pair + side < live, part, 0.0)
                put(slot, SLOT_PAIRS * PATCHES, pair * PATCHES, value)


def gradient_call(mode, shards, pairs, groups, scalars, blocks, gathered, targets, extra=()):
    rows = blocks.shape[1]
    places = pairs + SPARE
    single, double = jnp.bfloat16, jnp.float32
    packed = (places * PATCHES, LANES)
    half_out = (groups * SLOT_PAIRS if mode == "final" else pairs) * PATCHES // 2
    shard = (2 * half_out // shards, LANES)
    ahead = half_out // 2 + (0 if mode == "final" else shard[0])
    outs = [((half_out, LANES), double), ((ahead, LANES), single), ((half_out - ahead, LANES), single)]
    if mode == "first":
        outs += [(shard, single), (shard, double)]
    if mode == "final":
        outs += [((SLOT_PAIRS, PATCHES, LANES), single), ((PATCHES, LANES), double)]
    codes = groups * SLOT_PAIRS * PATCHES if mode == "first" else packed[0]
    scratch = [((places, rows, LANES), single), ((codes, LANES), single), (packed, double)]
    if mode == "first":
        scratch += [(packed, single), (packed, double)]
    room = sum(math.prod(shape) * jnp.dtype(kind).itemsize for shape, kind in scratch)
    return pl.pallas_call(
        functools.partial(gradient_kernel, mode, shards, pairs, groups),
        grid_spec=pltpu.PrefetchScalarGridSpec(
            num_scalar_prefetch=1,
            grid=(),
            in_specs=[pl.BlockSpec(memory_space=pltpu.HBM)]
            + [pl.BlockSpec(memory_space=pltpu.VMEM)] * (5 + len(extra)),
            out_specs=[pl.BlockSpec(memory_space=pltpu.VMEM)] * len(outs),
            scratch_shapes=[pltpu.VMEM(shape, kind) for shape, kind in scratch]
            + [pltpu.SMEM((groups,), jnp.int32), pltpu.SemaphoreType.DMA((pairs // PIECE,))],
        ),
        out_shape=[jax.ShapeDtypeStruct(shape, kind) for shape, kind in outs],
        compiler_params=pltpu.CompilerParams(vmem_limit_bytes=room + VMEM_MARGIN),
        cost_estimate=pl.CostEstimate(
            flops=4 * pairs * rows * LANES * MATRIX_UNIT, transcendentals=0, bytes_accessed=pairs * rows * LANES * 2
        ),
        name="gradient",
    )(scalars, blocks, *gathered, targets, *extra)


def exchange(value, even, odd=None):
    devices = lax.axis_size("rows")
    apart = (even, even if odd is None else odd)
    return lax.ppermute(value, "rows", [(i, i ^ apart[i % 2]) for i in range(devices)])


def gather_shards(own, beside=()):
    core, row, *columns = stage_distances(lax.axis_size("rows"))
    apart = [slot_distance(slot, columns) for slot in range(lax.axis_size("rows") // 4)]
    made = ()
    arrived = {distance: exchange(own, distance) for distance in sorted(apart[1:] + [row], reverse=True)}
    near = jnp.concatenate([own] + [arrived[distance] for distance in apart[1:] + [row]], axis=0)
    if beside:
        near, *made = lax.optimization_barrier((near, beside[0]()))
    other = exchange(near[own.shape[0] : len(apart) * own.shape[0]], row)
    far = exchange(near, core)
    if beside:
        other, *made = lax.optimization_barrier((other, beside[1](*made)))
    return (near, other, far, exchange(other, core)), made


def add_cores(keep, *send):
    ahead = send[0].shape[0]
    after = keep[ahead:] + exchange(send[1], 1).astype(jnp.float32)
    return keep[:ahead] + exchange(send[0], 1).astype(jnp.float32), after


def reduce_shards(keep, *send):
    devices = lax.axis_size("rows")
    _, row, *columns = stage_distances(devices)
    size = 2 * keep.shape[0] // devices
    near, other = add_cores(keep, *send)
    sums = near[size:-size] + exchange(other.astype(jnp.bfloat16), row).astype(jnp.float32)
    last, sums = lax.optimization_barrier((near[-size:].astype(jnp.bfloat16), sums.astype(jnp.bfloat16)))
    total = near[:size]
    for slot in sorted(range(1, devices // 4), key=lambda slot: -slot_distance(slot, columns)):
        share = exchange(sums[(slot - 1) * size : slot * size], slot_distance(slot, columns))
        total = total + share.astype(jnp.float32)
    return total + exchange(last, row).astype(jnp.float32)


def last_reduce(keep, *send):
    devices = lax.axis_size("rows")
    even, odd = last_orders(devices)
    near, other = add_cores(keep, *send)
    sums = near + exchange(other.astype(jnp.bfloat16), even[1], odd[1]).astype(jnp.float32)
    size = 2 * keep.shape[0] // devices
    sent = sums.astype(jnp.bfloat16)
    total = sums[:size]
    for slot in sorted(range(1, devices // 4), key=lambda slot: -slot_distance(slot, even[2:])):
        share = sent[slot * size : (slot + 1) * size]
        total = total + exchange(share, slot_distance(slot, even[2:]), slot_distance(slot, odd[2:])).astype(jnp.float32)
    return total


def packed_order(live):
    index = jnp.arange(live.shape[0])
    key = (live + live % 2 * (SLOTS + 1)) * live.shape[0] + index
    ahead = key[None, :] < key[:, None]
    rank = jnp.sum(ahead.astype(jnp.int32), axis=1)
    return jnp.sum(jnp.where(rank[:, None] == index[None, :], index[:, None], 0), axis=0).astype(jnp.int32)


def shrink(value, thresh):
    return value - jnp.clip(value, -thresh, thresh)


def local(dictionary, patches, initial_codes, support, counts, group_order, penalty):
    groups = group_order.shape[0]
    position = lax.axis_index("rows")
    devices = lax.axis_size("rows")
    momenta = momentum_list()
    pairs = MEAN_LIVE * groups // 2

    laid = initial_codes.reshape(SLOT_PAIRS, 2, PATCHES, BLOCK).transpose(0, 2, 1, 3)
    laid = laid.reshape(SLOT_PAIRS * PATCHES, LANES)
    live = jnp.sum(jnp.where(group_order[:, None] == jnp.arange(groups)[None, :], counts[None, :], 0), axis=1)
    own = position.astype(jnp.int32).reshape(1)
    scalars = jnp.concatenate([packed_order(live), group_order, counts, support.reshape(groups * SLOTS), own])
    collect = functools.partial(collect_support, scalars, groups, dictionary, pairs)
    gathered, (blocks,) = gather_shards(laid, [functools.partial(collect, part) for part in range(SUPPORT_PARTS)])

    targets = patches.T
    half_penalty = 0.5 * penalty
    thresh_tiles = jnp.broadcast_to(half_penalty[:, :, None], (groups, PATCHES, LANES))

    run = functools.partial(
        gradient_call, shards=devices, pairs=pairs, groups=groups, scalars=scalars, blocks=blocks, targets=targets
    )
    *shares, start, thresh = run("first", gathered=gathered, extra=(thresh_tiles,))
    point = previous = start.astype(jnp.float32)
    for turn in range(ITERS - 1):
        if turn:
            shares = run("packed", gathered=gathered)
        current = shrink(point - 0.5 * reduce_shards(*shares), thresh)
        point = current + momenta[turn] * (current - previous)
        previous = current
        gathered, _ = gather_shards(point.astype(jnp.bfloat16))
    *shares, sent, thresh = run("final", gathered=gathered, extra=(thresh_tiles,))
    gradient = last_reduce(*shares).reshape(SLOT_PAIRS, PATCHES, LANES)
    sent = sent.astype(jnp.float32)
    result = shrink(sent - 0.5 * gradient, thresh[None])
    result = result.reshape(SLOT_PAIRS, PATCHES, 2, BLOCK).transpose(0, 2, 1, 3)
    return result.reshape(1, SLOTS, PATCHES * BLOCK)


def solution(mesh):
    in_specs = (
        P("rows", None),
        P("rows", "groups"),
        P(("groups", "rows"), None, None),
        P("groups", None),
        P("groups"),
        P("groups"),
        P("groups", None),
    )
    out_specs = P(("groups", "rows"), None, None)
    return jax.shard_map(local, mesh=mesh, in_specs=in_specs, out_specs=out_specs, check_vma=False)
```

```python
import functools
import math

import jax
import jax.numpy as jnp
from jax import lax
from jax.experimental import pallas as pl
from jax.experimental.pallas import tpu as pltpu
from jax.sharding import PartitionSpec as P

BLOCK = 64
SLOTS = 16
PATCHES = 64
ITERS = 3
MEAN_LIVE = 10
LANES = 2 * BLOCK
SLOT_PAIRS = SLOTS // 2
SPARE = SLOT_PAIRS + 2
ROW_TILE = 16
SUPPORT_PARTS = 2
SUPPORT_STEP = 4
PIECE = 5
MATRIX_UNIT = 256
VMEM_MARGIN = 3 * 1024 * 1024
SUPPORT_VMEM = 40 * 1024 * 1024
HELD_BYTES = 65 * 1024 * 1024


def momentum_list():
    values = []
    tvalue = 1.0
    for turn in range(ITERS):
        tnext = (1.0 + (1.0 + 4.0 * tvalue * tvalue) ** 0.5) / 2.0
        values.append((tvalue - 1.0) / tnext)
        tvalue = tnext
    return values


def swap_halves(value):
    return jnp.concatenate([value[:, BLOCK:], value[:, :BLOCK]], axis=1)


def upper_half(shape):
    return lax.broadcasted_iota(jnp.int32, shape, 1) >= BLOCK


class Part:
    def __init__(self, ref, begin):
        self.ref, self.begin = ref, begin

    def __getitem__(self, index):
        return self.ref[self.begin + index]


def scalar_parts(scalars, groups):
    seq, order, counts = (Part(scalars, part * groups) for part in range(3))
    return seq, order, counts, scalars[3 * groups]


def group_at(index, seq, order, counts):
    position = seq[index]
    group = order[position]
    return position, group, counts[group]


def support_kernel(begin, groups, scalars, support, dictionary, *refs):
    out, held, picks, ids, sems, out_sems = refs[-6:]
    seq, order, counts, _ = scalar_parts(scalars, groups)
    entries, rows, _ = held.shape
    pairs = entries // 2

    def fetch(entry, block):
        start = pl.multiple_of((block // 2) * LANES, LANES)
        return pltpu.make_async_copy(dictionary.at[:, pl.ds(start, LANES)], held.at[entry], sems.at[entry])

    def start_group(index, offset):
        _, group, live = group_at(index, seq, order, counts)

        def start_slot(slot, carry):
            block = support[group, slot]
            ids[offset + slot] = block
            fetch(offset + slot, block).start()
            return carry

        lax.fori_loop(jnp.clip(-offset, 0, live), jnp.clip(entries - offset, 0, live), start_slot, 0)
        return offset + live

    lax.fori_loop(0, groups, start_group, jnp.int32(-begin))
    steps = pairs // SUPPORT_STEP
    shape = (2 * LANES, LANES)
    source = lax.broadcasted_iota(jnp.int32, shape, 0)
    target = lax.broadcasted_iota(jnp.int32, shape, 1)
    for choice in range(4):
        wanted = jnp.where(target < BLOCK, (choice % 2) * BLOCK + target, LANES + (choice // 2) * BLOCK + target - BLOCK)
        picks[choice] = (source == wanted).astype(jnp.float32).astype(jnp.bfloat16)

    def store(pair):
        return pltpu.make_async_copy(held.at[2 * pair], out.at[begin // 2 + pair], out_sems.at[pair])

    def pack(step, carry):
        span = [SUPPORT_STEP * step + pair for pair in range(SUPPORT_STEP)]
        for pair in span:
            fetch(2 * pair, ids[2 * pair]).wait()
            fetch(2 * pair + 1, ids[2 * pair + 1]).wait()
        packed = []
        for pair in span:
            choice = ids[2 * pair] % 2 + 2 * (ids[2 * pair + 1] % 2)
            both = jnp.concatenate([held[2 * pair], held[2 * pair + 1]], axis=1)
            packed.append(jnp.dot(both, picks[choice], preferred_element_type=jnp.float32).astype(jnp.bfloat16))
        for pair, value in zip(span, packed):
            held[2 * pair] = value
            store(pair).start()
        return carry

    lax.fori_loop(0, steps, pack, 0)

    def drain(pair, carry):
        store(pair).wait()
        return carry

    lax.fori_loop(0, pairs, drain, 0)


def collect_support(scalars, support, groups, dictionary, pairs, part, *before):
    rows = dictionary.shape[0]
    pairs = pairs // SUPPORT_PARTS
    entries = 2 * pairs
    return pl.pallas_call(
        functools.partial(support_kernel, part * entries, groups),
        grid_spec=pltpu.PrefetchScalarGridSpec(
            num_scalar_prefetch=2,
            grid=(),
            in_specs=[pl.BlockSpec(memory_space=pltpu.HBM)] * (1 + len(before)),
            out_specs=pl.BlockSpec(memory_space=pltpu.HBM),
            scratch_shapes=[
                pltpu.VMEM((entries, rows, LANES), dictionary.dtype),
                pltpu.VMEM((4, 2 * LANES, LANES), jnp.bfloat16),
                pltpu.SMEM((entries,), jnp.int32),
                pltpu.SemaphoreType.DMA((entries,)),
                pltpu.SemaphoreType.DMA((pairs,)),
            ],
        ),
        out_shape=jax.ShapeDtypeStruct((HELD_BYTES // (rows * LANES * 2), rows, LANES), dictionary.dtype),
        compiler_params=pltpu.CompilerParams(vmem_limit_bytes=SUPPORT_VMEM),
        cost_estimate=pl.CostEstimate(flops=0, transcendentals=0, bytes_accessed=6 * pairs * rows * LANES * 2),
        input_output_aliases={3: 0} if before else {},
        name="collect_support",
    )(scalars, support, dictionary, *before)


def stage_distances(devices):
    return [2**bit for bit in range(devices.bit_length() - 1)]


def last_orders(devices):
    distances = stage_distances(devices)
    return distances, distances[:1] + distances[2:] + distances[1:2]


def slot_distance(slot, distances):
    bits = reversed(range(len(distances)))
    return sum(distance for bit, distance in zip(bits, distances) if slot >> bit & 1)


def gradient_kernel(mode, shards, pairs, groups, scalars, blocks, *refs):
    seq, order, counts, me = scalar_parts(scalars, groups)
    refs = list(refs)
    take = lambda: refs.pop(0)
    gathered, targets = [take() for _ in range(4)], take()
    if mode in ("first", "final"):
        thresh = take()
    keep, send = take(), (take(), take())
    if mode == "first":
        start_out, thresh_out = take(), take()
    if mode == "final":
        sent, thresh_out = take(), take()
    held, codes, total = take(), take(), take()
    if mode == "first":
        starts, limits = take(), take()
    offsets, sems = refs

    pieces = pairs // PIECE

    def load(index):
        span = pl.ds(index * PIECE, PIECE)
        return pltpu.make_async_copy(blocks.at[span], held.at[span], sems.at[index])

    for index in range(pieces):
        load(index).start()
    held[pairs:] = jnp.zeros((SPARE,) + held.shape[1:], held.dtype)

    distances = stage_distances(shards)

    def shard_span(slot, size):
        return pl.ds(pl.multiple_of((slot_distance(slot, distances) ^ me) * size, ROW_TILE), size)

    def last_holder(slot):
        even, odd = (slot_distance(slot, order) for order in last_orders(shards))
        if slot >= shards // 2:
            even, odd = odd, even
        return jnp.where(me % 2 == 0, even, odd) ^ me

    quarter = shards // 4
    size_in = gathered[0].shape[0] // (quarter + 1)
    for slot in range(shards):
        half, inside = divmod(slot, 2 * quarter)
        second = inside > quarter
        begin = (inside - (quarter + 1) * second) * size_in
        codes[shard_span(slot, size_in), :] = gathered[2 * half + second][begin : begin + size_in, :]

    def put(slot, size, begin, value):
        far, inside = divmod(slot, 2 * quarter)
        if far:
            ahead = send[0].shape[0] // size
            second = inside >= ahead
            start = (inside - ahead * second) * size + begin
            send[second][start : start + value.shape[0], :] = value.astype(jnp.bfloat16)
        else:
            start = inside * size + begin
            keep[start : start + value.shape[0], :] = value

    def seat(index, offset):
        position, _, live = group_at(index, seq, order, counts)
        offsets[position] = offset
        return offset + live

    lax.fori_loop(0, groups, seat, jnp.int32(0))

    upper = upper_half((PATCHES, LANES))
    side = upper.astype(jnp.int32)

    def tile(pair):
        return pl.ds(pl.multiple_of(pair * PATCHES, PATCHES), PATCHES)

    def shifted(parts, count, odd, ahead):
        turned = [swap_halves(part) for part in parts]
        last = len(parts) - 1
        moved = []
        for pair in range(count):
            low, high = (pair, pair + 1) if ahead else (pair - 1, pair)
            low, high = min(max(low, 0), last), min(max(high, 0), last)
            value = jnp.where(upper[: turned[low].shape[0]], turned[high], turned[low])
            moved.append(jnp.where(odd, value, parts[min(pair, last)]))
        return moved

    def read_codes(position, offset, live, count):
        first = offset // 2
        if mode == "first":
            parts = [codes[tile(position * SLOT_PAIRS + pair), :] for pair in range(min(count, SLOT_PAIRS))]
            parts = shifted(parts, count, offset % 2 == 1, False)
        else:
            parts = [codes[tile(first + pair), :] for pair in range(count)]
        masked = []
        for pair, part in enumerate(parts):
            entry = 2 * (first + pair) + side
            mine = (entry >= offset) & (entry < offset + live)
            masked.append(jnp.where(mine, part, jnp.zeros_like(part)))
        return masked

    def write_packed(ref, parts, offset):
        first = offset // 2
        for pair, part in enumerate(parts):
            if pair == 0:
                part = jnp.where(upper | (offset % 2 == 0), part, ref[tile(first), :])
            ref[tile(first + pair), :] = part

    def one_group(position, group, offset, live, count):
        first = offset // 2
        parts = read_codes(position, offset, live, count)
        if mode == "first":
            write_packed(starts, parts, offset)
            write_packed(limits, [thresh[group]] * count, offset)
        matrix = jnp.concatenate([held[first + pair] for pair in range(count)], axis=1)
        point = jnp.concatenate(parts, axis=1)
        residual = lax.dot_general(point, matrix, (((1,), (1,)), ((), ())), preferred_element_type=jnp.float32)
        target = targets[tile(group), :].astype(jnp.float32)
        residual = (residual - target).astype(jnp.bfloat16)
        gradient = jnp.dot(residual, matrix, preferred_element_type=jnp.float32)
        write_packed(total, [gradient[:, pair * LANES : (pair + 1) * LANES] for pair in range(count)], offset)

    def wait_piece(index, carry):
        load(index).wait()
        return carry

    def two_groups(step, waited):
        picks = []
        count_needed = 1
        for index in (2 * step, 2 * step + 1):
            position, group, live = group_at(index, seq, order, counts)
            offset = offsets[position]
            picks.append((position, group, offset, live))
            count_needed = jnp.maximum(count_needed, (live + offset % 2 + 1) // 2)
        reach = jnp.minimum(picks[1][2] // 2 + count_needed - 1, pairs - 1)
        needed = jnp.maximum(reach // PIECE + 1, waited)
        lax.fori_loop(waited, needed, wait_piece, 0)
        for count in range(1, SLOT_PAIRS + 2):

            @pl.when(count_needed == count)
            def _(count=count):
                for pick in picks:
                    one_group(*pick, count)

        return needed

    waited = lax.fori_loop(0, groups // 2, two_groups, jnp.int32(0))
    lax.fori_loop(waited, pieces, wait_piece, 0)

    if mode != "final":
        size = 2 * keep.shape[0] // shards
        for slot in range(shards):
            put(slot, size, 0, total[shard_span(slot, size), :])
    if mode == "first":
        size = start_out.shape[0]
        span = pl.ds(pl.multiple_of(me * size, ROW_TILE), size)
        start_out[...] = starts[span, :]
        thresh_out[...] = limits[span, :]
    if mode == "final":
        offset = offsets[me]
        parts = read_codes(me, offset, counts[order[me]], SLOT_PAIRS + 1)
        for pair, part in enumerate(shifted(parts, SLOT_PAIRS, offset % 2 == 1, True)):
            sent[pair] = part
        thresh_out[...] = thresh[order[me]]
        for slot in range(shards):
            position = last_holder(slot)
            offset = offsets[position]
            live = counts[order[position]]
            parts = [total[tile(offset // 2 + pair), :] for pair in range(SLOT_PAIRS + 1)]
            for pair, part in enumerate(shifted(parts, SLOT_PAIRS, offset % 2 == 1, True)):
                value = jnp.where(2 * pair + side < live, part, 0.0)
                put(slot, SLOT_PAIRS * PATCHES, pair * PATCHES, value)


def gradient_call(mode, shards, pairs, groups, scalars, blocks, gathered, targets, extra=()):
    rows = blocks.shape[1]
    places = pairs + SPARE
    single, double = jnp.bfloat16, jnp.float32
    packed = (places * PATCHES, LANES)
    half_out = (groups * SLOT_PAIRS if mode == "final" else pairs) * PATCHES // 2
    shard = (2 * half_out // shards, LANES)
    ahead = half_out // 2 + (0 if mode == "final" else shard[0])
    outs = [((half_out, LANES), double), ((ahead, LANES), single), ((half_out - ahead, LANES), single)]
    if mode == "first":
        outs += [(shard, single), (shard, double)]
    if mode == "final":
        outs += [((SLOT_PAIRS, PATCHES, LANES), single), ((PATCHES, LANES), double)]
    codes = groups * SLOT_PAIRS * PATCHES if mode == "first" else packed[0]
    scratch = [((places, rows, LANES), single), ((codes, LANES), single), (packed, double)]
    if mode == "first":
        scratch += [(packed, single), (packed, double)]
    room = sum(math.prod(shape) * jnp.dtype(kind).itemsize for shape, kind in scratch)
    return pl.pallas_call(
        functools.partial(gradient_kernel, mode, shards, pairs, groups),
        grid_spec=pltpu.PrefetchScalarGridSpec(
            num_scalar_prefetch=1,
            grid=(),
            in_specs=[pl.BlockSpec(memory_space=pltpu.HBM)]
            + [pl.BlockSpec(memory_space=pltpu.VMEM)] * (5 + len(extra)),
            out_specs=[pl.BlockSpec(memory_space=pltpu.VMEM)] * len(outs),
            scratch_shapes=[pltpu.VMEM(shape, kind) for shape, kind in scratch]
            + [pltpu.SMEM((groups,), jnp.int32), pltpu.SemaphoreType.DMA((pairs // PIECE,))],
        ),
        out_shape=[jax.ShapeDtypeStruct(shape, kind) for shape, kind in outs],
        compiler_params=pltpu.CompilerParams(vmem_limit_bytes=room + VMEM_MARGIN),
        cost_estimate=pl.CostEstimate(
            flops=4 * pairs * rows * LANES * MATRIX_UNIT, transcendentals=0, bytes_accessed=pairs * rows * LANES * 2
        ),
        name="gradient",
    )(scalars, blocks, *gathered, targets, *extra)


def exchange(value, even, odd=None):
    devices = lax.axis_size("rows")
    apart = (even, even if odd is None else odd)
    return lax.ppermute(value, "rows", [(i, i ^ apart[i % 2]) for i in range(devices)])


def gather_shards(own, beside=()):
    core, row, *columns = stage_distances(lax.axis_size("rows"))
    apart = [slot_distance(slot, columns) for slot in range(lax.axis_size("rows") // 4)]
    made = ()
    near = jnp.concatenate([own] + [exchange(own, distance) for distance in apart[1:] + [row]], axis=0)
    if beside:
        near, *made = lax.optimization_barrier((near, beside[0]()))
    other = exchange(near[own.shape[0] : len(apart) * own.shape[0]], row)
    far = exchange(near, core)
    if beside:
        other, *made = lax.optimization_barrier((other, beside[1](*made)))
    return (near, other, far, exchange(other, core)), made


def add_cores(keep, *send):
    ahead = send[0].shape[0]
    after = keep[ahead:] + exchange(send[1], 1).astype(jnp.float32)
    return keep[:ahead] + exchange(send[0], 1).astype(jnp.float32), after


def reduce_shards(keep, *send):
    devices = lax.axis_size("rows")
    _, row, *columns = stage_distances(devices)
    size = 2 * keep.shape[0] // devices
    near, other = add_cores(keep, *send)
    sums = near[size:-size] + exchange(other.astype(jnp.bfloat16), row).astype(jnp.float32)
    last, sums = lax.optimization_barrier((near[-size:].astype(jnp.bfloat16), sums.astype(jnp.bfloat16)))
    total = near[:size]
    for slot in sorted(range(1, devices // 4), key=lambda slot: -slot_distance(slot, columns)):
        share = exchange(sums[(slot - 1) * size : slot * size], slot_distance(slot, columns))
        total = total + share.astype(jnp.float32)
    return total + exchange(last, row).astype(jnp.float32)


def last_reduce(keep, *send):
    devices = lax.axis_size("rows")
    even, odd = last_orders(devices)
    near, other = add_cores(keep, *send)
    sums = near + exchange(other.astype(jnp.bfloat16), even[1], odd[1]).astype(jnp.float32)
    size = 2 * keep.shape[0] // devices
    sent = sums.astype(jnp.bfloat16)
    total = sums[:size]
    for slot in range(1, devices // 4):
        share = sent[slot * size : (slot + 1) * size]
        total = total + exchange(share, slot_distance(slot, even[2:]), slot_distance(slot, odd[2:])).astype(jnp.float32)
    return total


def packed_order(live):
    index = jnp.arange(live.shape[0])
    key = (live + live % 2 * (SLOTS + 1)) * live.shape[0] + index
    ahead = key[None, :] < key[:, None]
    rank = jnp.sum(ahead.astype(jnp.int32), axis=1)
    return jnp.sum(jnp.where(rank[:, None] == index[None, :], index[:, None], 0), axis=0).astype(jnp.int32)


def shrink(value, thresh):
    return value - jnp.clip(value, -thresh, thresh)


def local(dictionary, patches, initial_codes, support, counts, group_order, penalty):
    groups = group_order.shape[0]
    position = lax.axis_index("rows")
    devices = lax.axis_size("rows")
    momenta = momentum_list()
    pairs = MEAN_LIVE * groups // 2

    laid = initial_codes.reshape(SLOT_PAIRS, 2, PATCHES, BLOCK).transpose(0, 2, 1, 3)
    laid = laid.reshape(SLOT_PAIRS * PATCHES, LANES)
    live = jnp.sum(jnp.where(group_order[:, None] == jnp.arange(groups)[None, :], counts[None, :], 0), axis=1)
    own = position.astype(jnp.int32).reshape(1)
    scalars = jnp.concatenate([packed_order(live), group_order, counts, own])
    collect = functools.partial(collect_support, scalars, support, groups, dictionary, pairs)
    gathered, (blocks,) = gather_shards(laid, [functools.partial(collect, part) for part in range(SUPPORT_PARTS)])

    targets = patches.T
    half_penalty = 0.5 * penalty
    thresh_tiles = jnp.broadcast_to(half_penalty[:, :, None], (groups, PATCHES, LANES))

    run = functools.partial(
        gradient_call, shards=devices, pairs=pairs, groups=groups, scalars=scalars, blocks=blocks, targets=targets
    )
    *shares, start, thresh = run("first", gathered=gathered, extra=(thresh_tiles,))
    point = previous = start.astype(jnp.float32)
    for turn in range(ITERS - 1):
        if turn:
            shares = run("packed", gathered=gathered)
        current = shrink(point - 0.5 * reduce_shards(*shares), thresh)
        point = current + momenta[turn] * (current - previous)
        previous = current
        gathered, _ = gather_shards(point.astype(jnp.bfloat16))
    *shares, sent, thresh = run("final", gathered=gathered, extra=(thresh_tiles,))
    gradient = last_reduce(*shares).reshape(SLOT_PAIRS, PATCHES, LANES)
    sent = sent.astype(jnp.float32)
    result = shrink(sent - 0.5 * gradient, thresh[None])
    result = result.reshape(SLOT_PAIRS, PATCHES, 2, BLOCK).transpose(0, 2, 1, 3)
    return result.reshape(1, SLOTS, PATCHES * BLOCK)


def solution(mesh):
    in_specs = (
        P("rows", None),
        P("rows", "groups"),
        P(("groups", "rows"), None, None),
        P("groups", None),
        P("groups"),
        P("groups"),
        P("groups", None),
    )
    out_specs = P(("groups", "rows"), None, None)
    return jax.shard_map(local, mesh=mesh, in_specs=in_specs, out_specs=out_specs, check_vma=False)
```

```python
import functools
import math

import jax
import jax.numpy as jnp
from jax import lax
from jax.experimental import pallas as pl
from jax.experimental.pallas import tpu as pltpu
from jax.sharding import PartitionSpec as P

BLOCK = 64
SLOTS = 16
PATCHES = 64
ITERS = 3
MEAN_LIVE = 10
LANES = 2 * BLOCK
SLOT_PAIRS = SLOTS // 2
SPARE = SLOT_PAIRS + 2
ROW_TILE = 16
SUPPORT_PARTS = 2
SUPPORT_STEP = 8
PIECE = 5
MATRIX_UNIT = 256
VMEM_MARGIN = 3 * 1024 * 1024
SUPPORT_VMEM = 40 * 1024 * 1024
HELD_BYTES = 65 * 1024 * 1024


def momentum_list():
    values = []
    tvalue = 1.0
    for turn in range(ITERS):
        tnext = (1.0 + (1.0 + 4.0 * tvalue * tvalue) ** 0.5) / 2.0
        values.append((tvalue - 1.0) / tnext)
        tvalue = tnext
    return values


def swap_halves(value):
    return jnp.concatenate([value[:, BLOCK:], value[:, :BLOCK]], axis=1)


def upper_half(shape):
    return lax.broadcasted_iota(jnp.int32, shape, 1) >= BLOCK


class Part:
    def __init__(self, ref, begin, width=1):
        self.ref, self.begin, self.width = ref, begin, width

    def __getitem__(self, index):
        if isinstance(index, tuple):
            index = index[0] * self.width + index[1]
        return self.ref[self.begin + index]


def scalar_parts(scalars, groups):
    seq, order, counts = (Part(scalars, part * groups) for part in range(3))
    return seq, order, counts, Part(scalars, 3 * groups, SLOTS), scalars[groups * (3 + SLOTS)]


def group_at(index, seq, order, counts):
    position = seq[index]
    group = order[position]
    return position, group, counts[group]


def support_kernel(begin, groups, scalars, dictionary, *refs):
    out, held, picks, ids, sems, out_sems = refs[-6:]
    seq, order, counts, support, _ = scalar_parts(scalars, groups)
    entries, rows, _ = held.shape
    pairs = entries // 2

    def fetch(entry, block):
        start = pl.multiple_of((block // 2) * LANES, LANES)
        return pltpu.make_async_copy(dictionary.at[:, pl.ds(start, LANES)], held.at[entry], sems.at[entry])

    def start_group(index, offset):
        _, group, live = group_at(index, seq, order, counts)

        def start_slot(slot, carry):
            block = support[group, slot]
            ids[offset + slot] = block
            fetch(offset + slot, block).start()
            return carry

        lax.fori_loop(jnp.clip(-offset, 0, live), jnp.clip(entries - offset, 0, live), start_slot, 0)
        return offset + live

    lax.fori_loop(0, groups, start_group, jnp.int32(-begin))
    steps = pairs // SUPPORT_STEP
    shape = (2 * LANES, LANES)
    source = lax.broadcasted_iota(jnp.int32, shape, 0)
    target = lax.broadcasted_iota(jnp.int32, shape, 1)
    for choice in range(4):
        wanted = jnp.where(target < BLOCK, (choice % 2) * BLOCK + target, LANES + (choice // 2) * BLOCK + target - BLOCK)
        picks[choice] = (source == wanted).astype(jnp.float32).astype(jnp.bfloat16)

    def store(pair):
        return pltpu.make_async_copy(held.at[2 * pair], out.at[begin // 2 + pair], out_sems.at[pair])

    def pack(step, carry):
        span = [SUPPORT_STEP * step + pair for pair in range(SUPPORT_STEP)]
        for pair in span:
            fetch(2 * pair, ids[2 * pair]).wait()
            fetch(2 * pair + 1, ids[2 * pair + 1]).wait()
        packed = []
        for pair in span:
            choice = ids[2 * pair] % 2 + 2 * (ids[2 * pair + 1] % 2)
            both = jnp.concatenate([held[2 * pair], held[2 * pair + 1]], axis=1)
            packed.append(jnp.dot(both, picks[choice], preferred_element_type=jnp.float32).astype(jnp.bfloat16))
        for pair, value in zip(span, packed):
            held[2 * pair] = value
            store(pair).start()
        return carry

    lax.fori_loop(0, steps, pack, 0)

    def drain(pair, carry):
        store(pair).wait()
        return carry

    lax.fori_loop(0, pairs, drain, 0)


def collect_support(scalars, groups, dictionary, pairs, part, *before):
    rows = dictionary.shape[0]
    pairs = pairs // SUPPORT_PARTS
    entries = 2 * pairs
    return pl.pallas_call(
        functools.partial(support_kernel, part * entries, groups),
        grid_spec=pltpu.PrefetchScalarGridSpec(
            num_scalar_prefetch=1,
            grid=(),
            in_specs=[pl.BlockSpec(memory_space=pltpu.HBM)] * (1 + len(before)),
            out_specs=pl.BlockSpec(memory_space=pltpu.HBM),
            scratch_shapes=[
                pltpu.VMEM((entries, rows, LANES), dictionary.dtype),
                pltpu.VMEM((4, 2 * LANES, LANES), jnp.bfloat16),
                pltpu.SMEM((entries,), jnp.int32),
                pltpu.SemaphoreType.DMA((entries,)),
                pltpu.SemaphoreType.DMA((pairs,)),
            ],
        ),
        out_shape=jax.ShapeDtypeStruct((HELD_BYTES // (rows * LANES * 2), rows, LANES), dictionary.dtype),
        compiler_params=pltpu.CompilerParams(vmem_limit_bytes=SUPPORT_VMEM),
        cost_estimate=pl.CostEstimate(flops=0, transcendentals=0, bytes_accessed=6 * pairs * rows * LANES * 2),
        input_output_aliases={2: 0} if before else {},
        name="collect_support",
    )(scalars, dictionary, *before)


def stage_distances(devices):
    return [2**bit for bit in range(devices.bit_length() - 1)]


def last_orders(devices):
    distances = stage_distances(devices)
    return distances, distances[:1] + distances[2:] + distances[1:2]


def slot_distance(slot, distances):
    bits = reversed(range(len(distances)))
    return sum(distance for bit, distance in zip(bits, distances) if slot >> bit & 1)


def gradient_kernel(mode, shards, pairs, groups, scalars, blocks, *refs):
    seq, order, counts, _, me = scalar_parts(scalars, groups)
    refs = list(refs)
    take = lambda: refs.pop(0)
    gathered, targets = [take() for _ in range(4)], take()
    if mode in ("first", "final"):
        thresh = take()
    keep, send = take(), (take(), take())
    if mode == "first":
        start_out, thresh_out = take(), take()
    if mode == "final":
        sent, thresh_out = take(), take()
    held, codes, total = take(), take(), take()
    if mode == "first":
        starts, limits = take(), take()
    offsets, sems = refs

    pieces = pairs // PIECE

    def load(index):
        span = pl.ds(index * PIECE, PIECE)
        return pltpu.make_async_copy(blocks.at[span], held.at[span], sems.at[index])

    for index in range(pieces):
        load(index).start()
    held[pairs:] = jnp.zeros((SPARE,) + held.shape[1:], held.dtype)

    distances = stage_distances(shards)

    def shard_span(slot, size):
        return pl.ds(pl.multiple_of((slot_distance(slot, distances) ^ me) * size, ROW_TILE), size)

    def last_holder(slot):
        even, odd = (slot_distance(slot, order) for order in last_orders(shards))
        if slot >= shards // 2:
            even, odd = odd, even
        return jnp.where(me % 2 == 0, even, odd) ^ me

    quarter = shards // 4
    size_in = gathered[0].shape[0] // (quarter + 1)
    for slot in range(shards):
        half, inside = divmod(slot, 2 * quarter)
        second = inside > quarter
        begin = (inside - (quarter + 1) * second) * size_in
        codes[shard_span(slot, size_in), :] = gathered[2 * half + second][begin : begin + size_in, :]

    def put(slot, size, begin, value):
        far, inside = divmod(slot, 2 * quarter)
        if far:
            ahead = send[0].shape[0] // size
            second = inside >= ahead
            start = (inside - ahead * second) * size + begin
            send[second][start : start + value.shape[0], :] = value.astype(jnp.bfloat16)
        else:
            start = inside * size + begin
            keep[start : start + value.shape[0], :] = value

    def seat(index, offset):
        position, _, live = group_at(index, seq, order, counts)
        offsets[position] = offset
        return offset + live

    lax.fori_loop(0, groups, seat, jnp.int32(0))

    upper = upper_half((PATCHES, LANES))
    side = upper.astype(jnp.int32)

    def tile(pair):
        return pl.ds(pl.multiple_of(pair * PATCHES, PATCHES), PATCHES)

    def shifted(parts, count, odd, ahead):
        turned = [swap_halves(part) for part in parts]
        last = len(parts) - 1
        moved = []
        for pair in range(count):
            low, high = (pair, pair + 1) if ahead else (pair - 1, pair)
            low, high = min(max(low, 0), last), min(max(high, 0), last)
            value = jnp.where(upper[: turned[low].shape[0]], turned[high], turned[low])
            moved.append(jnp.where(odd, value, parts[min(pair, last)]))
        return moved

    def read_codes(position, offset, live, count):
        first = offset // 2
        if mode == "first":
            parts = [codes[tile(position * SLOT_PAIRS + pair), :] for pair in range(min(count, SLOT_PAIRS))]
            parts = shifted(parts, count, offset % 2 == 1, False)
        else:
            parts = [codes[tile(first + pair), :] for pair in range(count)]
        masked = []
        for pair, part in enumerate(parts):
            entry = 2 * (first + pair) + side
            mine = (entry >= offset) & (entry < offset + live)
            masked.append(jnp.where(mine, part, jnp.zeros_like(part)))
        return masked

    def write_packed(ref, parts, offset):
        first = offset // 2
        for pair, part in enumerate(parts):
            if pair == 0:
                part = jnp.where(upper | (offset % 2 == 0), part, ref[tile(first), :])
            ref[tile(first + pair), :] = part

    def one_group(position, group, offset, live, count):
        first = offset // 2
        parts = read_codes(position, offset, live, count)
        if mode == "first":
            write_packed(starts, parts, offset)
            write_packed(limits, [thresh[group]] * count, offset)
        matrix = jnp.concatenate([held[first + pair] for pair in range(count)], axis=1)
        point = jnp.concatenate(parts, axis=1)
        residual = lax.dot_general(point, matrix, (((1,), (1,)), ((), ())), preferred_element_type=jnp.float32)
        target = targets[tile(group), :].astype(jnp.float32)
        residual = (residual - target).astype(jnp.bfloat16)
        gradient = jnp.dot(residual, matrix, preferred_element_type=jnp.float32)
        write_packed(total, [gradient[:, pair * LANES : (pair + 1) * LANES] for pair in range(count)], offset)

    def wait_piece(index, carry):
        load(index).wait()
        return carry

    def two_groups(step, waited):
        picks = []
        count_needed = 1
        for index in (2 * step, 2 * step + 1):
            position, group, live = group_at(index, seq, order, counts)
            offset = offsets[position]
            picks.append((position, group, offset, live))
            count_needed = jnp.maximum(count_needed, (live + offset % 2 + 1) // 2)
        reach = jnp.minimum(picks[1][2] // 2 + count_needed - 1, pairs - 1)
        needed = jnp.maximum(reach // PIECE + 1, waited)
        lax.fori_loop(waited, needed, wait_piece, 0)
        for count in range(1, SLOT_PAIRS + 2):

            @pl.when(count_needed == count)
            def _(count=count):
                for pick in picks:
                    one_group(*pick, count)

        return needed

    waited = lax.fori_loop(0, groups // 2, two_groups, jnp.int32(0))
    lax.fori_loop(waited, pieces, wait_piece, 0)

    if mode != "final":
        size = 2 * keep.shape[0] // shards
        for slot in range(shards):
            put(slot, size, 0, total[shard_span(slot, size), :])
    if mode == "first":
        size = start_out.shape[0]
        span = pl.ds(pl.multiple_of(me * size, ROW_TILE), size)
        start_out[...] = starts[span, :]
        thresh_out[...] = limits[span, :]
    if mode == "final":
        offset = offsets[me]
        parts = read_codes(me, offset, counts[order[me]], SLOT_PAIRS + 1)
        for pair, part in enumerate(shifted(parts, SLOT_PAIRS, offset % 2 == 1, True)):
            sent[pair] = part
        thresh_out[...] = thresh[order[me]]
        for slot in range(shards):
            position = last_holder(slot)
            offset = offsets[position]
            live = counts[order[position]]
            parts = [total[tile(offset // 2 + pair), :] for pair in range(SLOT_PAIRS + 1)]
            for pair, part in enumerate(shifted(parts, SLOT_PAIRS, offset % 2 == 1, True)):
                value = jnp.where(2 * pair + side < live, part, 0.0)
                put(slot, SLOT_PAIRS * PATCHES, pair * PATCHES, value)


def gradient_call(mode, shards, pairs, groups, scalars, blocks, gathered, targets, extra=()):
    rows = blocks.shape[1]
    places = pairs + SPARE
    single, double = jnp.bfloat16, jnp.float32
    packed = (places * PATCHES, LANES)
    half_out = (groups * SLOT_PAIRS if mode == "final" else pairs) * PATCHES // 2
    shard = (2 * half_out // shards, LANES)
    ahead = half_out // 2 + (0 if mode == "final" else shard[0])
    outs = [((half_out, LANES), double), ((ahead, LANES), single), ((half_out - ahead, LANES), single)]
    if mode == "first":
        outs += [(shard, single), (shard, double)]
    if mode == "final":
        outs += [((SLOT_PAIRS, PATCHES, LANES), single), ((PATCHES, LANES), double)]
    codes = groups * SLOT_PAIRS * PATCHES if mode == "first" else packed[0]
    scratch = [((places, rows, LANES), single), ((codes, LANES), single), (packed, double)]
    if mode == "first":
        scratch += [(packed, single), (packed, double)]
    room = sum(math.prod(shape) * jnp.dtype(kind).itemsize for shape, kind in scratch)
    return pl.pallas_call(
        functools.partial(gradient_kernel, mode, shards, pairs, groups),
        grid_spec=pltpu.PrefetchScalarGridSpec(
            num_scalar_prefetch=1,
            grid=(),
            in_specs=[pl.BlockSpec(memory_space=pltpu.HBM)]
            + [pl.BlockSpec(memory_space=pltpu.VMEM)] * (5 + len(extra)),
            out_specs=[pl.BlockSpec(memory_space=pltpu.VMEM)] * len(outs),
            scratch_shapes=[pltpu.VMEM(shape, kind) for shape, kind in scratch]
            + [pltpu.SMEM((groups,), jnp.int32), pltpu.SemaphoreType.DMA((pairs // PIECE,))],
        ),
        out_shape=[jax.ShapeDtypeStruct(shape, kind) for shape, kind in outs],
        compiler_params=pltpu.CompilerParams(vmem_limit_bytes=room + VMEM_MARGIN),
        cost_estimate=pl.CostEstimate(
            flops=4 * pairs * rows * LANES * MATRIX_UNIT, transcendentals=0, bytes_accessed=pairs * rows * LANES * 2
        ),
        name="gradient",
    )(scalars, blocks, *gathered, targets, *extra)


def exchange(value, even, odd=None):
    devices = lax.axis_size("rows")
    apart = (even, even if odd is None else odd)
    return lax.ppermute(value, "rows", [(i, i ^ apart[i % 2]) for i in range(devices)])


def gather_shards(own, beside=()):
    core, row, *columns = stage_distances(lax.axis_size("rows"))
    apart = [slot_distance(slot, columns) for slot in range(lax.axis_size("rows") // 4)]
    made = ()
    near = jnp.concatenate([own] + [exchange(own, distance) for distance in apart[1:] + [row]], axis=0)
    if beside:
        near, *made = lax.optimization_barrier((near, beside[0]()))
    other = exchange(near[own.shape[0] : len(apart) * own.shape[0]], row)
    far = exchange(near, core)
    if beside:
        other, *made = lax.optimization_barrier((other, beside[1](*made)))
    return (near, other, far, exchange(other, core)), made


def add_cores(keep, *send):
    ahead = send[0].shape[0]
    after = keep[ahead:] + exchange(send[1], 1).astype(jnp.float32)
    return keep[:ahead] + exchange(send[0], 1).astype(jnp.float32), after


def reduce_shards(keep, *send):
    devices = lax.axis_size("rows")
    _, row, *columns = stage_distances(devices)
    size = 2 * keep.shape[0] // devices
    near, other = add_cores(keep, *send)
    sums = near[size:-size] + exchange(other.astype(jnp.bfloat16), row).astype(jnp.float32)
    last, sums = lax.optimization_barrier((near[-size:].astype(jnp.bfloat16), sums.astype(jnp.bfloat16)))
    total = near[:size] + exchange(last, row).astype(jnp.float32)
    for slot in range(1, devices // 4):
        share = exchange(sums[(slot - 1) * size : slot * size], slot_distance(slot, columns))
        total = total + share.astype(jnp.float32)
    return total


def last_reduce(keep, *send):
    devices = lax.axis_size("rows")
    even, odd = last_orders(devices)
    near, other = add_cores(keep, *send)
    sums = near + exchange(other.astype(jnp.bfloat16), even[1], odd[1]).astype(jnp.float32)
    size = 2 * keep.shape[0] // devices
    sent = sums.astype(jnp.bfloat16)
    total = sums[:size]
    for slot in range(1, devices // 4):
        share = sent[slot * size : (slot + 1) * size]
        total = total + exchange(share, slot_distance(slot, even[2:]), slot_distance(slot, odd[2:])).astype(jnp.float32)
    return total


def packed_order(live):
    index = jnp.arange(live.shape[0])
    key = (live + live % 2 * (SLOTS + 1)) * live.shape[0] + index
    ahead = key[None, :] < key[:, None]
    rank = jnp.sum(ahead.astype(jnp.int32), axis=1)
    return jnp.sum(jnp.where(rank[:, None] == index[None, :], index[:, None], 0), axis=0).astype(jnp.int32)


def shrink(value, thresh):
    return value - jnp.clip(value, -thresh, thresh)


def local(dictionary, patches, initial_codes, support, counts, group_order, penalty):
    groups = group_order.shape[0]
    position = lax.axis_index("rows")
    devices = lax.axis_size("rows")
    momenta = momentum_list()
    pairs = MEAN_LIVE * groups // 2

    laid = initial_codes.reshape(SLOT_PAIRS, 2, PATCHES, BLOCK).transpose(0, 2, 1, 3)
    laid = laid.reshape(SLOT_PAIRS * PATCHES, LANES)
    live = jnp.sum(jnp.where(group_order[:, None] == jnp.arange(groups)[None, :], counts[None, :], 0), axis=1)
    own = position.astype(jnp.int32).reshape(1)
    scalars = jnp.concatenate([packed_order(live), group_order, counts, support.reshape(groups * SLOTS), own])
    collect = functools.partial(collect_support, scalars, groups, dictionary, pairs)
    gathered, (blocks,) = gather_shards(laid, [functools.partial(collect, part) for part in range(SUPPORT_PARTS)])

    targets = patches.T
    half_penalty = 0.5 * penalty
    thresh_tiles = jnp.broadcast_to(half_penalty[:, :, None], (groups, PATCHES, LANES))

    run = functools.partial(
        gradient_call, shards=devices, pairs=pairs, groups=groups, scalars=scalars, blocks=blocks, targets=targets
    )
    *shares, start, thresh = run("first", gathered=gathered, extra=(thresh_tiles,))
    point = previous = start.astype(jnp.float32)
    for turn in range(ITERS - 1):
        if turn:
            shares = run("packed", gathered=gathered)
        current = shrink(point - 0.5 * reduce_shards(*shares), thresh)
        point = current + momenta[turn] * (current - previous)
        previous = current
        gathered, _ = gather_shards(point.astype(jnp.bfloat16))
    *shares, sent, thresh = run("final", gathered=gathered, extra=(thresh_tiles,))
    gradient = last_reduce(*shares).reshape(SLOT_PAIRS, PATCHES, LANES)
    sent = sent.astype(jnp.float32)
    result = shrink(sent - 0.5 * gradient, thresh[None])
    result = result.reshape(SLOT_PAIRS, PATCHES, 2, BLOCK).transpose(0, 2, 1, 3)
    return result.reshape(1, SLOTS, PATCHES * BLOCK)


def solution(mesh):
    in_specs = (
        P("rows", None),
        P("rows", "groups"),
        P(("groups", "rows"), None, None),
        P("groups", None),
        P("groups"),
        P("groups"),
        P("groups", None),
    )
    out_specs = P(("groups", "rows"), None, None)
    return jax.shard_map(local, mesh=mesh, in_specs=in_specs, out_specs=out_specs, check_vma=False)
```
